256 devices in a mesh: grp: 4 (over x_hi, core), gx: 16 (over z, x_lo), gy: 4 (over y).
Axes of the slice: x: 4 (x_hi: 2, x_lo: 2; x = x_hi * 2 + x_lo), y: 4, z: 8, core: 2. Of those that a mesh axis runs over, the one named last changes fastest.
Arguments:
- state: float32 [16, 4096, 512], P(None, ('grp', 'gx'), 'gy'), may hold values from -6 to 6
- winds: float32 [2, 16, 4096, 512], P(None, None, ('grp', 'gx'), 'gy'), may hold values from -0.2 to 0.2
- diffusivity: float32 [2, 16], replicated, may hold values from 0.05 to 0.2
- coupling: float32 [8, 16], replicated, may hold values from -1.5 to 1.5
- heat_coef: float32 [8], replicated, may hold values from 0.2 to 0.6
- remap_blocks: bfloat16 [64, 128, 128], replicated, may hold values from -0.21875 to 0.21875
- source_patch: int32 [16, 4, 64, 6], P('gx', 'gy'), may hold values from 0 to 191
- block_ids: int32 [16, 4, 64, 6], P('gx', 'gy'), may hold values from 0 to 63
- land_sea: int32 [16, 4, 64], P('gx', 'gy'), may hold values 0 or 1
Outputs:
- state_out: float32 [16, 4096, 512], P(None, ('grp', 'gx'), 'gy')
- boundary_field: float32 [4096, 512], P(('grp', 'gx'), 'gy')
- fluxes: float32 [8, 4096, 512], P(None, ('grp', 'gx'), 'gy')
The draws below stay inside these ranges and needn't reach their ends.
All inputs are finite; a program needn't handle non-finite values. No bound on the sum of `land_sea` on one device may be relied on, other than what follows from the above.
Results may differ from the reference program's by a relative error of at most 0.0013.
Values may be sent and summed in bfloat16 or wider, within the bound.
No kernel may reach another device: no remote copies, remote signals or barrier semaphores. Data moves between devices by JAX's collectives and lax.ppermute only.
A program may use at most 64 MiB of HBM per device.

```python
import math
import jax
import jax.numpy as jnp
from jax import lax

LEVELS = 16
DEVICE_GRID_TALL = 64
DEVICE_GRID_WIDE = 128
FIELDS = 8
REMAP_PIECE_SITES = 128
INTERSECTIONS = 6
BLOCKS = 64
SUBSTEPS = 4
PATCHES = 64
GRID_ROWS = 4096
GRID_COLS = 512
N_GX = 16
N_GY = 4


def set_ends(drawn, own_key, smallest, largest):
    longest = drawn.shape.index(max(drawn.shape))
    spots = []
    for shift in (0, 1):
        where = [jax.random.randint(jax.random.fold_in(own_key, axis), (), 0, length) for axis, length in enumerate(drawn.shape)]
        where[longest] = (where[longest] + shift) % drawn.shape[longest]
        spots.append(tuple(where))
    return drawn.at[spots[0]].set(smallest).at[spots[1]].set(largest)


def levels(rng, shape, shards, smallest, largest):
    def one(dim, shards_of):
        steps = jax.random.uniform(jax.random.fold_in(jax.random.fold_in(rng, 6), dim), (shards_of,), jnp.float32, smallest / len(shards), largest / len(shards))
        return jnp.repeat(jnp.exp(steps), shape[dim] // shards_of).reshape((-1,) + (1,) * (len(shape) - dim - 1))

    factor_of = one(*shards[0])
    for cut in shards[1:]:
        factor_of = factor_of * one(*cut)
    return factor_of


def noise(stream_key, dims, scale, most, cuts=(), held_as=jnp.bfloat16):
    entries = scale * jax.random.normal(stream_key, dims, jnp.float32)
    if cuts:
        entries = entries * levels(stream_key, dims, cuts, -0.22, 0.18)
    return jnp.clip(entries, -most, most).astype(held_as)


def setup_inputs(seed: int = 0) -> dict:
    seeds = jax.random.split(jax.random.key(seed), 10)
    return {
        "state": noise(seeds[0], (LEVELS, GRID_ROWS, GRID_COLS), 1.0, 6.0, ((1, 64), (2, 4)), jnp.float32),
        "winds": jnp.clip(jax.random.uniform(seeds[1], (2, LEVELS, GRID_ROWS, GRID_COLS), jnp.float32, -0.2, 0.2) * levels(seeds[1], (2, LEVELS, GRID_ROWS, GRID_COLS), ((2, 64), (3, 4)), -0.4, 0.0), -0.2, 0.2),
        "diffusivity": jnp.clip(jnp.exp(jax.random.uniform(seeds[2], (2, LEVELS), jnp.float32, math.log(0.05), math.log(0.2))), 0.05, 0.2),
        "coupling": noise(seeds[3], (FIELDS, LEVELS), LEVELS ** -0.5, 1.5, (), jnp.float32),
        "heat_coef": jnp.clip(jax.random.uniform(seeds[4], (FIELDS,), jnp.float32, 0.2, 0.6), 0.2, 0.6),
        "remap_blocks": noise(seeds[5], (BLOCKS, REMAP_PIECE_SITES, REMAP_PIECE_SITES), (REMAP_PIECE_SITES * INTERSECTIONS) ** -0.5, 0.21875),
        "source_patch": set_ends(jax.random.randint(seeds[6], (N_GX, N_GY, PATCHES, INTERSECTIONS), 0, 3 * PATCHES), jax.random.fold_in(seeds[6], 1), 0, (3 * PATCHES) - 1).astype(jnp.int32),
        "block_ids": set_ends(jax.random.randint(seeds[7], (N_GX, N_GY, PATCHES, INTERSECTIONS), 0, BLOCKS), jax.random.fold_in(seeds[7], 1), 0, BLOCKS - 1).astype(jnp.int32),
        "land_sea": set_ends((jax.random.randint(seeds[8], (N_GX, N_GY, PATCHES), 0, 3) < 2).astype(jnp.int32), jax.random.fold_in(seeds[8], 1), 0, 1),
    }


def advance(field, east_wind, north_wind, rate):
    padded = jnp.pad(field, ((0, 0), (1, 1), (1, 1)))
    north = padded[:, :-2, 1:-1]
    south = padded[:, 2:, 1:-1]
    west = padded[:, 1:-1, :-2]
    east = padded[:, 1:-1, 2:]
    return field - 0.5 * east_wind * (east - west) - 0.5 * north_wind * (south - north) + rate * (north + south + east + west - 4.0 * field)


def reference(state, winds, diffusivity, coupling, heat_coef, remap_blocks, source_patch, block_ids, land_sea):
    split = 3 * N_GX * DEVICE_GRID_TALL
    runs_along_line = DEVICE_GRID_WIDE // REMAP_PIECE_SITES
    atmos = state[:, :split]
    ocean = state[:, split:]
    atmos_wind = winds[:, :, :split]
    ocean_wind = winds[:, :, split:]
    atmos_rate = diffusivity[0][:, None, None]
    ocean_rate = diffusivity[1][:, None, None]
    total = jnp.zeros((FIELDS,) + atmos.shape[1:], jnp.float32)
    for step in range(SUBSTEPS):
        atmos = advance(atmos, atmos_wind[0], atmos_wind[1], atmos_rate)
        total = total + jnp.einsum("fl,lrc->frc", coupling, atmos, precision=lax.Precision.HIGHEST)
        ocean = advance(ocean, ocean_wind[0], ocean_wind[1], ocean_rate)
    averaged_exchange = total / float(SUBSTEPS)
    rounded = averaged_exchange.astype(jnp.bfloat16)
    device_piece_sequence = rounded.reshape(FIELDS, 3, N_GX, DEVICE_GRID_TALL, N_GY, runs_along_line, REMAP_PIECE_SITES)
    device_piece_sequence = device_piece_sequence.transpose(2, 4, 1, 3, 5, 0, 6).reshape(N_GX * N_GY, 3 * PATCHES, FIELDS, REMAP_PIECE_SITES)
    uppermost_layer = ocean[0].reshape(N_GX, DEVICE_GRID_TALL, N_GY, runs_along_line, REMAP_PIECE_SITES)
    uppermost_layer = uppermost_layer.transpose(0, 2, 1, 3, 4).reshape(N_GX * N_GY, PATCHES, REMAP_PIECE_SITES)
    donor_sequence = source_patch.reshape(N_GX * N_GY, PATCHES, INTERSECTIONS)
    marine_parts_sequence = block_ids.reshape(N_GX * N_GY, PATCHES, INTERSECTIONS)
    water_indicator = land_sea.reshape(N_GX * N_GY, PATCHES)

    def lone_device_piece(items):
        patches, source, block, surface_top, sea = items
        acc = jnp.zeros((PATCHES, FIELDS, REMAP_PIECE_SITES), jnp.float32)
        for entry in range(INTERSECTIONS):
            picked = patches[source[:, entry]].astype(jnp.float32)
            weights = remap_blocks[block[:, entry]].astype(jnp.float32)
            acc = acc + jnp.einsum("nfp,nqp->nfq", picked, weights, precision=lax.Precision.HIGHEST)
        thermal_forcing = jnp.sum(heat_coef[:, None] * acc, axis=-2)
        water_share = sea.astype(jnp.float32)
        return surface_top + water_share[:, None] * thermal_forcing, water_share[:, None, None] * acc

    marine_skin_warmth, marine_boundary_forcing = lax.map(lone_device_piece, (device_piece_sequence, donor_sequence, marine_parts_sequence, uppermost_layer, water_indicator))
    marine_skin_warmth = marine_skin_warmth.reshape(N_GX, N_GY, DEVICE_GRID_TALL, runs_along_line, REMAP_PIECE_SITES).transpose(0, 2, 1, 3, 4).reshape(N_GX * DEVICE_GRID_TALL, N_GY * DEVICE_GRID_WIDE)
    marine_boundary_forcing = marine_boundary_forcing.reshape(N_GX, N_GY, DEVICE_GRID_TALL, runs_along_line, FIELDS, REMAP_PIECE_SITES)
    marine_boundary_forcing = marine_boundary_forcing.transpose(4, 0, 2, 1, 3, 5).reshape(FIELDS, N_GX * DEVICE_GRID_TALL, N_GY * DEVICE_GRID_WIDE)
    state_out = jnp.concatenate([atmos, ocean], axis=1)
    boundary_field = jnp.concatenate([averaged_exchange[0], marine_skin_warmth], axis=0)
    fluxes = jnp.concatenate([averaged_exchange, marine_boundary_forcing], axis=1)
    return state_out, boundary_field, fluxes
```

```python
import jax
import jax.numpy as jnp
from jax import lax
from jax.experimental import pallas as pl
from jax.experimental.pallas import tpu as pltpu
from jax.sharding import PartitionSpec as P

FIELDS = 8
LEVELS = 16
SUBSTEPS = 4
ROWS = 64
COLS = 128
TILES = ROWS // 8
BASE = 16
DEEP = ROWS + 32
F32 = jnp.float32
BF16 = jnp.bfloat16

VMEM = pl.BlockSpec(memory_space=pltpu.VMEM)
SMEM = pl.BlockSpec(memory_space=pltpu.SMEM)
ANY = pl.BlockSpec(memory_space=pl.ANY)


def sub_ids():
    return lax.broadcasted_iota(jnp.int32, (8, COLS), 0)


def lane_ids():
    return lax.broadcasted_iota(jnp.int32, (8, COLS), 1)


def edge_rows_kernel(st_top, st_low, wi_top, wi_low, to_up, to_down, sheet_up, sheet_down):
    upper = sub_ids() < 4
    for l in range(LEVELS):
        top, low = st_top[l], st_low[l]
        top_hi, low_hi = top.astype(BF16).astype(F32), low.astype(BF16).astype(F32)
        sheet_up[8 * l : 8 * l + 8] = jnp.where(upper, top_hi, pltpu.roll(top - top_hi, 4, 0))
        sheet_down[8 * l : 8 * l + 8] = jnp.where(upper, pltpu.roll(low_hi, 4, 0), low - low_hi)
        k = LEVELS + l
        sheet_up[8 * k : 8 * k + 8] = jnp.where(upper, wi_top[0, l], pltpu.roll(wi_top[1, l], 4, 0))
        sheet_down[8 * k : 8 * k + 8] = jnp.where(upper, pltpu.roll(wi_low[0, l], 4, 0), wi_low[1, l])
    to_up[...] = sheet_up[...].astype(BF16)
    to_down[...] = sheet_down[...].astype(BF16)


def packed(strip, tile, l):
    turned = pltpu.roll(tile, 8 * l + 4, 1)
    return jnp.where((lane_ids() >> 3) == l, turned, strip)


def own_strips_kernel(state, winds, strips):
    def row_tile(t, carry):
        r = pl.multiple_of(t * 8, 8)
        sources = (state, winds.at[0], winds.at[1])
        for c in range(3):
            strip = jnp.zeros((8, COLS), F32)
            for l in range(LEVELS):
                strip = packed(strip, sources[c][l, pl.ds(r, 8), :], l)
            strips[c, pl.ds(r, 8), :] = strip
        return carry

    lax.fori_loop(0, TILES, row_tile, 0)


def edge_columns_kernel(flags, from_below, from_above, own, halo, strip0, to_right, to_left,
                        below, above, full, right_sheet, left_sheet):
    below[...] = from_below[...].astype(F32)
    above[...] = from_above[...].astype(F32)
    upper = sub_ids() < 4
    ok = jnp.where(upper, flags[1], flags[0]) != 0
    full[:, 0:ROWS, :] = own[...]
    parts = [jnp.zeros((8, COLS), F32)] * 3
    for l in range(LEVELS):
        b, a = below[8 * l : 8 * l + 8], above[8 * l : 8 * l + 8]
        s = jnp.where(upper, b + pltpu.roll(b, 4, 0), a + pltpu.roll(a, 4, 0))
        k = LEVELS + l
        b, a = below[8 * k : 8 * k + 8], above[8 * k : 8 * k + 8]
        u = jnp.where(upper, b, pltpu.roll(a, 4, 0))
        v = jnp.where(upper, pltpu.roll(b, 4, 0), a)
        for c, x in enumerate((s, u, v)):
            x = jnp.where(ok, x, 0.0)
            halo[c, 8 * l : 8 * l + 8] = x
            parts[c] = packed(parts[c], x, l)
    for c in range(3):
        full[c, ROWS : ROWS + 8] = parts[c]
    strip0[...] = full[0]
    first = (lane_ids() & 7) < 4
    n = ROWS + 8
    for t in range(TILES + 1):
        r = 8 * t
        s, u, v = full[0, r : r + 8], full[1, r : r + 8], full[2, r : r + 8]
        hi = s.astype(BF16).astype(F32)
        lo = s - hi
        right_sheet[r : r + 8] = jnp.where(first, hi, pltpu.roll(lo, 4, 1))
        left_sheet[r : r + 8] = jnp.where(first, pltpu.roll(lo, COLS - 4, 1), hi)
        right_sheet[n + r : n + r + 8] = jnp.where(first, u, pltpu.roll(v, 4, 1))
        left_sheet[n + r : n + r + 8] = jnp.where(first, pltpu.roll(v, COLS - 4, 1), u)
    to_right[...] = right_sheet[...].astype(BF16)
    to_left[...] = left_sheet[...].astype(BF16)


def stencil(s, n, so, w, e, u, v, d):
    drift = u * (e - w) + v * (so - n)
    return s + d * ((n + so) + (w + e) - 4.0 * s) - 0.5 * drift


def substeps_kernel(flags, diffusivity, coupling, state, winds, halo, strip0, from_left, from_right,
                    state_out, fluxes, boundary, rounded,
                    cells, strips, inner, wind_strips, rate_strip, rate_halo_ok, total, left, right):
    lane = lane_ids()
    sub = sub_ids()
    upper = sub < 4
    place = lane & 7
    first = place < 4
    last_lane, first_lane = lane == COLS - 1, lane == 0
    inner_left, inner_right = place == 3, place == 4
    ocean = flags[4]
    is_ocean = ocean == 1

    left[...] = from_left[...].astype(F32)
    right[...] = from_right[...].astype(F32)
    side_ok = jnp.where(first, flags[2], flags[3]) != 0
    row_ok = jnp.where(upper, flags[1], flags[0]) != 0
    n = ROWS + 8
    rate = jnp.zeros((8, COLS), F32)
    for l in range(LEVELS):
        rate = jnp.where((lane >> 3) == l, diffusivity[ocean, l], rate)
    rate = jnp.where(side_ok, rate, 0.0)
    rate_strip[0:8] = rate
    rate_strip[8:16] = jnp.where(row_ok, rate, 0.0)
    rate_halo_ok[...] = jnp.where(row_ok, 1.0, 0.0)

    def put_strip(buf, t, x):
        if t < TILES:
            strips[buf, BASE + 8 * t : BASE + 8 * t + 8] = x
        else:
            strips[buf, BASE - 8 : BASE] = x
            strips[buf, BASE + ROWS : BASE + ROWS + 8] = x

    for t in range(TILES + 1):
        r = 8 * t
        a, b = left[r : r + 8], right[r : r + 8]
        s = jnp.where(first, a + pltpu.roll(a, COLS - 4, 1), b + pltpu.roll(b, 4, 1))
        put_strip(0, t, jnp.where(side_ok, s, 0.0))
        a, b = left[n + r : n + r + 8], right[n + r : n + r + 8]
        u = jnp.where(first, a, b)
        v = jnp.where(first, pltpu.roll(a, COLS - 4, 1), pltpu.roll(b, 4, 1))
        wind_strips[0, r : r + 8] = jnp.where(side_ok, u, 0.0)
        wind_strips[1, r : r + 8] = jnp.where(side_ok, v, 0.0)
        inner[0, r : r + 8] = strip0[r : r + 8]

    def copy_level(l, carry):
        h = pl.multiple_of(8 * l, 8)
        cells[0, l, BASE : BASE + ROWS] = state[l]
        x = halo[0, pl.ds(h, 8), :]
        cells[0, l, BASE - 8 : BASE] = x
        cells[0, l, BASE + ROWS : BASE + ROWS + 8] = x
        return carry

    lax.fori_loop(0, LEVELS, copy_level, 0)

    def rows_of(load, t):
        if t < TILES:
            r = BASE + 8 * t
            return load(r), load(r - 1), load(r + 1)
        low, up = BASE + ROWS, BASE - 8
        north = jnp.where(upper, load(low - 1), load(up - 1))
        south = jnp.where(upper, load(low + 1), load(up + 1))
        return load(low), north, south

    for step in range(SUBSTEPS):
        now, later = step % 2, (step + 1) % 2
        last = step == SUBSTEPS - 1
        count = TILES if last else TILES + 1
        if not last:
            for t in range(count):
                s, no, so = rows_of(lambda r: strips[now, r : r + 8], t)
                edge = inner[now, 8 * t : 8 * t + 8]
                w = pltpu.roll(jnp.where(inner_left, edge, s), 1, 1)
                e = pltpu.roll(jnp.where(inner_right, edge, s), COLS - 1, 1)
                u, v = wind_strips[0, 8 * t : 8 * t + 8], wind_strips[1, 8 * t : 8 * t + 8]
                d = rate_strip[0:8] if t < TILES else rate_strip[8:16]
                put_strip(later, t, stencil(s, no, so, w, e, u, v, d))

        def level(l, carry):
            h = pl.multiple_of(8 * l, 8)
            d_level = diffusivity[ocean, l]
            mine = (lane >> 3) == l
            for t in range(count):
                s, no, so = rows_of(lambda r: cells[now, l, r : r + 8, :], t)
                r = BASE + 8 * t
                side = pltpu.roll(strips[now, r : r + 8], COLS - 4 - 8 * l, 1)
                w = pltpu.roll(jnp.where(last_lane, side, s), 1, 1)
                e = pltpu.roll(jnp.where(first_lane, side, s), COLS - 1, 1)
                if t < TILES:
                    u, v = winds[0, l, 8 * t : 8 * t + 8, :], winds[1, l, 8 * t : 8 * t + 8, :]
                    d = d_level
                else:
                    u, v = halo[1, pl.ds(h, 8), :], halo[2, pl.ds(h, 8), :]
                    d = d_level * rate_halo_ok[...]
                x = stencil(s, no, so, w, e, u, v, d)
                if not last:
                    if t < TILES:
                        cells[later, l, r : r + 8, :] = x
                    else:
                        cells[later, l, BASE - 8 : BASE, :] = x
                        cells[later, l, BASE + ROWS : BASE + ROWS + 8, :] = x
                    turned = pltpu.roll(x, 8 * l + 4, 1)
                    old = inner[later, 8 * t : 8 * t + 8]
                    inner[later, 8 * t : 8 * t + 8] = jnp.where(mine, turned, old)
                else:
                    state_out[l, 8 * t : 8 * t + 8, :] = x
                if t < TILES:
                    if step == 0:
                        total[l, 8 * t : 8 * t + 8, :] = x
                    else:
                        total[l, 8 * t : 8 * t + 8, :] = total[l, 8 * t : 8 * t + 8, :] + x
            return carry

        if step == 0:
            inner[later] = jnp.zeros((n, COLS), F32)
        lax.fori_loop(0, LEVELS, level, 0)

    def flux(t, carry):
        r = pl.multiple_of(16 * t, 16)
        sums = [None] * FIELDS
        for l in range(LEVELS):
            x = total[l, pl.ds(r, 16), :]
            for f in range(FIELDS):
                term = coupling[f, l] * x
                sums[f] = term if l == 0 else sums[f] + term
        for f in range(FIELDS):
            mean = sums[f] * (1.0 / SUBSTEPS)
            fluxes[f, pl.ds(r, 16), :] = mean
            rounded[pl.ds(pl.multiple_of(f * ROWS + r, 16), 16), :] = mean.astype(BF16)
            if f == 0:
                boundary[pl.ds(r, 16), :] = jnp.where(is_ocean, state_out[0, pl.ds(r, 16), :], mean)
        return carry

    lax.fori_loop(0, ROWS // 16, flux, 0)


def remap_kernel(flags, source, blocks, sea, heat, gathered, weights, flux_in, boundary_in,
                 flux_out, boundary_out, patches, remapped, surface, sems):
    @pl.when(flags[4] == 1)
    def _():
        fetch = pltpu.make_async_copy(boundary_in, surface, sems.at[0])
        fetch.start()
        patches[...] = gathered[...].astype(F32)

        def patch(o, carry):
            total = jnp.zeros((FIELDS, COLS), F32)
            for entry in range(6):
                where = source[o, entry]
                start = (where >> 6) * (FIELDS * ROWS) + (where & 63)
                picked = patches[pl.ds(start, FIELDS, stride=ROWS), :].astype(BF16)
                block = weights[blocks[o, entry]]
                total = total + lax.dot_general(
                    picked, block, (((1,), (1,)), ((), ())), preferred_element_type=F32
                )
            remapped[pl.ds(o, FIELDS, stride=ROWS), :] = total * sea[0, o].astype(F32)
            return carry

        lax.fori_loop(0, ROWS, patch, 0, unroll=4)
        send = pltpu.make_async_copy(remapped, flux_out, sems.at[1])
        send.start()
        warmth = jnp.zeros((ROWS, COLS), F32)
        for f in range(FIELDS):
            warmth = warmth + heat[f] * remapped[f * ROWS : (f + 1) * ROWS, :]
        fetch.wait()
        surface[...] = surface[...] + warmth
        put = pltpu.make_async_copy(surface, boundary_out, sems.at[2])
        put.start()
        send.wait()
        put.wait()


def body(
    state, winds, diffusivity, coupling, heat_coef, remap_blocks, source_patch, block_ids, land_sea
):
    group = lax.axis_index("grp")
    row_tile = lax.axis_index("gx")
    column_tile = lax.axis_index("gy")
    tiles_x = lax.axis_size("gx")
    tiles_y = lax.axis_size("gy")
    groups = lax.axis_size("grp")
    ocean = group == groups - 1
    line = group * tiles_x + row_tile
    top = (line == 0) | (ocean & (row_tile == 0))
    bottom = (row_tile == tiles_x - 1) & (group >= groups - 2)
    flags = jnp.stack(
        [~top, ~bottom, column_tile > 0, column_tile < tiles_y - 1, ocean]
    ).astype(jnp.int32)

    def ring(x, axis, shift):
        count = lax.axis_size(axis)
        return lax.ppermute(x, axis, [(i, (i + shift) % count) for i in range(count)])

    sheet = jax.ShapeDtypeStruct((2 * LEVELS * 8, COLS), BF16)
    first_rows = pl.BlockSpec((LEVELS, 8, COLS), lambda i: (0, 0, 0))
    last_rows = pl.BlockSpec((LEVELS, 8, COLS), lambda i: (0, TILES - 1, 0))
    first_winds = pl.BlockSpec((2, LEVELS, 8, COLS), lambda i: (0, 0, 0, 0))
    last_winds = pl.BlockSpec((2, LEVELS, 8, COLS), lambda i: (0, 0, TILES - 1, 0))
    whole = pl.BlockSpec(sheet.shape, lambda i: (0, 0))
    to_up, to_down = pl.pallas_call(
        edge_rows_kernel,
        grid=(1,),
        in_specs=[first_rows, last_rows, first_winds, last_winds],
        out_specs=[whole, whole],
        out_shape=[sheet, sheet],
        scratch_shapes=[pltpu.VMEM(sheet.shape, F32)] * 2,
        name="edge_rows",
    )(state, state, winds, winds)
    from_below = ring(to_up, ("grp", "gx"), -1)
    from_above = ring(to_down, ("grp", "gx"), 1)
    own = pl.pallas_call(
        own_strips_kernel,
        in_specs=[VMEM, VMEM],
        out_specs=VMEM,
        out_shape=jax.ShapeDtypeStruct((3, ROWS, COLS), F32),
        name="own_strips",
    )(state, winds)
    n = ROWS + 8
    columns = jax.ShapeDtypeStruct((2 * n, COLS), BF16)
    halo, strip0, to_right, to_left = pl.pallas_call(
        edge_columns_kernel,
        in_specs=[SMEM, VMEM, VMEM, VMEM],
        out_specs=[VMEM] * 4,
        out_shape=[
            jax.ShapeDtypeStruct((3, LEVELS * 8, COLS), F32),
            jax.ShapeDtypeStruct((n, COLS), F32),
            columns,
            columns,
        ],
        scratch_shapes=[
            pltpu.VMEM(sheet.shape, F32),
            pltpu.VMEM(sheet.shape, F32),
            pltpu.VMEM((3, n, COLS), F32),
            pltpu.VMEM((2 * n, COLS), F32),
            pltpu.VMEM((2 * n, COLS), F32),
        ],
        name="edge_columns",
    )(flags, from_below, from_above, own)
    from_left = ring(to_right, "gy", 1)
    from_right = ring(to_left, "gy", -1)
    state_out, fluxes, boundary, rounded = pl.pallas_call(
        substeps_kernel,
        in_specs=[SMEM] * 3 + [VMEM] * 6,
        out_specs=[VMEM] * 4,
        out_shape=[
            jax.ShapeDtypeStruct(state.shape, F32),
            jax.ShapeDtypeStruct((FIELDS, ROWS, COLS), F32),
            jax.ShapeDtypeStruct((ROWS, COLS), F32),
            jax.ShapeDtypeStruct((FIELDS * ROWS, COLS), BF16),
        ],
        scratch_shapes=[
            pltpu.VMEM((2, LEVELS, DEEP, COLS), F32),
            pltpu.VMEM((2, DEEP, COLS), F32),
            pltpu.VMEM((2, n, COLS), F32),
            pltpu.VMEM((2, n, COLS), F32),
            pltpu.VMEM((16, COLS), F32),
            pltpu.VMEM((8, COLS), F32),
            pltpu.VMEM((LEVELS, ROWS, COLS), F32),
            pltpu.VMEM((2 * n, COLS), F32),
            pltpu.VMEM((2 * n, COLS), F32),
        ],
        compiler_params=pltpu.CompilerParams(vmem_limit_bytes=16 * 2**20),
        name="substeps",
    )(flags, diffusivity, coupling, state, winds, halo, strip0, from_left, from_right)
    gathered = lax.all_gather(rounded, "grp", axis=0, tiled=True)
    fluxes, boundary = pl.pallas_call(
        remap_kernel,
        in_specs=[SMEM] * 5 + [VMEM] * 2 + [ANY] * 2,
        out_specs=[ANY] * 2,
        out_shape=[
            jax.ShapeDtypeStruct((FIELDS * ROWS, COLS), F32),
            jax.ShapeDtypeStruct((ROWS, COLS), F32),
        ],
        input_output_aliases={7: 0, 8: 1},
        scratch_shapes=[
            pltpu.VMEM(gathered.shape, F32),
            pltpu.VMEM((FIELDS * ROWS, COLS), F32),
            pltpu.VMEM((ROWS, COLS), F32),
            pltpu.SemaphoreType.DMA((3,)),
        ],
        compiler_params=pltpu.CompilerParams(vmem_limit_bytes=16 * 2**20),
        name="remap",
    )(
        flags,
        source_patch[0, 0],
        block_ids[0, 0],
        land_sea[0],
        heat_coef,
        gathered,
        remap_blocks,
        fluxes.reshape(FIELDS * ROWS, COLS),
        boundary,
    )
    return state_out, boundary, fluxes.reshape(FIELDS, ROWS, COLS)


def solution(mesh):
    return jax.shard_map(
        body,
        mesh=mesh,
        in_specs=(
            P(None, ("grp", "gx"), "gy"),
            P(None, None, ("grp", "gx"), "gy"),
            P(),
            P(),
            P(),
            P(),
            P("gx", "gy", None, None),
            P("gx", "gy", None, None),
            P("gx", "gy", None),
        ),
        out_specs=(
            P(None, ("grp", "gx"), "gy"),
            P(("grp", "gx"), "gy"),
            P(None, ("grp", "gx"), "gy"),
        ),
        check_vma=False,
    )
```

```python
import jax
import jax.numpy as jnp
from jax import lax
from jax.experimental import pallas as pl
from jax.experimental.pallas import tpu as pltpu
from jax.sharding import PartitionSpec as P

FIELDS = 8
LEVELS = 16
SUBSTEPS = 4
INTERSECTIONS = 6
ROWS = 64
COLS = 128
TILES = ROWS // 8
BASE = 16
DEEP = ROWS + 32
UNROLL = 4
BLOCK = 8
FLUX_ROWS = 32
FLUX_ON = True
STEPS = 4
CHUNK = 16
F32 = jnp.float32
BF16 = jnp.bfloat16

VMEM = pl.BlockSpec(memory_space=pltpu.VMEM)
SMEM = pl.BlockSpec(memory_space=pltpu.SMEM)
ANY = pl.BlockSpec(memory_space=pl.ANY)
HBM = pl.BlockSpec(memory_space=pltpu.HBM)


def sub_ids():
    return lax.broadcasted_iota(jnp.int32, (8, COLS), 0)


def lane_ids():
    return lax.broadcasted_iota(jnp.int32, (8, COLS), 1)


def edge_rows_kernel(state, winds, to_up, to_down, st_top, st_low, wi_top, wi_low,
                     sheet_up, sheet_down, sems):
    first, last = slice(0, 8), slice(ROWS - 8, ROWS)
    fetches = [
        pltpu.make_async_copy(source, target, sems.at[i])
        for i, (source, target) in enumerate((
            (winds.at[:, :, first], wi_top),
            (winds.at[:, :, last], wi_low),
            (state.at[:, first], st_top),
            (state.at[:, last], st_low),
        ))
    ]
    for fetch in fetches:
        fetch.start()
    for fetch in fetches:
        fetch.wait()
    upper = sub_ids() < 4
    for l in range(LEVELS):
        top, low = st_top[l], st_low[l]
        top_hi, low_hi = top.astype(BF16).astype(F32), low.astype(BF16).astype(F32)
        sheet_up[8 * l : 8 * l + 8] = jnp.where(upper, top_hi, pltpu.roll(top - top_hi, 4, 0))
        sheet_down[8 * l : 8 * l + 8] = jnp.where(upper, pltpu.roll(low_hi, 4, 0), low - low_hi)
        k = LEVELS + l
        sheet_up[8 * k : 8 * k + 8] = jnp.where(upper, wi_top[0, l], pltpu.roll(wi_top[1, l], 4, 0))
        sheet_down[8 * k : 8 * k + 8] = jnp.where(upper, pltpu.roll(wi_low[0, l], 4, 0), wi_low[1, l])
    to_up[...] = sheet_up[...].astype(BF16)
    to_down[...] = sheet_down[...].astype(BF16)


def packed(strip, tile, l):
    turned = pltpu.roll(tile, 8 * l + 4, 1)
    return jnp.where((lane_ids() >> 3) == l, turned, strip)


def own_strips_kernel(state, winds, strips):
    def row_tile(t, carry):
        r = pl.multiple_of(t * 8, 8)
        sources = (state, winds.at[0], winds.at[1])
        for c in range(3):
            strip = jnp.zeros((8, COLS), F32)
            for l in range(LEVELS):
                strip = packed(strip, sources[c][l, pl.ds(r, 8), :], l)
            strips[c, pl.ds(r, 8), :] = strip
        return carry

    lax.fori_loop(0, TILES, row_tile, 0)


def edge_columns_kernel(masks, from_below, from_above, own, halo, strip0, to_right, to_left,
                        below, above, full, right_sheet, left_sheet):
    below[...] = from_below[...].astype(F32)
    above[...] = from_above[...].astype(F32)
    upper = sub_ids() < 4
    ok = masks[0]
    full[:, 0:ROWS, :] = own[...]
    parts = [jnp.zeros((8, COLS), F32)] * 3
    for l in range(LEVELS):
        b, a = below[8 * l : 8 * l + 8], above[8 * l : 8 * l + 8]
        s = jnp.where(upper, b + pltpu.roll(b, 4, 0), a + pltpu.roll(a, 4, 0))
        k = LEVELS + l
        b, a = below[8 * k : 8 * k + 8], above[8 * k : 8 * k + 8]
        u = jnp.where(upper, b, pltpu.roll(a, 4, 0))
        v = jnp.where(upper, pltpu.roll(b, 4, 0), a)
        for c, x in enumerate((s, u, v)):
            x = x * ok
            halo[c, 8 * l : 8 * l + 8] = x
            parts[c] = packed(parts[c], x, l)
    for c in range(3):
        full[c, ROWS : ROWS + 8] = parts[c]
    strip0[...] = full[0]
    first = (lane_ids() & 7) < 4
    n = ROWS + 8
    for t in range(TILES + 1):
        r = 8 * t
        s, u, v = full[0, r : r + 8], full[1, r : r + 8], full[2, r : r + 8]
        hi = s.astype(BF16).astype(F32)
        lo = s - hi
        right_sheet[r : r + 8] = jnp.where(first, hi, pltpu.roll(lo, 4, 1))
        left_sheet[r : r + 8] = jnp.where(first, pltpu.roll(lo, COLS - 4, 1), hi)
        right_sheet[n + r : n + r + 8] = jnp.where(first, u, pltpu.roll(v, 4, 1))
        left_sheet[n + r : n + r + 8] = jnp.where(first, pltpu.roll(v, COLS - 4, 1), u)
    to_right[...] = right_sheet[...].astype(BF16)
    to_left[...] = left_sheet[...].astype(BF16)


def stencil(s, n, so, w, e, u, v, d, c):
    drift = u * (e - w) + v * (so - n)
    return c * s + d * ((n + so) + (w + e)) - 0.5 * drift


def substeps_kernel(scalars, masks, state, winds, halo, strip0, from_left, from_right,
                    state_out, fluxes, boundary, rounded,
                    cells0, cells1, cells2, cells3, strips0, strips1, strips2, strips3,
                    inner0, inner1, inner2, inner3, wind_strips, left, right):
    cells = (cells0, cells1, cells2, cells3)
    strips = (strips0, strips1, strips2, strips3)
    inner = (inner0, inner1, inner2, inner3)
    upper = sub_ids() < 4
    is_ocean = scalars[0] != 0.0
    n = ROWS + 8
    own = slice(BASE, BASE + ROWS)
    high, low = slice(BASE - 8, BASE), slice(BASE + ROWS, BASE + ROWS + 8)

    def lanes(rows):
        return lax.broadcasted_iota(jnp.int32, (rows, COLS), 1)

    row_one, side_one, rate = masks[0], masks[1], masks[2]
    rate_low = rate * row_one
    left[...] = from_left[...].astype(F32)
    right[...] = from_right[...].astype(F32)
    first = (lane_ids() & 7) < 4
    for t in range(TILES + 1):
        r = slice(8 * t, 8 * t + 8)
        a, b = left[r], right[r]
        x = jnp.where(first, a + pltpu.roll(a, COLS - 4, 1), b + pltpu.roll(b, 4, 1)) * side_one
        if t < TILES:
            strips0[BASE + 8 * t : BASE + 8 * t + 8] = x
        else:
            strips0[high] = x
            strips0[low] = x
        a, b = left[n + 8 * t : n + 8 * t + 8], right[n + 8 * t : n + 8 * t + 8]
        wind_strips[0, r] = jnp.where(first, a, b) * side_one
        wind_strips[1, r] = jnp.where(first, pltpu.roll(a, COLS - 4, 1), pltpu.roll(b, 4, 1)) * side_one
        inner0[r] = strip0[r]

    def copy_level(l, carry):
        h = pl.multiple_of(8 * l, 8)
        cells0[l, own] = state[l]
        x = halo[0, pl.ds(h, 8), :]
        cells0[l, high] = x
        cells0[l, low] = x
        return carry

    lax.fori_loop(0, LEVELS, copy_level, 0, unroll=2)

    def halo_rows(load):
        d, u = BASE + ROWS, BASE - 8
        return (
            load(d),
            jnp.where(upper, load(d - 1), load(u - 1)),
            jnp.where(upper, load(d + 1), load(u + 1)),
        )

    def beside(s, west_lane, west, east_lane, east):
        return (
            pltpu.roll(jnp.where(west_lane, west, s), 1, 1),
            pltpu.roll(jnp.where(east_lane, east, s), COLS - 1, 1),
        )

    lane = lanes(BLOCK)
    lane8 = lane_ids()
    place = lane8 & 7

    for step in range(STEPS):
        last = step == SUBSTEPS - 1
        src, strip, edge = cells[step], strips[step], inner[step]
        if not last:
            dst, strip_next, edge_next = cells[step + 1], strips[step + 1], inner[step + 1]
            for t in range(TILES + 1):
                r = BASE + 8 * t
                if t < TILES:
                    s, no, so = strip[r : r + 8], strip[r - 1 : r + 7], strip[r + 1 : r + 9]
                else:
                    s, no, so = halo_rows(lambda r: strip[r : r + 8])
                k = slice(8 * t, 8 * t + 8)
                w, e = beside(s, place == 3, edge[k], place == 4, edge[k])
                d = rate if t < TILES else rate_low
                x = stencil(s, no, so, w, e, wind_strips[0, k], wind_strips[1, k], d, 1.0 - 4.0 * d)
                if t < TILES:
                    strip_next[r : r + 8] = x
                else:
                    strip_next[high] = x
                    strip_next[low] = x

        def level(l, carry):
            h = pl.multiple_of(8 * l, 8)
            d = scalars[1 + l]
            c = 1.0 - 4.0 * d
            turn = COLS - 4 - 8 * l
            mine = (lane >> 3) == l
            for t in range(ROWS // BLOCK):
                k = slice(BLOCK * t, BLOCK * (t + 1))
                r = BASE + BLOCK * t
                s = src[l, r : r + BLOCK, :]
                side = pltpu.roll(strip[r : r + BLOCK], turn, 1)
                w, e = beside(s, lane == COLS - 1, side, lane == 0, side)
                x = stencil(s, src[l, r - 1 : r + BLOCK - 1, :], src[l, r + 1 : r + BLOCK + 1, :],
                            w, e, winds[0, l, k, :], winds[1, l, k, :], d, c)
                if last:
                    state_out[l, k, :] = x
                else:
                    dst[l, r : r + BLOCK, :] = x
                    edge_next[k] = jnp.where(mine, pltpu.roll(x, 8 * l + 4, 1), edge_next[k])
            if last:
                return carry
            s, no, so = halo_rows(lambda r: src[l, r : r + 8, :])
            side = pltpu.roll(strip[low], turn, 1)
            w, e = beside(s, lane8 == COLS - 1, side, lane8 == 0, side)
            d = d * row_one
            y = stencil(s, no, so, w, e, halo[1, pl.ds(h, 8), :], halo[2, pl.ds(h, 8), :], d, 1.0 - 4.0 * d)
            edge_next[ROWS:n] = jnp.where(mine[0:8], pltpu.roll(y, 8 * l + 4, 1), edge_next[ROWS:n])
            dst[l, high, :] = y
            dst[l, low, :] = y
            return carry

        lax.fori_loop(0, LEVELS, level, 0, unroll=UNROLL)

    def flux(t, carry):
        r = pl.multiple_of(FLUX_ROWS * t, FLUX_ROWS)
        at = pl.ds(BASE + r, FLUX_ROWS)
        out = pl.ds(r, FLUX_ROWS)
        sums = [None] * FIELDS
        for l in range(LEVELS):
            x = (cells1[l, at, :] + cells2[l, at, :]) + (cells3[l, at, :] + state_out[l, out, :])
            for f in range(FIELDS):
                term = scalars[1 + LEVELS + f * LEVELS + l] * x
                sums[f] = term if l == 0 else sums[f] + term
        for f in range(FIELDS):
            mean = sums[f] * (1.0 / SUBSTEPS)
            fluxes[f, out, :] = mean
            rounded[pl.ds(pl.multiple_of(f * ROWS + r, FLUX_ROWS), FLUX_ROWS), :] = mean.astype(BF16)
            if f == 0:
                boundary[out, :] = jnp.where(is_ocean, state_out[0, out, :], mean)
        return carry

    if FLUX_ON:
        lax.fori_loop(0, ROWS // FLUX_ROWS, flux, 0)


def remap_kernel(table, heat, gathered, weights, flux_in, boundary_in,
                 flux_out, boundary_out, patches, remapped, surface, fetch_sem, flux_sems, surface_sems):
    @pl.when(table[0] == 1)
    def _():
        fetch = pltpu.make_async_copy(boundary_in, surface, fetch_sem.at[0])
        fetch.start()
        size = FIELDS * ROWS
        patches[...] = gathered[0 : 3 * size].astype(F32)
        fetch.wait()

        def sends(i):
            at = pl.ds(pl.multiple_of(i * CHUNK, CHUNK), CHUNK)
            return (
                pltpu.make_async_copy(remapped.at[:, at], flux_out.at[:, at], flux_sems.at[i]),
                pltpu.make_async_copy(surface.at[at], boundary_out.at[at], surface_sems.at[i]),
            )

        def chunk(i, carry):
            at = pl.ds(pl.multiple_of(i * CHUNK, CHUNK), CHUNK)
            for j in range(CHUNK):
                o = i * CHUNK + j
                picked, chosen = [], []
                for entry in range(INTERSECTIONS):
                    at_entry = 1 + ROWS + 2 * ROWS * entry + o
                    start = table[at_entry]
                    picked.append(patches[pl.ds(start, FIELDS, stride=ROWS), :].astype(BF16))
                    chosen.append(weights[table[at_entry + ROWS]])
                total = lax.dot_general(
                    jnp.concatenate(picked, 1),
                    jnp.concatenate(chosen, 1),
                    (((1,), (1,)), ((), ())),
                    preferred_element_type=F32,
                )
                remapped[:, o, :] = total * table[1 + o].astype(F32)
            warmth = surface[at, :]
            for f in range(FIELDS):
                warmth = warmth + heat[f : f + 1] * remapped[f, at, :]
            surface[at, :] = warmth
            for send in sends(i):
                send.start()
            return carry

        lax.fori_loop(0, ROWS // CHUNK, chunk, 0)
        for i in range(ROWS // CHUNK):
            for send in sends(i):
                send.wait()


LIMIT = pltpu.CompilerParams(vmem_limit_bytes=16 * 2**20)
N = ROWS + 8
SHEET = jax.ShapeDtypeStruct((2 * LEVELS * 8, COLS), BF16)
COLUMNS = jax.ShapeDtypeStruct((2 * N, COLS), BF16)


def f32(*shape):
    return jax.ShapeDtypeStruct(shape, F32)


def edge_rows(state, winds):
    return pl.pallas_call(
        edge_rows_kernel,
        in_specs=[HBM, HBM],
        out_specs=[VMEM, VMEM],
        out_shape=[SHEET, SHEET],
        scratch_shapes=[
            *[pltpu.VMEM((LEVELS, 8, COLS), F32)] * 2,
            *[pltpu.VMEM((2, LEVELS, 8, COLS), F32)] * 2,
            *[pltpu.VMEM(SHEET.shape, F32)] * 2,
            pltpu.SemaphoreType.DMA((4,)),
        ],
        compiler_params=LIMIT,
        name="edge_rows",
    )(state, winds)


def own_strips(state, winds):
    return pl.pallas_call(
        own_strips_kernel,
        in_specs=[VMEM, VMEM],
        out_specs=VMEM,
        out_shape=f32(3, ROWS, COLS),
        compiler_params=LIMIT,
        name="own_strips",
    )(state, winds)


def edge_columns(masks, from_below, from_above, own):
    return pl.pallas_call(
        edge_columns_kernel,
        in_specs=[VMEM] * 4,
        out_specs=[VMEM] * 4,
        out_shape=[f32(3, LEVELS * 8, COLS), f32(N, COLS), COLUMNS, COLUMNS],
        scratch_shapes=[
            pltpu.VMEM(SHEET.shape, F32),
            pltpu.VMEM(SHEET.shape, F32),
            pltpu.VMEM((3, N, COLS), F32),
            pltpu.VMEM((2 * N, COLS), F32),
            pltpu.VMEM((2 * N, COLS), F32),
        ],
        compiler_params=LIMIT,
        name="edge_columns",
    )(masks, from_below, from_above, own)


def substeps(scalars, masks, state, winds, halo, strip0, from_left, from_right):
    return pl.pallas_call(
        substeps_kernel,
        in_specs=[SMEM] + [VMEM] * 7,
        out_specs=[VMEM] * 4,
        out_shape=[
            f32(LEVELS, ROWS, COLS),
            f32(FIELDS, ROWS, COLS),
            f32(ROWS, COLS),
            jax.ShapeDtypeStruct((FIELDS * ROWS, COLS), BF16),
        ],
        scratch_shapes=[
            *[pltpu.VMEM((LEVELS, DEEP, COLS), F32)] * 4,
            *[pltpu.VMEM((DEEP, COLS), F32)] * 4,
            *[pltpu.VMEM((N, COLS), F32)] * 4,
            pltpu.VMEM((2, N, COLS), F32),
            pltpu.VMEM((2 * N, COLS), F32),
            pltpu.VMEM((2 * N, COLS), F32),
        ],
        compiler_params=LIMIT,
        name="substeps",
    )(scalars, masks, state, winds, halo, strip0, from_left, from_right)


def remap(table, heat, gathered, weights, fluxes, boundary):
    return pl.pallas_call(
        remap_kernel,
        in_specs=[SMEM] + [VMEM] * 3 + [ANY] * 2,
        out_specs=[ANY] * 2,
        out_shape=[f32(FIELDS, ROWS, COLS), f32(ROWS, COLS)],
        input_output_aliases={4: 0, 5: 1},
        scratch_shapes=[
            pltpu.VMEM((3 * FIELDS * ROWS, COLS), F32),
            pltpu.VMEM((FIELDS, ROWS, COLS), F32),
            pltpu.VMEM((ROWS, COLS), F32),
            pltpu.SemaphoreType.DMA((1,)),
            pltpu.SemaphoreType.DMA((ROWS // CHUNK,)),
            pltpu.SemaphoreType.DMA((ROWS // CHUNK,)),
        ],
        compiler_params=LIMIT,
        name="remap",
    )(table, heat, gathered, weights, fluxes, boundary)


def body(
    state, winds, diffusivity, coupling, heat_coef, remap_blocks, source_patch, block_ids, land_sea
):
    group = lax.axis_index("grp")
    row_tile = lax.axis_index("gx")
    column_tile = lax.axis_index("gy")
    tiles_x = lax.axis_size("gx")
    tiles_y = lax.axis_size("gy")
    groups = lax.axis_size("grp")
    ocean = group == groups - 1
    line = group * tiles_x + row_tile
    top = (line == 0) | (ocean & (row_tile == 0))
    bottom = (row_tile == tiles_x - 1) & (group >= groups - 2)
    row = lax.broadcasted_iota(jnp.int32, (8, COLS), 0)
    lane = lax.broadcasted_iota(jnp.int32, (8, COLS), 1)
    row_one = jnp.where(row < 4, ~bottom, ~top).astype(F32)
    side_one = jnp.where((lane & 7) < 4, column_tile > 0, column_tile < tiles_y - 1).astype(F32)
    own_rate = jnp.where(ocean, diffusivity[1], diffusivity[0])
    rate = jnp.broadcast_to(own_rate[:, None], (LEVELS, 8)).reshape(1, COLS) * side_one
    masks = jnp.stack([row_one, side_one, rate])
    scalars = jnp.concatenate([ocean.astype(F32)[None], own_rate, coupling.reshape(-1)])
    source = source_patch[0, 0].T
    starts = (source // ROWS) * (FIELDS * ROWS) + source % ROWS
    table = jnp.concatenate([
        ocean.astype(jnp.int32)[None],
        land_sea.reshape(-1),
        jnp.concatenate([starts, block_ids[0, 0].T], 1).reshape(-1),
    ])
    heat = jnp.broadcast_to(heat_coef[:, None], (FIELDS, COLS))

    def ring(x, axis, shift):
        count = lax.axis_size(axis)
        return lax.ppermute(x, axis, [(i, (i + shift) % count) for i in range(count)])

    to_up, to_down = edge_rows(state, winds)
    from_below = ring(to_up, ("grp", "gx"), -1)
    from_above = ring(to_down, ("grp", "gx"), 1)
    own = own_strips(state, winds)
    halo, strip0, to_right, to_left = edge_columns(masks, from_below, from_above, own)
    from_left = ring(to_right, "gy", 1)
    from_right = ring(to_left, "gy", -1)
    state_out, fluxes, boundary, rounded = substeps(
        scalars, masks, state, winds, halo, strip0, from_left, from_right
    )
    gathered = lax.all_gather(rounded, "grp", axis=0, tiled=True)
    fluxes, boundary = remap(table, heat, gathered, remap_blocks, fluxes, boundary)
    return state_out, boundary, fluxes


def solution(mesh):
    return jax.shard_map(
        body,
        mesh=mesh,
        in_specs=(
            P(None, ("grp", "gx"), "gy"),
            P(None, None, ("grp", "gx"), "gy"),
            P(),
            P(),
            P(),
            P(),
            P("gx", "gy", None, None),
            P("gx", "gy", None, None),
            P("gx", "gy", None),
        ),
        out_specs=(
            P(None, ("grp", "gx"), "gy"),
            P(("grp", "gx"), "gy"),
            P(None, ("grp", "gx"), "gy"),
        ),
        check_vma=False,
    )
```

```python
import jax
import jax.numpy as jnp
from jax import lax
from jax.experimental import pallas as pl
from jax.experimental.pallas import tpu as pltpu
from jax.sharding import PartitionSpec as P

FIELDS = 8
LEVELS = 16
SUBSTEPS = 4
INTERSECTIONS = 6
ROWS = 64
COLS = 128
TILES = ROWS // 8
BASE = 16
DEEP = ROWS + 32
UNROLL = 4
BLOCK = 8
FLUX_ROWS = 32
STEPS = 4
CHUNK = 32
F32 = jnp.float32
BF16 = jnp.bfloat16

VMEM = pl.BlockSpec(memory_space=pltpu.VMEM)
SMEM = pl.BlockSpec(memory_space=pltpu.SMEM)
ANY = pl.BlockSpec(memory_space=pl.ANY)
HBM = pl.BlockSpec(memory_space=pltpu.HBM)


def sub_ids():
    return lax.broadcasted_iota(jnp.int32, (8, COLS), 0)


def lane_ids():
    return lax.broadcasted_iota(jnp.int32, (8, COLS), 1)


def edge_rows_kernel(state, winds, to_up, to_down, st_top, st_low, wi_top, wi_low,
                     sheet_up, sheet_down, sems):
    first, last = slice(0, 8), slice(ROWS - 8, ROWS)
    fetches = [
        pltpu.make_async_copy(source, target, sems.at[i])
        for i, (source, target) in enumerate((
            (winds.at[:, :, first], wi_top),
            (winds.at[:, :, last], wi_low),
            (state.at[:, first], st_top),
            (state.at[:, last], st_low),
        ))
    ]
    for fetch in fetches:
        fetch.start()
    for fetch in fetches:
        fetch.wait()
    upper = sub_ids() < 4
    for l in range(LEVELS):
        top, low = st_top[l], st_low[l]
        top_hi, low_hi = top.astype(BF16).astype(F32), low.astype(BF16).astype(F32)
        sheet_up[8 * l : 8 * l + 8] = jnp.where(upper, top_hi, pltpu.roll(top - top_hi, 4, 0))
        sheet_down[8 * l : 8 * l + 8] = jnp.where(upper, pltpu.roll(low_hi, 4, 0), low - low_hi)
        k = LEVELS + l
        sheet_up[8 * k : 8 * k + 8] = jnp.where(upper, wi_top[0, l], pltpu.roll(wi_top[1, l], 4, 0))
        sheet_down[8 * k : 8 * k + 8] = jnp.where(upper, pltpu.roll(wi_low[0, l], 4, 0), wi_low[1, l])
    to_up[...] = sheet_up[...].astype(BF16)
    to_down[...] = sheet_down[...].astype(BF16)


def packed(strip, tile, l):
    turned = pltpu.roll(tile, 8 * l + 4, 1)
    return jnp.where((lane_ids() >> 3) == l, turned, strip)


def own_strips_kernel(state, winds, strips):
    def row_tile(t, carry):
        r = pl.multiple_of(t * 8, 8)
        sources = (state, winds.at[0], winds.at[1])
        for c in range(3):
            strip = jnp.zeros((8, COLS), F32)
            for l in range(LEVELS):
                strip = packed(strip, sources[c][l, pl.ds(r, 8), :], l)
            strips[c, pl.ds(r, 8), :] = strip
        return carry

    lax.fori_loop(0, TILES, row_tile, 0)


def edge_columns_kernel(masks, from_below, from_above, own, halo, strip0, to_right, to_left,
                        below, above, full, right_sheet, left_sheet):
    below[...] = from_below[...].astype(F32)
    above[...] = from_above[...].astype(F32)
    upper = sub_ids() < 4
    ok = masks[0]
    full[:, 0:ROWS, :] = own[...]
    parts = [jnp.zeros((8, COLS), F32)] * 3
    for l in range(LEVELS):
        b, a = below[8 * l : 8 * l + 8], above[8 * l : 8 * l + 8]
        s = jnp.where(upper, b + pltpu.roll(b, 4, 0), a + pltpu.roll(a, 4, 0))
        k = LEVELS + l
        b, a = below[8 * k : 8 * k + 8], above[8 * k : 8 * k + 8]
        u = jnp.where(upper, b, pltpu.roll(a, 4, 0))
        v = jnp.where(upper, pltpu.roll(b, 4, 0), a)
        for c, x in enumerate((s, u, v)):
            x = x * ok
            halo[c, 8 * l : 8 * l + 8] = x
            parts[c] = packed(parts[c], x, l)
    for c in range(3):
        full[c, ROWS : ROWS + 8] = parts[c]
    strip0[...] = full[...]
    first = (lane_ids() & 7) < 4
    n = ROWS + 8
    for t in range(TILES + 1):
        r = 8 * t
        s, u, v = full[0, r : r + 8], full[1, r : r + 8], full[2, r : r + 8]
        hi = s.astype(BF16).astype(F32)
        lo = s - hi
        right_sheet[r : r + 8] = jnp.where(first, hi, pltpu.roll(lo, 4, 1))
        left_sheet[r : r + 8] = jnp.where(first, pltpu.roll(lo, COLS - 4, 1), hi)
        right_sheet[n + r : n + r + 8] = jnp.where(first, u, pltpu.roll(v, 4, 1))
        left_sheet[n + r : n + r + 8] = jnp.where(first, pltpu.roll(v, COLS - 4, 1), u)
    to_right[...] = right_sheet[...].astype(BF16)
    to_left[...] = left_sheet[...].astype(BF16)


def stencil(s, n, so, w, e, u, v, d, c):
    drift = u * (e - w) + v * (so - n)
    return c * s + d * ((n + so) + (w + e)) - 0.5 * drift


def substeps_kernel(rates, weights, masks, state, winds, halo, strip0, from_left, from_right,
                    state_out, fluxes, rounded, top,
                    cells0, cells1, cells2, cells3, ready,
                    lefts, rights, sides, left_winds, right_winds, left, right, sems):
    cells = (cells0, cells1, cells2, cells3)
    upper = sub_ids() < 4
    n = ROWS + 8
    own = slice(BASE, BASE + ROWS)
    high, low = slice(BASE - 8, BASE), slice(BASE + ROWS, BASE + ROWS + 8)
    lane = lane_ids()
    place = lane & 7
    first = place < 4
    row_one, side_one, rate = masks[0], masks[1], masks[2]

    def halo_rows(load):
        d, u = BASE + ROWS, BASE - 8
        return (
            load(d),
            jnp.where(upper, load(d - 1), load(u - 1)),
            jnp.where(upper, load(d + 1), load(u + 1)),
        )

    def put(buf, t, x):
        if t < TILES:
            buf[BASE + 8 * t : BASE + 8 * t + 8] = x
        else:
            buf[high] = x
            buf[low] = x

    left[...] = from_left[...].astype(F32)
    right[...] = from_right[...].astype(F32)
    for t in range(TILES + 1):
        r, q = slice(8 * t, 8 * t + 8), slice(n + 8 * t, n + 8 * t + 8)
        a, b = left[r], right[r]
        a = (a + pltpu.roll(a, COLS - 4, 1)) * side_one
        b = (b + pltpu.roll(b, 4, 1)) * side_one
        put(lefts[0], t, jnp.where(first, a, strip0[0, r]))
        put(rights[0], t, jnp.where(first, strip0[0, r], b))
        put(sides[0], t, jnp.where(first, a, b))
        a, b = left[q], right[q]
        left_winds[0, r] = jnp.where(first, a * side_one, strip0[1, r])
        right_winds[0, r] = jnp.where(first, strip0[1, r], b * side_one)
        a, b = pltpu.roll(a, COLS - 4, 1), pltpu.roll(b, 4, 1)
        left_winds[1, r] = jnp.where(first, a * side_one, strip0[2, r])
        right_winds[1, r] = jnp.where(first, strip0[2, r], b * side_one)
    left_rate = jnp.where(first, rate * side_one, rate)
    right_rate = jnp.where(first, rate, rate * side_one)
    for step in range(SUBSTEPS - 1):
        for t in range(TILES + 1):
            r, k = BASE + 8 * t, slice(8 * t, 8 * t + 8)
            new = []
            for strip, wind, d in ((lefts[step], left_winds, left_rate), (rights[step], right_winds, right_rate)):
                if t < TILES:
                    s, no, so = strip[r : r + 8], strip[r - 1 : r + 7], strip[r + 1 : r + 9]
                else:
                    s, no, so = halo_rows(lambda r: strip[r : r + 8])
                    d = d * row_one
                w, e = pltpu.roll(s, 1, 1), pltpu.roll(s, COLS - 1, 1)
                new.append(stencil(s, no, so, w, e, wind[0, k], wind[1, k], d, 1.0 - 4.0 * d))
            if step < SUBSTEPS - 2:
                put(lefts[step + 1], t, new[0])
                put(rights[step + 1], t, new[1])
            put(sides[step + 1], t, jnp.where(first, new[0], new[1]))

    def copy_level(l, carry):
        h = pl.multiple_of(8 * l, 8)
        cells0[l, own] = state[l]
        x = halo[0, pl.ds(h, 8), :]
        cells0[l, high] = x
        cells0[l, low] = x
        return carry

    lax.fori_loop(0, LEVELS, copy_level, 0, unroll=2)

    def beside(s, side, last, first):
        return (
            pltpu.roll(jnp.where(last, side, s), 1, 1),
            pltpu.roll(jnp.where(first, side, s), COLS - 1, 1),
        )

    wide = lax.broadcasted_iota(jnp.int32, (BLOCK, COLS), 1)
    last_wide, first_wide = wide == COLS - 1, wide == 0
    last_lane, first_lane = lane == COLS - 1, lane == 0

    for step in range(SUBSTEPS):
        last = step == SUBSTEPS - 1
        src, strip = cells[step], sides[step]

        def level(l, carry):
            h = pl.multiple_of(8 * l, 8)
            d = rates[pl.ds(l, 1), :]
            c = 1.0 - 4.0 * d
            turn = COLS - 4 - 8 * l
            for t in range(ROWS // BLOCK):
                k = slice(BLOCK * t, BLOCK * (t + 1))
                r = BASE + BLOCK * t
                s = src[l, r : r + BLOCK, :]
                w, e = beside(s, pltpu.roll(strip[r : r + BLOCK], turn, 1), last_wide, first_wide)
                x = stencil(s, src[l, r - 1 : r + BLOCK - 1, :], src[l, r + 1 : r + BLOCK + 1, :],
                            w, e, winds[0, l, k, :], winds[1, l, k, :], d, c)
                if last:
                    ready[l, k, :] = x
                else:
                    cells[step + 1][l, r : r + BLOCK, :] = x
            if last:
                return carry
            s, no, so = halo_rows(lambda r: src[l, r : r + 8, :])
            w, e = beside(s, pltpu.roll(strip[low], turn, 1), last_lane, first_lane)
            d = d * row_one
            y = stencil(s, no, so, w, e, halo[1, pl.ds(h, 8), :], halo[2, pl.ds(h, 8), :], d, 1.0 - 4.0 * d)
            cells[step + 1][l, high, :] = y
            cells[step + 1][l, low, :] = y
            return carry

        if step < STEPS:
            lax.fori_loop(0, LEVELS, level, 0, unroll=UNROLL)

    send = pltpu.make_async_copy(ready, state_out, sems.at[0])
    send.start()

    def flux(t, carry):
        r = pl.multiple_of(FLUX_ROWS * t, FLUX_ROWS)
        at = pl.ds(BASE + r, FLUX_ROWS)
        out = pl.ds(r, FLUX_ROWS)
        sums = [None] * FIELDS
        for l in range(LEVELS):
            x = (cells1[l, at, :] + cells2[l, at, :]) + (cells3[l, at, :] + ready[l, out, :])
            for f in range(FIELDS):
                k = f * LEVELS + l
                term = weights[k : k + 1, :] * x
                sums[f] = term if l == 0 else sums[f] + term
        for f in range(FIELDS):
            mean = sums[f] * (1.0 / SUBSTEPS)
            fluxes[f, out, :] = mean
            rounded[pl.ds(pl.multiple_of(f * ROWS + r, FLUX_ROWS), FLUX_ROWS), :] = mean.astype(BF16)
        return carry

    lax.fori_loop(0, ROWS // FLUX_ROWS, flux, 0)
    top[...] = ready[0]
    send.wait()


def turn_blocks_kernel(blocks, turned):
    def turn(i, carry):
        turned[i] = blocks[i].T
        return carry

    lax.fori_loop(0, blocks.shape[0], turn, 0, unroll=8)


def remap_kernel(words, heat, gathered, weights, fluxes, top, flux_out, boundary_out,
                 table, patches, remapped, surface, table_sem, out_sems, flux_sems, surface_sems):
    size = FIELDS * ROWS
    fetch = pltpu.make_async_copy(words, table, table_sem.at[0])
    fetch.start()
    patches[...] = gathered[0 : 3 * size].astype(F32)
    fetch.wait()
    is_ocean = table[table.shape[0] - 1] == 1

    @pl.when(is_ocean)
    def _():
        def sends(i):
            at = pl.ds(pl.multiple_of(i * CHUNK, CHUNK), CHUNK)
            return (
                pltpu.make_async_copy(remapped.at[:, at], flux_out.at[:, at], flux_sems.at[i]),
                pltpu.make_async_copy(surface.at[at], boundary_out.at[at], surface_sems.at[i]),
            )

        def chunk(i, carry):
            at = pl.ds(pl.multiple_of(i * CHUNK, CHUNK), CHUNK)
            for j in range(CHUNK):
                o = i * CHUNK + j
                picked, chosen = [], []
                for entry in range(INTERSECTIONS):
                    at_entry = ROWS + 2 * ROWS * entry + o
                    start = table[at_entry]
                    picked.append(patches[pl.ds(start, FIELDS, stride=ROWS), :].astype(BF16))
                    chosen.append(weights[table[at_entry + ROWS]])
                total = jnp.dot(
                    jnp.concatenate(picked, 1), jnp.concatenate(chosen, 0), preferred_element_type=F32
                )
                remapped[:, o, :] = total * table[o].astype(F32)
            warmth = top[at, :]
            for f in range(FIELDS):
                warmth = warmth + heat[f : f + 1] * remapped[f, at, :]
            surface[at, :] = warmth
            for send in sends(i):
                send.start()
            return carry

        lax.fori_loop(0, ROWS // CHUNK, chunk, 0)
        for i in range(ROWS // CHUNK):
            for send in sends(i):
                send.wait()

    @pl.when(jnp.logical_not(is_ocean))
    def _():
        copies = (
            pltpu.make_async_copy(fluxes, flux_out, out_sems.at[0]),
            pltpu.make_async_copy(fluxes.at[0], boundary_out, out_sems.at[1]),
        )
        for copy in copies:
            copy.start()
        for copy in copies:
            copy.wait()


WIDE = pltpu.CompilerParams(vmem_limit_bytes=63 * 2**20 + 2**19)
LIMIT = pltpu.CompilerParams(vmem_limit_bytes=16 * 2**20)
N = ROWS + 8
SHEET = jax.ShapeDtypeStruct((2 * LEVELS * 8, COLS), BF16)
COLUMNS = jax.ShapeDtypeStruct((2 * N, COLS), BF16)


def f32(*shape):
    return jax.ShapeDtypeStruct(shape, F32)


def edge_rows(state, winds):
    return pl.pallas_call(
        edge_rows_kernel,
        in_specs=[HBM, HBM],
        out_specs=[VMEM, VMEM],
        out_shape=[SHEET, SHEET],
        scratch_shapes=[
            *[pltpu.VMEM((LEVELS, 8, COLS), F32)] * 2,
            *[pltpu.VMEM((2, LEVELS, 8, COLS), F32)] * 2,
            *[pltpu.VMEM(SHEET.shape, F32)] * 2,
            pltpu.SemaphoreType.DMA((4,)),
        ],
        compiler_params=WIDE,
        name="edge_rows",
    )(state, winds)


def own_strips(state, winds):
    return pl.pallas_call(
        own_strips_kernel,
        in_specs=[VMEM, VMEM],
        out_specs=VMEM,
        out_shape=f32(3, ROWS, COLS),
        compiler_params=LIMIT,
        name="own_strips",
    )(state, winds)


def edge_columns(masks, from_below, from_above, own):
    return pl.pallas_call(
        edge_columns_kernel,
        in_specs=[VMEM] * 4,
        out_specs=[VMEM] * 4,
        out_shape=[f32(3, LEVELS * 8, COLS), f32(3, N, COLS), COLUMNS, COLUMNS],
        scratch_shapes=[
            pltpu.VMEM(SHEET.shape, F32),
            pltpu.VMEM(SHEET.shape, F32),
            pltpu.VMEM((3, N, COLS), F32),
            pltpu.VMEM((2 * N, COLS), F32),
            pltpu.VMEM((2 * N, COLS), F32),
        ],
        compiler_params=LIMIT,
        name="edge_columns",
    )(masks, from_below, from_above, own)


def substeps(rates, weights, masks, state, winds, halo, strip0, from_left, from_right):
    return pl.pallas_call(
        substeps_kernel,
        in_specs=[VMEM] * 9,
        out_specs=[ANY] + [VMEM] * 3,
        out_shape=[
            f32(LEVELS, ROWS, COLS),
            f32(FIELDS, ROWS, COLS),
            jax.ShapeDtypeStruct((FIELDS * ROWS, COLS), BF16),
            f32(ROWS, COLS),
        ],
        scratch_shapes=[
            *[pltpu.VMEM((LEVELS, DEEP, COLS), F32)] * 4,
            pltpu.VMEM((LEVELS, ROWS, COLS), F32),
            [pltpu.VMEM((DEEP, COLS), F32)] * 3,
            [pltpu.VMEM((DEEP, COLS), F32)] * 3,
            [pltpu.VMEM((DEEP, COLS), F32)] * 4,
            *[pltpu.VMEM((2, N, COLS), F32)] * 2,
            *[pltpu.VMEM((2 * N, COLS), F32)] * 2,
            pltpu.SemaphoreType.DMA((1,)),
        ],
        compiler_params=LIMIT,
        name="substeps",
    )(rates, weights, masks, state, winds, halo, strip0, from_left, from_right)


def turn_blocks(blocks):
    return pl.pallas_call(
        turn_blocks_kernel,
        in_specs=[VMEM],
        out_specs=VMEM,
        out_shape=jax.ShapeDtypeStruct(blocks.shape, BF16),
        compiler_params=LIMIT,
        name="turn_blocks",
    )(blocks)


def remap(table, heat, gathered, weights, fluxes, top):
    chunks = ROWS // CHUNK
    return pl.pallas_call(
        remap_kernel,
        in_specs=[ANY] + [VMEM] * 5,
        out_specs=[ANY] * 2,
        out_shape=[f32(FIELDS, ROWS, COLS), f32(ROWS, COLS)],
        scratch_shapes=[
            pltpu.SMEM(table.shape, jnp.int32),
            pltpu.VMEM((3 * FIELDS * ROWS, COLS), F32),
            pltpu.VMEM((FIELDS, ROWS, COLS), F32),
            pltpu.VMEM((ROWS, COLS), F32),
            pltpu.SemaphoreType.DMA((1,)),
            pltpu.SemaphoreType.DMA((2,)),
            pltpu.SemaphoreType.DMA((chunks,)),
            pltpu.SemaphoreType.DMA((chunks,)),
        ],
        compiler_params=LIMIT,
        name="remap",
    )(table, heat, gathered, weights, fluxes, top)


def body(
    state, winds, diffusivity, coupling, heat_coef, remap_blocks, source_patch, block_ids, land_sea
):
    group = lax.axis_index("grp")
    row_tile = lax.axis_index("gx")
    column_tile = lax.axis_index("gy")
    tiles_x = lax.axis_size("gx")
    tiles_y = lax.axis_size("gy")
    groups = lax.axis_size("grp")
    ocean = group == groups - 1
    line = group * tiles_x + row_tile
    top = (line == 0) | (ocean & (row_tile == 0))
    bottom = (row_tile == tiles_x - 1) & (group >= groups - 2)
    row = lax.broadcasted_iota(jnp.int32, (8, COLS), 0)
    lane = lax.broadcasted_iota(jnp.int32, (8, COLS), 1)
    row_one = jnp.where(row < 4, ~bottom, ~top).astype(F32)
    side_one = jnp.where((lane & 7) < 4, column_tile > 0, column_tile < tiles_y - 1).astype(F32)
    own_rate = jnp.where(ocean, diffusivity[1], diffusivity[0])
    rate = jnp.broadcast_to(own_rate[:, None], (LEVELS, 8)).reshape(1, COLS) * jnp.ones((8, 1), F32)
    masks = jnp.stack([row_one, side_one, rate])
    rates = jnp.broadcast_to(own_rate[:, None], (LEVELS, COLS))
    weights = jnp.broadcast_to(coupling.reshape(-1, 1), (FIELDS * LEVELS, COLS))
    source = source_patch[0, 0].T
    starts = (source // ROWS) * (FIELDS * ROWS) + source % ROWS
    table = jnp.concatenate([
        land_sea.reshape(-1),
        jnp.concatenate([starts, block_ids[0, 0].T], 1).reshape(-1),
        ocean.astype(jnp.int32)[None],
    ])
    heat = jnp.broadcast_to(heat_coef[:, None], (FIELDS, COLS))

    def ring(x, axis, shift):
        count = lax.axis_size(axis)
        return lax.ppermute(x, axis, [(i, (i + shift) % count) for i in range(count)])

    to_up, to_down = edge_rows(state, winds)
    from_below = ring(to_up, ("grp", "gx"), -1)
    from_above = ring(to_down, ("grp", "gx"), 1)
    own = own_strips(state, winds)
    halo, strip0, to_right, to_left = edge_columns(masks, from_below, from_above, own)
    from_left = ring(to_right, "gy", 1)
    from_right = ring(to_left, "gy", -1)
    turned = turn_blocks(remap_blocks)
    state_out, fluxes, rounded, top_level = substeps(
        rates, weights, masks, state, winds, halo, strip0, from_left, from_right
    )
    gathered = lax.all_gather(rounded, "grp", axis=0, tiled=True)
    fluxes, boundary = remap(
        table, heat, gathered, turned, fluxes, top_level
    )
    return state_out, boundary, fluxes


def solution(mesh):
    return jax.shard_map(
        body,
        mesh=mesh,
        in_specs=(
            P(None, ("grp", "gx"), "gy"),
            P(None, None, ("grp", "gx"), "gy"),
            P(),
            P(),
            P(),
            P(),
            P("gx", "gy", None, None),
            P("gx", "gy", None, None),
            P("gx", "gy", None),
        ),
        out_specs=(
            P(None, ("grp", "gx"), "gy"),
            P(("grp", "gx"), "gy"),
            P(None, ("grp", "gx"), "gy"),
        ),
        check_vma=False,
    )
```

```python
import jax
import jax.numpy as jnp
from jax import lax
from jax.experimental import pallas as pl
from jax.experimental.pallas import tpu as pltpu
from jax.sharding import PartitionSpec as P

FIELDS = 8
LEVELS = 16
SUBSTEPS = 4
INTERSECTIONS = 6
ROWS = 64
COLS = 128
TILES = ROWS // 8
BASE = 16
DEEP = ROWS + 32
UNROLL = 4
BLOCK = 8
FLUX_ROWS = 32
CHUNK = 32
F32 = jnp.float32
BF16 = jnp.bfloat16

VMEM = pl.BlockSpec(memory_space=pltpu.VMEM)
SMEM = pl.BlockSpec(memory_space=pltpu.SMEM)
ANY = pl.BlockSpec(memory_space=pl.ANY)
HBM = pl.BlockSpec(memory_space=pltpu.HBM)


def sub_ids():
    return lax.broadcasted_iota(jnp.int32, (8, COLS), 0)


def lane_ids():
    return lax.broadcasted_iota(jnp.int32, (8, COLS), 1)


def edge_rows_kernel(state, winds, to_up, to_down, st_top, st_low, wi_top, wi_low,
                     sheet_up, sheet_down, sems):
    first, last = slice(0, 8), slice(ROWS - 8, ROWS)
    fetches = [
        pltpu.make_async_copy(source, target, sems.at[i])
        for i, (source, target) in enumerate((
            (winds.at[:, :, first], wi_top),
            (winds.at[:, :, last], wi_low),
            (state.at[:, first], st_top),
            (state.at[:, last], st_low),
        ))
    ]
    for fetch in fetches:
        fetch.start()
    for fetch in fetches:
        fetch.wait()
    upper = sub_ids() < 4
    for l in range(LEVELS):
        top, low = st_top[l], st_low[l]
        top_hi, low_hi = top.astype(BF16).astype(F32), low.astype(BF16).astype(F32)
        sheet_up[8 * l : 8 * l + 8] = jnp.where(upper, top_hi, pltpu.roll(top - top_hi, 4, 0))
        sheet_down[8 * l : 8 * l + 8] = jnp.where(upper, pltpu.roll(low_hi, 4, 0), low - low_hi)
        k = LEVELS + l
        sheet_up[8 * k : 8 * k + 8] = jnp.where(upper, wi_top[0, l], pltpu.roll(wi_top[1, l], 4, 0))
        sheet_down[8 * k : 8 * k + 8] = jnp.where(upper, pltpu.roll(wi_low[0, l], 4, 0), wi_low[1, l])
    to_up[...] = sheet_up[...].astype(BF16)
    to_down[...] = sheet_down[...].astype(BF16)


def packed(strip, tile, l):
    turned = pltpu.roll(tile, 8 * l + 4, 1)
    return jnp.where((lane_ids() >> 3) == l, turned, strip)


def own_strips_kernel(state, winds, strips):
    def row_tile(t, carry):
        r = pl.multiple_of(t * 8, 8)
        sources = (state, winds.at[0], winds.at[1])
        for c in range(3):
            strip = jnp.zeros((8, COLS), F32)
            for l in range(LEVELS):
                strip = packed(strip, sources[c][l, pl.ds(r, 8), :], l)
            strips[c, pl.ds(r, 8), :] = strip
        return carry

    lax.fori_loop(0, TILES, row_tile, 0)


def edge_columns_kernel(masks, from_below, from_above, own, halo, strip0, to_right, to_left,
                        below, above, full, right_sheet, left_sheet):
    below[...] = from_below[...].astype(F32)
    above[...] = from_above[...].astype(F32)
    upper = sub_ids() < 4
    ok = masks[0]
    full[:, 0:ROWS, :] = own[...]
    parts = [jnp.zeros((8, COLS), F32)] * 3
    for l in range(LEVELS):
        b, a = below[8 * l : 8 * l + 8], above[8 * l : 8 * l + 8]
        s = jnp.where(upper, b + pltpu.roll(b, 4, 0), a + pltpu.roll(a, 4, 0))
        k = LEVELS + l
        b, a = below[8 * k : 8 * k + 8], above[8 * k : 8 * k + 8]
        u = jnp.where(upper, b, pltpu.roll(a, 4, 0))
        v = jnp.where(upper, pltpu.roll(b, 4, 0), a)
        for c, x in enumerate((s, u, v)):
            x = x * ok
            halo[c, 8 * l : 8 * l + 8] = x
            parts[c] = packed(parts[c], x, l)
    for c in range(3):
        full[c, ROWS : ROWS + 8] = parts[c]
    strip0[...] = full[...]
    first = (lane_ids() & 7) < 4
    n = ROWS + 8
    for t in range(TILES + 1):
        r = 8 * t
        s, u, v = full[0, r : r + 8], full[1, r : r + 8], full[2, r : r + 8]
        hi = s.astype(BF16).astype(F32)
        lo = s - hi
        right_sheet[r : r + 8] = jnp.where(first, hi, pltpu.roll(lo, 4, 1))
        left_sheet[r : r + 8] = jnp.where(first, pltpu.roll(lo, COLS - 4, 1), hi)
        right_sheet[n + r : n + r + 8] = jnp.where(first, u, pltpu.roll(v, 4, 1))
        left_sheet[n + r : n + r + 8] = jnp.where(first, pltpu.roll(v, COLS - 4, 1), u)
    to_right[...] = right_sheet[...].astype(BF16)
    to_left[...] = left_sheet[...].astype(BF16)


def stencil(s, n, so, w, e, u, v, d, c):
    drift = u * (e - w) + v * (so - n)
    return c * s + d * ((n + so) + (w + e)) - 0.5 * drift


def first_step_kernel(rates, masks, state, winds, halo, partial, cells):
    own = slice(BASE, BASE + ROWS)
    high, low = slice(BASE - 8, BASE), slice(BASE + ROWS, BASE + ROWS + 8)
    upper = sub_ids() < 4
    lane = lane_ids()
    row_one = masks[0]

    def copy_level(l, carry):
        h = pl.multiple_of(8 * l, 8)
        cells[l, own] = state[l]
        x = halo[0, pl.ds(h, 8), :]
        cells[l, high] = x
        cells[l, low] = x
        return carry

    lax.fori_loop(0, LEVELS, copy_level, 0, unroll=2)

    def level(l, carry):
        h = pl.multiple_of(8 * l, 8)
        d = rates[pl.ds(l, 1), :]
        for t in range(TILES + 1):
            k = slice(8 * t, 8 * t + 8)
            r = BASE + 8 * t
            if t < TILES:
                s, no, so = cells[l, r : r + 8, :], cells[l, r - 1 : r + 7, :], cells[l, r + 1 : r + 9, :]
                u, v = winds[0, l, k, :], winds[1, l, k, :]
            else:
                s, no, so = halo_rows(lambda r: cells[l, r : r + 8, :], upper)
                u, v = halo[1, pl.ds(h, 8), :], halo[2, pl.ds(h, 8), :]
                d = d * row_one
            w = jnp.where(lane == 0, 0.0, pltpu.roll(s, 1, 1))
            e = jnp.where(lane == COLS - 1, 0.0, pltpu.roll(s, COLS - 1, 1))
            partial[l, k, :] = stencil(s, no, so, w, e, u, v, d, 1.0 - 4.0 * d)
        return carry

    lax.fori_loop(0, LEVELS, level, 0, unroll=4)


def halo_rows(load, upper):
    d, u = BASE + ROWS, BASE - 8
    return (
        load(d),
        jnp.where(upper, load(d - 1), load(u - 1)),
        jnp.where(upper, load(d + 1), load(u + 1)),
    )


def substeps_kernel(rates, weights, masks, partial, winds, halo, strip0, from_left, from_right,
                    state_out, fluxes, rounded, top,
                    cells1, cells2, cells3, ready,
                    lefts, rights, sides, left_winds, right_winds, left, right, sems):
    cells = (None, cells1, cells2, cells3)
    upper = sub_ids() < 4
    n = ROWS + 8
    own = slice(BASE, BASE + ROWS)
    high, low = slice(BASE - 8, BASE), slice(BASE + ROWS, BASE + ROWS + 8)
    lane = lane_ids()
    place = lane & 7
    first = place < 4
    row_one, side_one, rate = masks[0], masks[1], masks[2]

    def put(buf, t, x):
        if t < TILES:
            buf[BASE + 8 * t : BASE + 8 * t + 8] = x
        else:
            buf[high] = x
            buf[low] = x

    left[...] = from_left[...].astype(F32)
    right[...] = from_right[...].astype(F32)
    for t in range(TILES + 1):
        r, q = slice(8 * t, 8 * t + 8), slice(n + 8 * t, n + 8 * t + 8)
        a, b = left[r], right[r]
        a = (a + pltpu.roll(a, COLS - 4, 1)) * side_one
        b = (b + pltpu.roll(b, 4, 1)) * side_one
        put(lefts[0], t, jnp.where(first, a, strip0[0, r]))
        put(rights[0], t, jnp.where(first, strip0[0, r], b))
        put(sides[0], t, jnp.where(place == 4, pltpu.roll(a, 1, 1), pltpu.roll(b, COLS - 1, 1)))
        a, b = left[q], right[q]
        left_winds[0, r] = jnp.where(first, a * side_one, strip0[1, r])
        right_winds[0, r] = jnp.where(first, strip0[1, r], b * side_one)
        a, b = pltpu.roll(a, COLS - 4, 1), pltpu.roll(b, 4, 1)
        left_winds[1, r] = jnp.where(first, a * side_one, strip0[2, r])
        right_winds[1, r] = jnp.where(first, strip0[2, r], b * side_one)
    left_rate = jnp.where(first, rate * side_one, rate)
    right_rate = jnp.where(first, rate, rate * side_one)
    for step in range(SUBSTEPS - 1):
        for t in range(TILES + 1):
            r, k = BASE + 8 * t, slice(8 * t, 8 * t + 8)
            new = []
            for strip, wind, d in ((lefts[step], left_winds, left_rate), (rights[step], right_winds, right_rate)):
                if t < TILES:
                    s, no, so = strip[r : r + 8], strip[r - 1 : r + 7], strip[r + 1 : r + 9]
                else:
                    s, no, so = halo_rows(lambda r: strip[r : r + 8], upper)
                    d = d * row_one
                w, e = pltpu.roll(s, 1, 1), pltpu.roll(s, COLS - 1, 1)
                new.append(stencil(s, no, so, w, e, wind[0, k], wind[1, k], d, 1.0 - 4.0 * d))
            if step < SUBSTEPS - 2:
                put(lefts[step + 1], t, new[0])
                put(rights[step + 1], t, new[1])
            put(sides[step + 1], t, jnp.where(first, new[0], new[1]))

    def beside(s, side, last, first):
        return (
            pltpu.roll(jnp.where(last, side, s), 1, 1),
            pltpu.roll(jnp.where(first, side, s), COLS - 1, 1),
        )

    wide = lax.broadcasted_iota(jnp.int32, (BLOCK, COLS), 1)
    last_wide, first_wide = wide == COLS - 1, wide == 0
    last_lane, first_lane = lane == COLS - 1, lane == 0
    edge_one = jnp.where(last_lane | first_lane, 1.0, 0.0)
    edge_half = jnp.where(first_lane, 0.5, jnp.where(last_lane, -0.5, 0.0))

    for step in range(SUBSTEPS):
        last = step == SUBSTEPS - 1
        src, strip = cells[step], sides[step]

        def beyond(l, carry):
            h = pl.multiple_of(8 * l, 8)
            d = rates[pl.ds(l, 1), :] * edge_one
            turn = COLS - 4 - 8 * l
            for t in range(TILES + 1):
                k = slice(8 * t, 8 * t + 8)
                r = BASE + 8 * t
                side = pltpu.roll(strip[r : r + 8], turn, 1)
                if t < TILES:
                    cells1[l, r : r + 8, :] = partial[l, k, :] + side * (d + edge_half * winds[0, l, k, :])
                else:
                    y = partial[l, k, :] + side * (d * row_one + edge_half * halo[1, pl.ds(h, 8), :])
                    cells1[l, high, :] = y
                    cells1[l, low, :] = y
            return carry

        def level(l, carry):
            h = pl.multiple_of(8 * l, 8)
            d = rates[pl.ds(l, 1), :]
            c = 1.0 - 4.0 * d
            turn = COLS - 4 - 8 * l
            for t in range(ROWS // BLOCK):
                k = slice(BLOCK * t, BLOCK * (t + 1))
                r = BASE + BLOCK * t
                s = src[l, r : r + BLOCK, :]
                w, e = beside(s, pltpu.roll(strip[r : r + BLOCK], turn, 1), last_wide, first_wide)
                x = stencil(s, src[l, r - 1 : r + BLOCK - 1, :], src[l, r + 1 : r + BLOCK + 1, :],
                            w, e, winds[0, l, k, :], winds[1, l, k, :], d, c)
                if last:
                    ready[l, k, :] = x
                else:
                    cells[step + 1][l, r : r + BLOCK, :] = x
            if last:
                return carry
            s, no, so = halo_rows(lambda r: src[l, r : r + 8, :], upper)
            w, e = beside(s, pltpu.roll(strip[low], turn, 1), last_lane, first_lane)
            d = d * row_one
            y = stencil(s, no, so, w, e, halo[1, pl.ds(h, 8), :], halo[2, pl.ds(h, 8), :], d, 1.0 - 4.0 * d)
            cells[step + 1][l, high, :] = y
            cells[step + 1][l, low, :] = y
            return carry

        lax.fori_loop(0, LEVELS, level if step else beyond, 0, unroll=UNROLL)

    send = pltpu.make_async_copy(ready, state_out, sems.at[0])
    send.start()

    def flux(t, carry):
        r = pl.multiple_of(FLUX_ROWS * t, FLUX_ROWS)
        at = pl.ds(BASE + r, FLUX_ROWS)
        out = pl.ds(r, FLUX_ROWS)
        sums = [None] * FIELDS
        for l in range(LEVELS):
            x = (cells1[l, at, :] + cells2[l, at, :]) + (cells3[l, at, :] + ready[l, out, :])
            for f in range(FIELDS):
                k = f * LEVELS + l
                term = weights[k : k + 1, :] * x
                sums[f] = term if l == 0 else sums[f] + term
        for f in range(FIELDS):
            mean = sums[f] * (1.0 / SUBSTEPS)
            fluxes[f, out, :] = mean
            rounded[pl.ds(pl.multiple_of(f * ROWS + r, FLUX_ROWS), FLUX_ROWS), :] = mean.astype(BF16)
        return carry

    lax.fori_loop(0, ROWS // FLUX_ROWS, flux, 0)
    top[...] = ready[0]
    send.wait()


def turn_blocks_kernel(blocks, turned):
    def turn(i, carry):
        turned[i] = blocks[i].T
        return carry

    lax.fori_loop(0, blocks.shape[0], turn, 0, unroll=8)


def remap_kernel(words, heat, gathered, weights, fluxes, top, flux_out, boundary_out,
                 table, patches, remapped, surface, table_sem, out_sems, flux_sems, surface_sems):
    size = FIELDS * ROWS
    fetch = pltpu.make_async_copy(words, table, table_sem.at[0])
    fetch.start()
    patches[...] = gathered[0 : 3 * size].astype(F32)
    fetch.wait()
    is_ocean = table[table.shape[0] - 1] == 1

    @pl.when(is_ocean)
    def _():
        def sends(i):
            at = pl.ds(pl.multiple_of(i * CHUNK, CHUNK), CHUNK)
            return (
                pltpu.make_async_copy(remapped.at[:, at], flux_out.at[:, at], flux_sems.at[i]),
                pltpu.make_async_copy(surface.at[at], boundary_out.at[at], surface_sems.at[i]),
            )

        def chunk(i, carry):
            at = pl.ds(pl.multiple_of(i * CHUNK, CHUNK), CHUNK)
            for j in range(CHUNK):
                o = i * CHUNK + j
                picked, chosen = [], []
                for entry in range(INTERSECTIONS):
                    at_entry = ROWS + 2 * ROWS * entry + o
                    start = table[at_entry]
                    picked.append(patches[pl.ds(start, FIELDS, stride=ROWS), :].astype(BF16))
                    chosen.append(weights[table[at_entry + ROWS]])
                total = jnp.dot(
                    jnp.concatenate(picked, 1), jnp.concatenate(chosen, 0), preferred_element_type=F32
                )
                remapped[:, o, :] = total * table[o].astype(F32)
            warmth = top[at, :]
            for f in range(FIELDS):
                warmth = warmth + heat[f : f + 1] * remapped[f, at, :]
            surface[at, :] = warmth
            for send in sends(i):
                send.start()
            return carry

        lax.fori_loop(0, ROWS // CHUNK, chunk, 0)
        for i in range(ROWS // CHUNK):
            for send in sends(i):
                send.wait()

    @pl.when(jnp.logical_not(is_ocean))
    def _():
        copies = (
            pltpu.make_async_copy(fluxes, flux_out, out_sems.at[0]),
            pltpu.make_async_copy(fluxes.at[0], boundary_out, out_sems.at[1]),
        )
        for copy in copies:
            copy.start()
        for copy in copies:
            copy.wait()


WIDE = pltpu.CompilerParams(vmem_limit_bytes=53 * 2**20 + 5 * 2**17)
LIMIT = pltpu.CompilerParams(vmem_limit_bytes=16 * 2**20)
N = ROWS + 8
SHEET = jax.ShapeDtypeStruct((2 * LEVELS * 8, COLS), BF16)
COLUMNS = jax.ShapeDtypeStruct((2 * N, COLS), BF16)


def cost(microseconds):
    return pl.CostEstimate(
        flops=int(1e9 * microseconds), bytes_accessed=int(3.6e6 * microseconds), transcendentals=0
    )


def f32(*shape):
    return jax.ShapeDtypeStruct(shape, F32)


def edge_rows(state, winds):
    return pl.pallas_call(
        edge_rows_kernel,
        in_specs=[HBM, HBM],
        out_specs=[VMEM, VMEM],
        out_shape=[SHEET, SHEET],
        scratch_shapes=[
            *[pltpu.VMEM((LEVELS, 8, COLS), F32)] * 2,
            *[pltpu.VMEM((2, LEVELS, 8, COLS), F32)] * 2,
            *[pltpu.VMEM(SHEET.shape, F32)] * 2,
            pltpu.SemaphoreType.DMA((4,)),
        ],
        compiler_params=WIDE,
        cost_estimate=cost(1.1),
        name="edge_rows",
    )(state, winds)


def own_strips(state, winds):
    return pl.pallas_call(
        own_strips_kernel,
        in_specs=[VMEM, VMEM],
        out_specs=VMEM,
        out_shape=f32(3, ROWS, COLS),
        compiler_params=LIMIT,
        cost_estimate=cost(1.0),
        name="own_strips",
    )(state, winds)


def edge_columns(masks, from_below, from_above, own):
    return pl.pallas_call(
        edge_columns_kernel,
        in_specs=[VMEM] * 4,
        out_specs=[VMEM] * 4,
        out_shape=[f32(3, LEVELS * 8, COLS), f32(3, N, COLS), COLUMNS, COLUMNS],
        scratch_shapes=[
            pltpu.VMEM(SHEET.shape, F32),
            pltpu.VMEM(SHEET.shape, F32),
            pltpu.VMEM((3, N, COLS), F32),
            pltpu.VMEM((2 * N, COLS), F32),
            pltpu.VMEM((2 * N, COLS), F32),
        ],
        compiler_params=LIMIT,
        cost_estimate=cost(0.2),
        name="edge_columns",
    )(masks, from_below, from_above, own)


def first_step(rates, masks, state, winds, halo):
    return pl.pallas_call(
        first_step_kernel,
        in_specs=[VMEM] * 5,
        out_specs=VMEM,
        out_shape=f32(LEVELS, N, COLS),
        scratch_shapes=[pltpu.VMEM((LEVELS, DEEP, COLS), F32)],
        compiler_params=LIMIT,
        cost_estimate=cost(1.0),
        name="first_step",
    )(rates, masks, state, winds, halo)


def substeps(rates, weights, masks, partial, winds, halo, strip0, from_left, from_right):
    return pl.pallas_call(
        substeps_kernel,
        in_specs=[VMEM] * 9,
        out_specs=[ANY] + [VMEM] * 3,
        out_shape=[
            f32(LEVELS, ROWS, COLS),
            f32(FIELDS, ROWS, COLS),
            jax.ShapeDtypeStruct((FIELDS * ROWS, COLS), BF16),
            f32(ROWS, COLS),
        ],
        scratch_shapes=[
            *[pltpu.VMEM((LEVELS, DEEP, COLS), F32)] * 3,
            pltpu.VMEM((LEVELS, ROWS, COLS), F32),
            [pltpu.VMEM((DEEP, COLS), F32)] * 3,
            [pltpu.VMEM((DEEP, COLS), F32)] * 3,
            [pltpu.VMEM((DEEP, COLS), F32)] * 4,
            *[pltpu.VMEM((2, N, COLS), F32)] * 2,
            *[pltpu.VMEM((2 * N, COLS), F32)] * 2,
            pltpu.SemaphoreType.DMA((1,)),
        ],
        compiler_params=LIMIT,
        name="substeps",
    )(rates, weights, masks, partial, winds, halo, strip0, from_left, from_right)


def turn_blocks(blocks):
    return pl.pallas_call(
        turn_blocks_kernel,
        in_specs=[VMEM],
        out_specs=VMEM,
        out_shape=jax.ShapeDtypeStruct(blocks.shape, BF16),
        compiler_params=LIMIT,
        cost_estimate=cost(1.0),
        name="turn_blocks",
    )(blocks)


def remap(table, heat, gathered, weights, fluxes, top):
    chunks = ROWS // CHUNK
    return pl.pallas_call(
        remap_kernel,
        in_specs=[ANY] + [VMEM] * 5,
        out_specs=[ANY] * 2,
        out_shape=[f32(FIELDS, ROWS, COLS), f32(ROWS, COLS)],
        scratch_shapes=[
            pltpu.SMEM(table.shape, jnp.int32),
            pltpu.VMEM((3 * FIELDS * ROWS, COLS), F32),
            pltpu.VMEM((FIELDS, ROWS, COLS), F32),
            pltpu.VMEM((ROWS, COLS), F32),
            pltpu.SemaphoreType.DMA((1,)),
            pltpu.SemaphoreType.DMA((2,)),
            pltpu.SemaphoreType.DMA((chunks,)),
            pltpu.SemaphoreType.DMA((chunks,)),
        ],
        compiler_params=LIMIT,
        name="remap",
    )(table, heat, gathered, weights, fluxes, top)


def body(
    state, winds, diffusivity, coupling, heat_coef, remap_blocks, source_patch, block_ids, land_sea
):
    group = lax.axis_index("grp")
    row_tile = lax.axis_index("gx")
    column_tile = lax.axis_index("gy")
    tiles_x = lax.axis_size("gx")
    tiles_y = lax.axis_size("gy")
    groups = lax.axis_size("grp")
    ocean = group == groups - 1
    line = group * tiles_x + row_tile
    top = (line == 0) | (ocean & (row_tile == 0))
    bottom = (row_tile == tiles_x - 1) & (group >= groups - 2)
    row = lax.broadcasted_iota(jnp.int32, (8, COLS), 0)
    lane = lax.broadcasted_iota(jnp.int32, (8, COLS), 1)
    row_one = jnp.where(row < 4, ~bottom, ~top).astype(F32)
    side_one = jnp.where((lane & 7) < 4, column_tile > 0, column_tile < tiles_y - 1).astype(F32)
    own_rate = jnp.where(ocean, diffusivity[1], diffusivity[0])
    rate = jnp.broadcast_to(own_rate[:, None], (LEVELS, 8)).reshape(1, COLS) * jnp.ones((8, 1), F32)
    masks = jnp.stack([row_one, side_one, rate])
    rates = jnp.broadcast_to(own_rate[:, None], (LEVELS, COLS))
    weights = jnp.broadcast_to(coupling.reshape(-1, 1), (FIELDS * LEVELS, COLS))
    source = source_patch[0, 0].T
    starts = (source // ROWS) * (FIELDS * ROWS) + source % ROWS
    table = jnp.concatenate([
        land_sea.reshape(-1),
        jnp.concatenate([starts, block_ids[0, 0].T], 1).reshape(-1),
        ocean.astype(jnp.int32)[None],
    ])
    heat = jnp.broadcast_to(heat_coef[:, None], (FIELDS, COLS))

    def ring(x, axis, shift):
        count = lax.axis_size(axis)
        return lax.ppermute(x, axis, [(i, (i + shift) % count) for i in range(count)])

    to_up, to_down = edge_rows(state, winds)
    from_below = ring(to_up, ("grp", "gx"), -1)
    from_above = ring(to_down, ("grp", "gx"), 1)
    own = own_strips(state, winds)
    halo, strip0, to_right, to_left = edge_columns(masks, from_below, from_above, own)
    from_left = ring(to_right, "gy", 1)
    from_right = ring(to_left, "gy", -1)
    partial = first_step(rates, masks, state, winds, halo)
    turned = turn_blocks(remap_blocks)
    state_out, fluxes, rounded, top_level = substeps(
        rates, weights, masks, partial, winds, halo, strip0, from_left, from_right
    )
    gathered = lax.all_gather(rounded, "grp", axis=0, tiled=True)
    fluxes, boundary = remap(
        table, heat, gathered, turned, fluxes, top_level
    )
    return state_out, boundary, fluxes


def solution(mesh):
    return jax.shard_map(
        body,
        mesh=mesh,
        in_specs=(
            P(None, ("grp", "gx"), "gy"),
            P(None, None, ("grp", "gx"), "gy"),
            P(),
            P(),
            P(),
            P(),
            P("gx", "gy", None, None),
            P("gx", "gy", None, None),
            P("gx", "gy", None),
        ),
        out_specs=(
            P(None, ("grp", "gx"), "gy"),
            P(("grp", "gx"), "gy"),
            P(None, ("grp", "gx"), "gy"),
        ),
        check_vma=False,
    )
```

```python
import jax
import jax.numpy as jnp
from jax import lax
from jax.experimental import pallas as pl
from jax.experimental.pallas import tpu as pltpu
from jax.sharding import PartitionSpec as P

FIELDS = 8
LEVELS = 16
SUBSTEPS = 4
INTERSECTIONS = 6
ROWS = 64
COLS = 128
TILES = ROWS // 8
BASE = 16
DEEP = ROWS + 32
UNROLL = 4
FLUX_ROWS = 32
CHUNK = 32
F32 = jnp.float32
BF16 = jnp.bfloat16

VMEM = pl.BlockSpec(memory_space=pltpu.VMEM)
SMEM = pl.BlockSpec(memory_space=pltpu.SMEM)
ANY = pl.BlockSpec(memory_space=pl.ANY)
HBM = pl.BlockSpec(memory_space=pltpu.HBM)


def sub_ids():
    return lax.broadcasted_iota(jnp.int32, (8, COLS), 0)


def lane_ids():
    return lax.broadcasted_iota(jnp.int32, (8, COLS), 1)


def edge_rows_kernel(state, winds, to_up, to_down, st_top, st_low, wi_top, wi_low,
                     sheet_up, sheet_down, sems):
    first, last = slice(0, 8), slice(ROWS - 8, ROWS)
    fetches = [
        pltpu.make_async_copy(source, target, sems.at[i])
        for i, (source, target) in enumerate((
            (winds.at[:, :, first], wi_top),
            (winds.at[:, :, last], wi_low),
            (state.at[:, first], st_top),
            (state.at[:, last], st_low),
        ))
    ]
    for fetch in fetches:
        fetch.start()
    for fetch in fetches:
        fetch.wait()
    upper = sub_ids() < 4
    for l in range(LEVELS):
        top, low = st_top[l], st_low[l]
        top_hi, low_hi = top.astype(BF16).astype(F32), low.astype(BF16).astype(F32)
        sheet_up[8 * l : 8 * l + 8] = jnp.where(upper, top_hi, pltpu.roll(top - top_hi, 4, 0))
        sheet_down[8 * l : 8 * l + 8] = jnp.where(upper, pltpu.roll(low_hi, 4, 0), low - low_hi)
        k = LEVELS + l
        sheet_up[8 * k : 8 * k + 8] = jnp.where(upper, wi_top[0, l], pltpu.roll(wi_top[1, l], 4, 0))
        sheet_down[8 * k : 8 * k + 8] = jnp.where(upper, pltpu.roll(wi_low[0, l], 4, 0), wi_low[1, l])
    to_up[...] = sheet_up[...].astype(BF16)
    to_down[...] = sheet_down[...].astype(BF16)


def packed(strip, tile, l):
    turned = pltpu.roll(tile, 8 * l + 4, 1)
    return jnp.where((lane_ids() >> 3) == l, turned, strip)


def own_strips_kernel(state, winds, strips):
    def row_tile(t, carry):
        r = pl.multiple_of(t * 8, 8)
        sources = (state, winds.at[0], winds.at[1])
        for c in range(3):
            strip = jnp.zeros((8, COLS), F32)
            for l in range(LEVELS):
                strip = packed(strip, sources[c][l, pl.ds(r, 8), :], l)
            strips[c, pl.ds(r, 8), :] = strip
        return carry

    lax.fori_loop(0, TILES, row_tile, 0)


def edge_columns_kernel(masks, from_below, from_above, own, halo, strip0, to_right, to_left,
                        below, above, full, right_sheet, left_sheet):
    below[...] = from_below[...].astype(F32)
    above[...] = from_above[...].astype(F32)
    upper = sub_ids() < 4
    ok = masks[0]
    full[:, 0:ROWS, :] = own[...]
    parts = [jnp.zeros((8, COLS), F32)] * 3
    for l in range(LEVELS):
        b, a = below[8 * l : 8 * l + 8], above[8 * l : 8 * l + 8]
        s = jnp.where(upper, b + pltpu.roll(b, 4, 0), a + pltpu.roll(a, 4, 0))
        k = LEVELS + l
        b, a = below[8 * k : 8 * k + 8], above[8 * k : 8 * k + 8]
        u = jnp.where(upper, b, pltpu.roll(a, 4, 0))
        v = jnp.where(upper, pltpu.roll(b, 4, 0), a)
        for c, x in enumerate((s, u, v)):
            x = x * ok
            halo[c, 8 * l : 8 * l + 8] = x
            parts[c] = packed(parts[c], x, l)
    for c in range(3):
        full[c, ROWS : ROWS + 8] = parts[c]
    strip0[...] = full[...]
    first = (lane_ids() & 7) < 4
    n = ROWS + 8
    for t in range(TILES + 1):
        r = 8 * t
        s, u, v = full[0, r : r + 8], full[1, r : r + 8], full[2, r : r + 8]
        hi = s.astype(BF16).astype(F32)
        lo = s - hi
        right_sheet[r : r + 8] = jnp.where(first, hi, pltpu.roll(lo, 4, 1))
        left_sheet[r : r + 8] = jnp.where(first, pltpu.roll(lo, COLS - 4, 1), hi)
        right_sheet[n + r : n + r + 8] = jnp.where(first, u, pltpu.roll(v, 4, 1))
        left_sheet[n + r : n + r + 8] = jnp.where(first, pltpu.roll(v, COLS - 4, 1), u)
    to_right[...] = right_sheet[...].astype(BF16)
    to_left[...] = left_sheet[...].astype(BF16)


def stencil(s, n, so, w, e, u, v, d, c):
    drift = u * (e - w) + v * (so - n)
    return c * s + d * ((n + so) + (w + e)) - 0.5 * drift


def inner_steps_kernel(rates, masks, state, winds, halo, last, total, cells0, cells1, cells2, cells3):
    own = slice(BASE, BASE + ROWS)
    high, low = slice(BASE - 8, BASE), slice(BASE + ROWS, BASE + ROWS + 8)
    upper = sub_ids() < 4
    lane = lane_ids()
    row_one = masks[0]

    def copy_level(l, carry):
        h = pl.multiple_of(8 * l, 8)
        cells0[l, own] = state[l]
        x = halo[0, pl.ds(h, 8), :]
        cells0[l, high] = x
        cells0[l, low] = x
        return carry

    lax.fori_loop(0, LEVELS, copy_level, 0, unroll=2)

    def step(src, dst):
        def level(l, carry):
            h = pl.multiple_of(8 * l, 8)
            d = rates[pl.ds(l, 1), :]
            for t in range(TILES if dst is None else TILES + 1):
                k = slice(8 * t, 8 * t + 8)
                r = BASE + 8 * t
                if t < TILES:
                    s, no, so = src[l, r : r + 8, :], src[l, r - 1 : r + 7, :], src[l, r + 1 : r + 9, :]
                    u, v = winds[0, l, k, :], winds[1, l, k, :]
                else:
                    s, no, so = halo_rows(lambda r: src[l, r : r + 8, :], upper)
                    u, v = halo[1, pl.ds(h, 8), :], halo[2, pl.ds(h, 8), :]
                    d = d * row_one
                w = jnp.where(lane == 0, 0.0, pltpu.roll(s, 1, 1))
                e = jnp.where(lane == COLS - 1, 0.0, pltpu.roll(s, COLS - 1, 1))
                x = stencil(s, no, so, w, e, u, v, d, 1.0 - 4.0 * d)
                if dst is None:
                    last[l, k, :] = x
                    total[l, k, :] = (cells1[l, r : r + 8, :] + cells2[l, r : r + 8, :]) + (s + x)
                elif t < TILES:
                    dst[l, r : r + 8, :] = x
                else:
                    dst[l, high, :] = x
                    dst[l, low, :] = x
            return carry

        lax.fori_loop(0, LEVELS, level, 0, unroll=UNROLL)

    step(cells0, cells1)
    step(cells1, cells2)
    step(cells2, cells3)
    step(cells3, None)


def halo_rows(load, upper):
    d, u = BASE + ROWS, BASE - 8
    return (
        load(d),
        jnp.where(upper, load(d - 1), load(u - 1)),
        jnp.where(upper, load(d + 1), load(u + 1)),
    )


def columns_kernel(weights, masks, inner_last, inner_total, strip0, from_left, from_right,
                   state_out, fluxes, rounded, top,
                   ready, lefts, rights, beyond, extras, left_winds, right_winds, left, right, extra_total, sems):
    upper = sub_ids() < 4
    n = ROWS + 8
    own = slice(BASE, BASE + ROWS)
    high, low = slice(BASE - 8, BASE), slice(BASE + ROWS, BASE + ROWS + 8)
    lane = lane_ids()
    place = lane & 7
    first = place < 4
    row_one, side_one, rate = masks[0], masks[1], masks[2]

    def put(buf, t, x):
        if t < TILES:
            buf[BASE + 8 * t : BASE + 8 * t + 8] = x
        else:
            buf[high] = x
            buf[low] = x

    left[...] = from_left[...].astype(F32)
    right[...] = from_right[...].astype(F32)
    for t in range(TILES + 1):
        r, q = slice(8 * t, 8 * t + 8), slice(n + 8 * t, n + 8 * t + 8)
        a, b = left[r], right[r]
        a = (a + pltpu.roll(a, COLS - 4, 1)) * side_one
        b = (b + pltpu.roll(b, 4, 1)) * side_one
        put(lefts[0], t, jnp.where(first, a, strip0[0, r]))
        put(rights[0], t, jnp.where(first, strip0[0, r], b))
        beyond[0][r] = jnp.where(first, a, b)
        a, b = left[q], right[q]
        left_winds[0, r] = jnp.where(first, a * side_one, strip0[1, r])
        right_winds[0, r] = jnp.where(first, strip0[1, r], b * side_one)
        a, b = pltpu.roll(a, COLS - 4, 1), pltpu.roll(b, 4, 1)
        left_winds[1, r] = jnp.where(first, a * side_one, strip0[2, r])
        right_winds[1, r] = jnp.where(first, strip0[2, r], b * side_one)
    left_rate = jnp.where(first, rate * side_one, rate)
    right_rate = jnp.where(first, rate, rate * side_one)
    for step in range(SUBSTEPS - 1):
        for t in range(TILES + 1):
            r, k = BASE + 8 * t, slice(8 * t, 8 * t + 8)
            new = []
            for strip, wind, d in ((lefts[step], left_winds, left_rate), (rights[step], right_winds, right_rate)):
                if t < TILES:
                    s, no, so = strip[r : r + 8], strip[r - 1 : r + 7], strip[r + 1 : r + 9]
                else:
                    s, no, so = halo_rows(lambda r: strip[r : r + 8], upper)
                    d = d * row_one
                w, e = pltpu.roll(s, 1, 1), pltpu.roll(s, COLS - 1, 1)
                new.append(stencil(s, no, so, w, e, wind[0, k], wind[1, k], d, 1.0 - 4.0 * d))
            if step < SUBSTEPS - 2:
                put(lefts[step + 1], t, new[0])
                put(rights[step + 1], t, new[1])
            beyond[step + 1][k] = jnp.where(first, new[0], new[1])

    for step in range(SUBSTEPS):
        last = step == SUBSTEPS - 1
        for t in range(TILES if last else TILES + 1):
            r, k = BASE + 8 * t, slice(8 * t, 8 * t + 8)
            side = beyond[step][k]
            d = rate if t < TILES else rate * row_one
            if step == 0:
                s = no = so = jnp.zeros((8, COLS), F32)
            elif t < TILES:
                old = extras[step - 1]
                s, no, so = old[r : r + 8], old[r - 1 : r + 7], old[r + 1 : r + 9]
            else:
                s, no, so = halo_rows(lambda r: extras[step - 1][r : r + 8], upper)
            w = pltpu.roll(jnp.where(place == 3, side, jnp.where(place == 7, 0.0, s)), 1, 1)
            e = pltpu.roll(jnp.where(place == 4, side, jnp.where(place == 0, 0.0, s)), COLS - 1, 1)
            x = stencil(s, no, so, w, e, strip0[1, k], strip0[2, k], d, 1.0 - 4.0 * d)
            put(extras[step], t, x)
            if t < TILES:
                extra_total[k] = x if step == 0 else extra_total[k] + x

    def edges(x, l):
        lanes = lax.broadcasted_iota(jnp.int32, x.shape, 1)
        return jnp.where((lanes < 4) | (lanes >= COLS - 4), pltpu.roll(x, COLS - 4 - 8 * l, 1), 0.0)

    for l in range(LEVELS):
        ready[l] = inner_last[l] + edges(extras[SUBSTEPS - 1][own], l)

    send = pltpu.make_async_copy(ready, state_out, sems.at[0])
    send.start()

    def flux(t, carry):
        r = pl.multiple_of(FLUX_ROWS * t, FLUX_ROWS)
        out = pl.ds(r, FLUX_ROWS)
        sums = [None] * FIELDS
        for l in range(LEVELS):
            x = inner_total[l, out, :] + edges(extra_total[out, :], l)
            for f in range(FIELDS):
                k = f * LEVELS + l
                term = weights[k : k + 1, :] * x
                sums[f] = term if l == 0 else sums[f] + term
        for f in range(FIELDS):
            mean = sums[f] * (1.0 / SUBSTEPS)
            fluxes[f, out, :] = mean
            rounded[pl.ds(pl.multiple_of(f * ROWS + r, FLUX_ROWS), FLUX_ROWS), :] = mean.astype(BF16)
        return carry

    lax.fori_loop(0, ROWS // FLUX_ROWS, flux, 0)
    top[...] = ready[0]
    send.wait()


def turn_blocks_kernel(blocks, turned):
    def turn(i, carry):
        turned[i] = blocks[i].T
        return carry

    lax.fori_loop(0, blocks.shape[0], turn, 0, unroll=8)


def remap_kernel(words, heat, gathered, weights, fluxes, top, flux_out, boundary_out,
                 table, patches, remapped, surface, table_sem, out_sems, flux_sems, surface_sems):
    size = FIELDS * ROWS
    fetch = pltpu.make_async_copy(words, table, table_sem.at[0])
    fetch.start()
    patches[...] = gathered[0 : 3 * size].astype(F32)
    fetch.wait()
    is_ocean = table[table.shape[0] - 1] == 1

    @pl.when(is_ocean)
    def _():
        def sends(i):
            at = pl.ds(pl.multiple_of(i * CHUNK, CHUNK), CHUNK)
            return (
                pltpu.make_async_copy(remapped.at[:, at], flux_out.at[:, at], flux_sems.at[i]),
                pltpu.make_async_copy(surface.at[at], boundary_out.at[at], surface_sems.at[i]),
            )

        def chunk(i, carry):
            at = pl.ds(pl.multiple_of(i * CHUNK, CHUNK), CHUNK)
            for j in range(CHUNK):
                o = i * CHUNK + j
                picked, chosen = [], []
                for entry in range(INTERSECTIONS):
                    at_entry = ROWS + 2 * ROWS * entry + o
                    start = table[at_entry]
                    picked.append(patches[pl.ds(start, FIELDS, stride=ROWS), :].astype(BF16))
                    chosen.append(weights[table[at_entry + ROWS]])
                total = jnp.dot(
                    jnp.concatenate(picked, 1), jnp.concatenate(chosen, 0), preferred_element_type=F32
                )
                remapped[:, o, :] = total * table[o].astype(F32)
            warmth = top[at, :]
            for f in range(FIELDS):
                warmth = warmth + heat[f : f + 1] * remapped[f, at, :]
            surface[at, :] = warmth
            for send in sends(i):
                send.start()
            return carry

        lax.fori_loop(0, ROWS // CHUNK, chunk, 0)
        for i in range(ROWS // CHUNK):
            for send in sends(i):
                send.wait()

    @pl.when(jnp.logical_not(is_ocean))
    def _():
        copies = (
            pltpu.make_async_copy(fluxes, flux_out, out_sems.at[0]),
            pltpu.make_async_copy(fluxes.at[0], boundary_out, out_sems.at[1]),
        )
        for copy in copies:
            copy.start()
        for copy in copies:
            copy.wait()


WIDE = pltpu.CompilerParams(vmem_limit_bytes=53 * 2**20 + 5 * 2**17)
LIMIT = pltpu.CompilerParams(vmem_limit_bytes=16 * 2**20)
N = ROWS + 8
SHEET = jax.ShapeDtypeStruct((2 * LEVELS * 8, COLS), BF16)
COLUMNS = jax.ShapeDtypeStruct((2 * N, COLS), BF16)


def cost(microseconds):
    return pl.CostEstimate(
        flops=int(1e9 * microseconds), bytes_accessed=int(3.6e6 * microseconds), transcendentals=0
    )


def f32(*shape):
    return jax.ShapeDtypeStruct(shape, F32)


def edge_rows(state, winds):
    return pl.pallas_call(
        edge_rows_kernel,
        in_specs=[HBM, HBM],
        out_specs=[VMEM, VMEM],
        out_shape=[SHEET, SHEET],
        scratch_shapes=[
            *[pltpu.VMEM((LEVELS, 8, COLS), F32)] * 2,
            *[pltpu.VMEM((2, LEVELS, 8, COLS), F32)] * 2,
            *[pltpu.VMEM(SHEET.shape, F32)] * 2,
            pltpu.SemaphoreType.DMA((4,)),
        ],
        compiler_params=WIDE,
        cost_estimate=cost(1.1),
        name="edge_rows",
    )(state, winds)


def own_strips(state, winds):
    return pl.pallas_call(
        own_strips_kernel,
        in_specs=[VMEM, VMEM],
        out_specs=VMEM,
        out_shape=f32(3, ROWS, COLS),
        compiler_params=LIMIT,
        cost_estimate=cost(1.0),
        name="own_strips",
    )(state, winds)


def edge_columns(masks, from_below, from_above, own):
    return pl.pallas_call(
        edge_columns_kernel,
        in_specs=[VMEM] * 4,
        out_specs=[VMEM] * 4,
        out_shape=[f32(3, LEVELS * 8, COLS), f32(3, N, COLS), COLUMNS, COLUMNS],
        scratch_shapes=[
            pltpu.VMEM(SHEET.shape, F32),
            pltpu.VMEM(SHEET.shape, F32),
            pltpu.VMEM((3, N, COLS), F32),
            pltpu.VMEM((2 * N, COLS), F32),
            pltpu.VMEM((2 * N, COLS), F32),
        ],
        compiler_params=LIMIT,
        cost_estimate=cost(0.2),
        name="edge_columns",
    )(masks, from_below, from_above, own)


def inner_steps(rates, masks, state, winds, halo):
    return pl.pallas_call(
        inner_steps_kernel,
        in_specs=[VMEM] * 5,
        out_specs=[VMEM] * 2,
        out_shape=[f32(LEVELS, ROWS, COLS)] * 2,
        scratch_shapes=[pltpu.VMEM((LEVELS, DEEP, COLS), F32)] * 4,
        compiler_params=LIMIT,
        cost_estimate=cost(2.5),
        name="inner_steps",
    )(rates, masks, state, winds, halo)


def columns(weights, masks, inner_last, inner_total, strip0, from_left, from_right):
    return pl.pallas_call(
        columns_kernel,
        in_specs=[VMEM] * 7,
        out_specs=[ANY] + [VMEM] * 3,
        out_shape=[
            f32(LEVELS, ROWS, COLS),
            f32(FIELDS, ROWS, COLS),
            jax.ShapeDtypeStruct((FIELDS * ROWS, COLS), BF16),
            f32(ROWS, COLS),
        ],
        scratch_shapes=[
            pltpu.VMEM((LEVELS, ROWS, COLS), F32),
            [pltpu.VMEM((DEEP, COLS), F32)] * 3,
            [pltpu.VMEM((DEEP, COLS), F32)] * 3,
            [pltpu.VMEM((N, COLS), F32)] * 4,
            [pltpu.VMEM((DEEP, COLS), F32)] * 4,
            *[pltpu.VMEM((2, N, COLS), F32)] * 2,
            *[pltpu.VMEM((2 * N, COLS), F32)] * 2,
            pltpu.VMEM((ROWS, COLS), F32),
            pltpu.SemaphoreType.DMA((1,)),
        ],
        compiler_params=LIMIT,
        name="columns",
    )(weights, masks, inner_last, inner_total, strip0, from_left, from_right)


def turn_blocks(blocks):
    return pl.pallas_call(
        turn_blocks_kernel,
        in_specs=[VMEM],
        out_specs=VMEM,
        out_shape=jax.ShapeDtypeStruct(blocks.shape, BF16),
        compiler_params=LIMIT,
        cost_estimate=cost(1.0),
        name="turn_blocks",
    )(blocks)


def remap(table, heat, gathered, weights, fluxes, top):
    chunks = ROWS // CHUNK
    return pl.pallas_call(
        remap_kernel,
        in_specs=[ANY] + [VMEM] * 5,
        out_specs=[ANY] * 2,
        out_shape=[f32(FIELDS, ROWS, COLS), f32(ROWS, COLS)],
        scratch_shapes=[
            pltpu.SMEM(table.shape, jnp.int32),
            pltpu.VMEM((3 * FIELDS * ROWS, COLS), F32),
            pltpu.VMEM((FIELDS, ROWS, COLS), F32),
            pltpu.VMEM((ROWS, COLS), F32),
            pltpu.SemaphoreType.DMA((1,)),
            pltpu.SemaphoreType.DMA((2,)),
            pltpu.SemaphoreType.DMA((chunks,)),
            pltpu.SemaphoreType.DMA((chunks,)),
        ],
        compiler_params=LIMIT,
        name="remap",
    )(table, heat, gathered, weights, fluxes, top)


def body(
    state, winds, diffusivity, coupling, heat_coef, remap_blocks, source_patch, block_ids, land_sea
):
    group = lax.axis_index("grp")
    row_tile = lax.axis_index("gx")
    column_tile = lax.axis_index("gy")
    tiles_x = lax.axis_size("gx")
    tiles_y = lax.axis_size("gy")
    groups = lax.axis_size("grp")
    ocean = group == groups - 1
    line = group * tiles_x + row_tile
    top = (line == 0) | (ocean & (row_tile == 0))
    bottom = (row_tile == tiles_x - 1) & (group >= groups - 2)
    row = lax.broadcasted_iota(jnp.int32, (8, COLS), 0)
    lane = lax.broadcasted_iota(jnp.int32, (8, COLS), 1)
    row_one = jnp.where(row < 4, ~bottom, ~top).astype(F32)
    side_one = jnp.where((lane & 7) < 4, column_tile > 0, column_tile < tiles_y - 1).astype(F32)
    own_rate = jnp.where(ocean, diffusivity[1], diffusivity[0])
    rate = jnp.broadcast_to(own_rate[:, None], (LEVELS, 8)).reshape(1, COLS) * jnp.ones((8, 1), F32)
    masks = jnp.stack([row_one, side_one, rate])
    rates = jnp.broadcast_to(own_rate[:, None], (LEVELS, COLS))
    weights = jnp.broadcast_to(coupling.reshape(-1, 1), (FIELDS * LEVELS, COLS))
    source = source_patch[0, 0].T
    starts = (source // ROWS) * (FIELDS * ROWS) + source % ROWS
    table = jnp.concatenate([
        land_sea.reshape(-1),
        jnp.concatenate([starts, block_ids[0, 0].T], 1).reshape(-1),
        ocean.astype(jnp.int32)[None],
    ])
    heat = jnp.broadcast_to(heat_coef[:, None], (FIELDS, COLS))

    def ring(x, axis, shift):
        count = lax.axis_size(axis)
        return lax.ppermute(x, axis, [(i, (i + shift) % count) for i in range(count)])

    to_up, to_down = edge_rows(state, winds)
    from_below = ring(to_up, ("grp", "gx"), -1)
    from_above = ring(to_down, ("grp", "gx"), 1)
    own = own_strips(state, winds)
    halo, strip0, to_right, to_left = edge_columns(masks, from_below, from_above, own)
    from_left = ring(to_right, "gy", 1)
    from_right = ring(to_left, "gy", -1)
    inner_last, inner_total = inner_steps(rates, masks, state, winds, halo)
    turned = turn_blocks(remap_blocks)
    state_out, fluxes, rounded, top_level = columns(
        weights, masks, inner_last, inner_total, strip0, from_left, from_right
    )
    gathered = lax.all_gather(rounded, "grp", axis=0, tiled=True)
    fluxes, boundary = remap(
        table, heat, gathered, turned, fluxes, top_level
    )
    return state_out, boundary, fluxes


def solution(mesh):
    return jax.shard_map(
        body,
        mesh=mesh,
        in_specs=(
            P(None, ("grp", "gx"), "gy"),
            P(None, None, ("grp", "gx"), "gy"),
            P(),
            P(),
            P(),
            P(),
            P("gx", "gy", None, None),
            P("gx", "gy", None, None),
            P("gx", "gy", None),
        ),
        out_specs=(
            P(None, ("grp", "gx"), "gy"),
            P(("grp", "gx"), "gy"),
            P(None, ("grp", "gx"), "gy"),
        ),
        check_vma=False,
    )
```

```python
import jax
import jax.numpy as jnp
from jax import lax
from jax.experimental import pallas as pl
from jax.experimental.pallas import tpu as pltpu
from jax.sharding import PartitionSpec as P

FIELDS = 8
LEVELS = 16
SUBSTEPS = 4
INTERSECTIONS = 6
ROWS = 64
COLS = 128
TILES = ROWS // 8
BASE = 16
DEEP = ROWS + 32
UNROLL = 8
FLUX_ROWS = 32
CHUNK = 32
F32 = jnp.float32
BF16 = jnp.bfloat16

VMEM = pl.BlockSpec(memory_space=pltpu.VMEM)
SMEM = pl.BlockSpec(memory_space=pltpu.SMEM)
ANY = pl.BlockSpec(memory_space=pl.ANY)
HBM = pl.BlockSpec(memory_space=pltpu.HBM)


def sub_ids():
    return lax.broadcasted_iota(jnp.int32, (8, COLS), 0)


def lane_ids():
    return lax.broadcasted_iota(jnp.int32, (8, COLS), 1)


def edge_rows_kernel(state, winds, to_up, to_down, st_top, st_low, wi_top, wi_low,
                     sheet_up, sheet_down, sems):
    first, last = slice(0, 8), slice(ROWS - 8, ROWS)
    fetches = [
        pltpu.make_async_copy(source, target, sems.at[i])
        for i, (source, target) in enumerate((
            (winds.at[0, :, first], wi_top.at[0]),
            (winds.at[1, :, first], wi_top.at[1]),
            (winds.at[0, :, last], wi_low.at[0]),
            (winds.at[1, :, last], wi_low.at[1]),
            (state.at[:, first], st_top),
            (state.at[:, last], st_low),
        ))
    ]
    for fetch in fetches:
        fetch.start()
    for fetch in fetches:
        fetch.wait()
    upper = sub_ids() < 4
    for l in range(LEVELS):
        top, low = st_top[l], st_low[l]
        top_hi, low_hi = top.astype(BF16).astype(F32), low.astype(BF16).astype(F32)
        sheet_up[8 * l : 8 * l + 8] = jnp.where(upper, top_hi, pltpu.roll(top - top_hi, 4, 0))
        sheet_down[8 * l : 8 * l + 8] = jnp.where(upper, pltpu.roll(low_hi, 4, 0), low - low_hi)
        k = LEVELS + l
        sheet_up[8 * k : 8 * k + 8] = jnp.where(upper, wi_top[0, l], pltpu.roll(wi_top[1, l], 4, 0))
        sheet_down[8 * k : 8 * k + 8] = jnp.where(upper, pltpu.roll(wi_low[0, l], 4, 0), wi_low[1, l])
    to_up[...] = sheet_up[...].astype(BF16)
    to_down[...] = sheet_down[...].astype(BF16)


def packed(strip, tile, l):
    turned = pltpu.roll(tile, 8 * l + 4, 1)
    return jnp.where((lane_ids() >> 3) == l, turned, strip)


def own_strips_kernel(state, winds, strips):
    def row_tile(t, carry):
        r = pl.multiple_of(t * 8, 8)
        sources = (state, winds.at[0], winds.at[1])
        for c in range(3):
            strip = jnp.zeros((8, COLS), F32)
            for l in range(LEVELS):
                strip = packed(strip, sources[c][l, pl.ds(r, 8), :], l)
            strips[c, pl.ds(r, 8), :] = strip
        return carry

    lax.fori_loop(0, TILES, row_tile, 0)


def edge_columns_kernel(masks, from_below, from_above, own, halo, strip0, to_right, to_left,
                        below, above, full, right_sheet, left_sheet):
    below[...] = from_below[...].astype(F32)
    above[...] = from_above[...].astype(F32)
    upper = sub_ids() < 4
    ok = masks[0]
    full[:, 0:ROWS, :] = own[...]
    parts = [jnp.zeros((8, COLS), F32)] * 3
    for l in range(LEVELS):
        b, a = below[8 * l : 8 * l + 8], above[8 * l : 8 * l + 8]
        s = jnp.where(upper, b + pltpu.roll(b, 4, 0), a + pltpu.roll(a, 4, 0))
        k = LEVELS + l
        b, a = below[8 * k : 8 * k + 8], above[8 * k : 8 * k + 8]
        u = jnp.where(upper, b, pltpu.roll(a, 4, 0))
        v = jnp.where(upper, pltpu.roll(b, 4, 0), a)
        for c, x in enumerate((s, u, v)):
            x = x * ok
            halo[c, 8 * l : 8 * l + 8] = x
            parts[c] = packed(parts[c], x, l)
    for c in range(3):
        full[c, ROWS : ROWS + 8] = parts[c]
    strip0[...] = full[...]
    first = (lane_ids() & 7) < 4
    n = ROWS + 8
    for t in range(TILES + 1):
        r = 8 * t
        s, u, v = full[0, r : r + 8], full[1, r : r + 8], full[2, r : r + 8]
        hi = s.astype(BF16).astype(F32)
        lo = s - hi
        right_sheet[r : r + 8] = jnp.where(first, hi, pltpu.roll(lo, 4, 1))
        left_sheet[r : r + 8] = jnp.where(first, pltpu.roll(lo, COLS - 4, 1), hi)
        right_sheet[n + r : n + r + 8] = jnp.where(first, u, pltpu.roll(v, 4, 1))
        left_sheet[n + r : n + r + 8] = jnp.where(first, pltpu.roll(v, COLS - 4, 1), u)
    to_right[...] = right_sheet[...].astype(BF16)
    to_left[...] = left_sheet[...].astype(BF16)


def stencil(s, n, so, w, e, u, v, d, c):
    drift = u * (e - w) + v * (so - n)
    return c * s + d * ((n + so) + (w + e)) - 0.5 * drift


def inner_steps_kernel(rates, masks, state, winds, halo, last, total, cells0, cells1, cells2, cells3):
    own = slice(BASE, BASE + ROWS)
    high, low = slice(BASE - 8, BASE), slice(BASE + ROWS, BASE + ROWS + 8)
    upper = sub_ids() < 4
    lane = lane_ids()
    row_one = masks[0]

    def copy_level(l, carry):
        h = pl.multiple_of(8 * l, 8)
        cells0[l, own] = state[l]
        x = halo[0, pl.ds(h, 8), :]
        cells0[l, high] = x
        cells0[l, low] = x
        return carry

    lax.fori_loop(0, LEVELS, copy_level, 0, unroll=2)

    def step(src, dst):
        def level(l, carry):
            h = pl.multiple_of(8 * l, 8)
            d = rates[pl.ds(l, 1), :]
            for t in range(TILES if dst is None else TILES + 1):
                k = slice(8 * t, 8 * t + 8)
                r = BASE + 8 * t
                if t < TILES:
                    s, no, so = src[l, r : r + 8, :], src[l, r - 1 : r + 7, :], src[l, r + 1 : r + 9, :]
                    u, v = winds[0, l, k, :], winds[1, l, k, :]
                else:
                    s, no, so = halo_rows(lambda r: src[l, r : r + 8, :], upper)
                    u, v = halo[1, pl.ds(h, 8), :], halo[2, pl.ds(h, 8), :]
                    d = d * row_one
                w = jnp.where(lane == 0, 0.0, pltpu.roll(s, 1, 1))
                e = jnp.where(lane == COLS - 1, 0.0, pltpu.roll(s, COLS - 1, 1))
                x = stencil(s, no, so, w, e, u, v, d, 1.0 - 4.0 * d)
                if dst is None:
                    last[l, k, :] = x
                    total[l, k, :] = (cells1[l, r : r + 8, :] + cells2[l, r : r + 8, :]) + (s + x)
                elif t < TILES:
                    dst[l, r : r + 8, :] = x
                else:
                    dst[l, high, :] = x
                    dst[l, low, :] = x
            return carry

        lax.fori_loop(0, LEVELS, level, 0, unroll=UNROLL)

    step(cells0, cells1)
    step(cells1, cells2)
    step(cells2, cells3)
    step(cells3, None)


def halo_rows(load, upper):
    d, u = BASE + ROWS, BASE - 8
    return (
        load(d),
        jnp.where(upper, load(d - 1), load(u - 1)),
        jnp.where(upper, load(d + 1), load(u + 1)),
    )


def columns_kernel(weights, masks, inner_last, inner_total, strip0, from_left, from_right,
                   ready, fluxes, rounded,
                   lefts, rights, beyond, extras, left_winds, right_winds, left, right, extra_total):
    upper = sub_ids() < 4
    n = ROWS + 8
    own = slice(BASE, BASE + ROWS)
    high, low = slice(BASE - 8, BASE), slice(BASE + ROWS, BASE + ROWS + 8)
    lane = lane_ids()
    place = lane & 7
    first = place < 4
    row_one, side_one, rate = masks[0], masks[1], masks[2]

    def put(buf, t, x):
        if t < TILES:
            buf[BASE + 8 * t : BASE + 8 * t + 8] = x
        else:
            buf[high] = x
            buf[low] = x

    left[...] = from_left[...].astype(F32)
    right[...] = from_right[...].astype(F32)
    for t in range(TILES + 1):
        r, q = slice(8 * t, 8 * t + 8), slice(n + 8 * t, n + 8 * t + 8)
        a, b = left[r], right[r]
        a = (a + pltpu.roll(a, COLS - 4, 1)) * side_one
        b = (b + pltpu.roll(b, 4, 1)) * side_one
        put(lefts[0], t, jnp.where(first, a, strip0[0, r]))
        put(rights[0], t, jnp.where(first, strip0[0, r], b))
        beyond[0][r] = jnp.where(first, a, b)
        a, b = left[q], right[q]
        left_winds[0, r] = jnp.where(first, a * side_one, strip0[1, r])
        right_winds[0, r] = jnp.where(first, strip0[1, r], b * side_one)
        a, b = pltpu.roll(a, COLS - 4, 1), pltpu.roll(b, 4, 1)
        left_winds[1, r] = jnp.where(first, a * side_one, strip0[2, r])
        right_winds[1, r] = jnp.where(first, strip0[2, r], b * side_one)
    left_rate = jnp.where(first, rate * side_one, rate)
    right_rate = jnp.where(first, rate, rate * side_one)
    for step in range(SUBSTEPS):
        last = step == SUBSTEPS - 1
        if not last:
            for t in range(TILES + 1):
                r, k = BASE + 8 * t, slice(8 * t, 8 * t + 8)
                new = []
                for strip, wind, d in ((lefts[step], left_winds, left_rate), (rights[step], right_winds, right_rate)):
                    if t < TILES:
                        s, no, so = strip[r : r + 8], strip[r - 1 : r + 7], strip[r + 1 : r + 9]
                    else:
                        s, no, so = halo_rows(lambda r: strip[r : r + 8], upper)
                        d = d * row_one
                    w, e = pltpu.roll(s, 1, 1), pltpu.roll(s, COLS - 1, 1)
                    new.append(stencil(s, no, so, w, e, wind[0, k], wind[1, k], d, 1.0 - 4.0 * d))
                if step < SUBSTEPS - 2:
                    put(lefts[step + 1], t, new[0])
                    put(rights[step + 1], t, new[1])
                beyond[step + 1][k] = jnp.where(first, new[0], new[1])
        for t in range(TILES if last else TILES + 1):
            r, k = BASE + 8 * t, slice(8 * t, 8 * t + 8)
            side = beyond[step][k]
            d = rate if t < TILES else rate * row_one
            if step == 0:
                s = no = so = jnp.zeros((8, COLS), F32)
            elif t < TILES:
                old = extras[step - 1]
                s, no, so = old[r : r + 8], old[r - 1 : r + 7], old[r + 1 : r + 9]
            else:
                s, no, so = halo_rows(lambda r: extras[step - 1][r : r + 8], upper)
            w = pltpu.roll(jnp.where(place == 3, side, jnp.where(place == 7, 0.0, s)), 1, 1)
            e = pltpu.roll(jnp.where(place == 4, side, jnp.where(place == 0, 0.0, s)), COLS - 1, 1)
            x = stencil(s, no, so, w, e, strip0[1, k], strip0[2, k], d, 1.0 - 4.0 * d)
            put(extras[step], t, x)
            if t < TILES:
                extra_total[k] = x if step == 0 else extra_total[k] + x

    def edges(x, l):
        lanes = lax.broadcasted_iota(jnp.int32, x.shape, 1)
        return jnp.where((lanes < 4) | (lanes >= COLS - 4), pltpu.roll(x, COLS - 4 - 8 * l, 1), 0.0)

    def flux(t, carry):
        r = pl.multiple_of(FLUX_ROWS * t, FLUX_ROWS)
        out = pl.ds(r, FLUX_ROWS)
        inner = pl.ds(BASE + r, FLUX_ROWS)
        sums = [None] * FIELDS
        for l in range(LEVELS):
            ready[l, out, :] = inner_last[l, out, :] + edges(extras[SUBSTEPS - 1][inner, :], l)
            x = inner_total[l, out, :] + edges(extra_total[out, :], l)
            for f in range(FIELDS):
                k = f * LEVELS + l
                term = weights[k : k + 1, :] * x
                sums[f] = term if l == 0 else sums[f] + term
        for f in range(FIELDS):
            mean = sums[f] * (1.0 / SUBSTEPS)
            fluxes[f, out, :] = mean
            rounded[pl.ds(pl.multiple_of(f * ROWS + r, FLUX_ROWS), FLUX_ROWS), :] = mean.astype(BF16)
        return carry

    lax.fori_loop(0, ROWS // FLUX_ROWS, flux, 0)


def turn_blocks_kernel(blocks, turned):
    def turn(i, carry):
        turned[i] = blocks[i].T
        return carry

    lax.fori_loop(0, blocks.shape[0], turn, 0, unroll=8)


def remap_kernel(words, heat, gathered, weights, fluxes, field, state_out, flux_out, boundary_out,
                 table, patches, remapped, surface, state_sem, table_sem, out_sems, flux_sems, surface_sems):
    size = FIELDS * ROWS
    fetch = pltpu.make_async_copy(words, table, table_sem.at[0])
    fetch.start()
    keep = pltpu.make_async_copy(field, state_out, state_sem.at[0])
    keep.start()
    patches[...] = gathered[0 : 3 * size].astype(F32)
    fetch.wait()
    is_ocean = table[table.shape[0] - 1] == 1

    @pl.when(is_ocean)
    def _():
        def sends(i):
            at = pl.ds(pl.multiple_of(i * CHUNK, CHUNK), CHUNK)
            return (
                pltpu.make_async_copy(remapped.at[:, at], flux_out.at[:, at], flux_sems.at[i]),
                pltpu.make_async_copy(surface.at[at], boundary_out.at[at], surface_sems.at[i]),
            )

        def chunk(i, carry):
            at = pl.ds(pl.multiple_of(i * CHUNK, CHUNK), CHUNK)
            for j in range(CHUNK):
                o = i * CHUNK + j
                picked, chosen = [], []
                for entry in range(INTERSECTIONS):
                    at_entry = ROWS + 2 * ROWS * entry + o
                    start = table[at_entry]
                    picked.append(patches[pl.ds(start, FIELDS, stride=ROWS), :].astype(BF16))
                    chosen.append(weights[table[at_entry + ROWS]])
                total = jnp.dot(
                    jnp.concatenate(picked, 1), jnp.concatenate(chosen, 0), preferred_element_type=F32
                )
                remapped[:, o, :] = total * table[o].astype(F32)
            warmth = field[0, at, :]
            for f in range(FIELDS):
                warmth = warmth + heat[f : f + 1] * remapped[f, at, :]
            surface[at, :] = warmth
            for send in sends(i):
                send.start()
            return carry

        lax.fori_loop(0, ROWS // CHUNK, chunk, 0)
        for i in range(ROWS // CHUNK):
            for send in sends(i):
                send.wait()

    @pl.when(jnp.logical_not(is_ocean))
    def _():
        copies = (
            pltpu.make_async_copy(fluxes, flux_out, out_sems.at[0]),
            pltpu.make_async_copy(fluxes.at[0], boundary_out, out_sems.at[1]),
        )
        for copy in copies:
            copy.start()
        for copy in copies:
            copy.wait()

    keep.wait()


WIDE = pltpu.CompilerParams(vmem_limit_bytes=53 * 2**20 + 5 * 2**17)
LIMIT = pltpu.CompilerParams(vmem_limit_bytes=16 * 2**20)
N = ROWS + 8
SHEET = jax.ShapeDtypeStruct((2 * LEVELS * 8, COLS), BF16)
COLUMNS = jax.ShapeDtypeStruct((2 * N, COLS), BF16)


def cost(microseconds):
    return pl.CostEstimate(
        flops=int(1e9 * microseconds), bytes_accessed=int(3.6e6 * microseconds), transcendentals=0
    )


def f32(*shape):
    return jax.ShapeDtypeStruct(shape, F32)


def edge_rows(state, winds):
    return pl.pallas_call(
        edge_rows_kernel,
        in_specs=[HBM, HBM],
        out_specs=[VMEM, VMEM],
        out_shape=[SHEET, SHEET],
        scratch_shapes=[
            *[pltpu.VMEM((LEVELS, 8, COLS), F32)] * 2,
            *[pltpu.VMEM((2, LEVELS, 8, COLS), F32)] * 2,
            *[pltpu.VMEM(SHEET.shape, F32)] * 2,
            pltpu.SemaphoreType.DMA((6,)),
        ],
        compiler_params=WIDE,
        cost_estimate=cost(1.1),
        name="edge_rows",
    )(state, winds)


def own_strips(state, winds):
    return pl.pallas_call(
        own_strips_kernel,
        in_specs=[VMEM, VMEM],
        out_specs=VMEM,
        out_shape=f32(3, ROWS, COLS),
        compiler_params=LIMIT,
        cost_estimate=cost(1.0),
        name="own_strips",
    )(state, winds)


def edge_columns(masks, from_below, from_above, own):
    return pl.pallas_call(
        edge_columns_kernel,
        in_specs=[VMEM] * 4,
        out_specs=[VMEM] * 4,
        out_shape=[f32(3, LEVELS * 8, COLS), f32(3, N, COLS), COLUMNS, COLUMNS],
        scratch_shapes=[
            pltpu.VMEM(SHEET.shape, F32),
            pltpu.VMEM(SHEET.shape, F32),
            pltpu.VMEM((3, N, COLS), F32),
            pltpu.VMEM((2 * N, COLS), F32),
            pltpu.VMEM((2 * N, COLS), F32),
        ],
        compiler_params=LIMIT,
        cost_estimate=cost(0.2),
        name="edge_columns",
    )(masks, from_below, from_above, own)


def inner_steps(rates, masks, state, winds, halo):
    return pl.pallas_call(
        inner_steps_kernel,
        in_specs=[VMEM] * 5,
        out_specs=[VMEM] * 2,
        out_shape=[f32(LEVELS, ROWS, COLS)] * 2,
        scratch_shapes=[pltpu.VMEM((LEVELS, DEEP, COLS), F32)] * 4,
        compiler_params=LIMIT,
        cost_estimate=cost(2.5),
        name="inner_steps",
    )(rates, masks, state, winds, halo)


def columns(weights, masks, inner_last, inner_total, strip0, from_left, from_right):
    return pl.pallas_call(
        columns_kernel,
        in_specs=[VMEM] * 7,
        out_specs=[VMEM] * 3,
        out_shape=[
            f32(LEVELS, ROWS, COLS),
            f32(FIELDS, ROWS, COLS),
            jax.ShapeDtypeStruct((FIELDS * ROWS, COLS), BF16),
        ],
        scratch_shapes=[
            [pltpu.VMEM((DEEP, COLS), F32)] * 3,
            [pltpu.VMEM((DEEP, COLS), F32)] * 3,
            [pltpu.VMEM((N, COLS), F32)] * 4,
            [pltpu.VMEM((DEEP, COLS), F32)] * 4,
            *[pltpu.VMEM((2, N, COLS), F32)] * 2,
            *[pltpu.VMEM((2 * N, COLS), F32)] * 2,
            pltpu.VMEM((ROWS, COLS), F32),
        ],
        compiler_params=LIMIT,
        name="columns",
    )(weights, masks, inner_last, inner_total, strip0, from_left, from_right)


def turn_blocks(blocks):
    return pl.pallas_call(
        turn_blocks_kernel,
        in_specs=[VMEM],
        out_specs=VMEM,
        out_shape=jax.ShapeDtypeStruct(blocks.shape, BF16),
        compiler_params=LIMIT,
        cost_estimate=cost(1.0),
        name="turn_blocks",
    )(blocks)


def remap(table, heat, gathered, weights, fluxes, field):
    chunks = ROWS // CHUNK
    return pl.pallas_call(
        remap_kernel,
        in_specs=[ANY] + [VMEM] * 5,
        out_specs=[ANY] * 3,
        out_shape=[f32(LEVELS, ROWS, COLS), f32(FIELDS, ROWS, COLS), f32(ROWS, COLS)],
        scratch_shapes=[
            pltpu.SMEM(table.shape, jnp.int32),
            pltpu.VMEM((3 * FIELDS * ROWS, COLS), F32),
            pltpu.VMEM((FIELDS, ROWS, COLS), F32),
            pltpu.VMEM((ROWS, COLS), F32),
            pltpu.SemaphoreType.DMA((1,)),
            pltpu.SemaphoreType.DMA((1,)),
            pltpu.SemaphoreType.DMA((2,)),
            pltpu.SemaphoreType.DMA((chunks,)),
            pltpu.SemaphoreType.DMA((chunks,)),
        ],
        compiler_params=LIMIT,
        name="remap",
    )(table, heat, gathered, weights, fluxes, field)


def body(
    state, winds, diffusivity, coupling, heat_coef, remap_blocks, source_patch, block_ids, land_sea
):
    group = lax.axis_index("grp")
    row_tile = lax.axis_index("gx")
    column_tile = lax.axis_index("gy")
    tiles_x = lax.axis_size("gx")
    tiles_y = lax.axis_size("gy")
    groups = lax.axis_size("grp")
    ocean = group == groups - 1
    line = group * tiles_x + row_tile
    top = (line == 0) | (ocean & (row_tile == 0))
    bottom = (row_tile == tiles_x - 1) & (group >= groups - 2)
    row = lax.broadcasted_iota(jnp.int32, (8, COLS), 0)
    lane = lax.broadcasted_iota(jnp.int32, (8, COLS), 1)
    row_one = jnp.where(row < 4, ~bottom, ~top).astype(F32)
    side_one = jnp.where((lane & 7) < 4, column_tile > 0, column_tile < tiles_y - 1).astype(F32)
    own_rate = jnp.where(ocean, diffusivity[1], diffusivity[0])
    rate = jnp.broadcast_to(own_rate[:, None], (LEVELS, 8)).reshape(1, COLS) * jnp.ones((8, 1), F32)
    masks = jnp.stack([row_one, side_one, rate])
    rates = jnp.broadcast_to(own_rate[:, None], (LEVELS, COLS))
    weights = jnp.broadcast_to(coupling.reshape(-1, 1), (FIELDS * LEVELS, COLS))
    source = source_patch[0, 0].T
    starts = (source // ROWS) * (FIELDS * ROWS) + source % ROWS
    table = jnp.concatenate([
        land_sea.reshape(-1),
        jnp.concatenate([starts, block_ids[0, 0].T], 1).reshape(-1),
        ocean.astype(jnp.int32)[None],
    ])
    heat = jnp.broadcast_to(heat_coef[:, None], (FIELDS, COLS))

    def ring(x, axis, shift):
        count = lax.axis_size(axis)
        return lax.ppermute(x, axis, [(i, (i + shift) % count) for i in range(count)])

    to_up, to_down = edge_rows(state, winds)
    from_below = ring(to_up, ("grp", "gx"), -1)
    from_above = ring(to_down, ("grp", "gx"), 1)
    own = own_strips(state, winds)
    halo, strip0, to_right, to_left = edge_columns(masks, from_below, from_above, own)
    from_left = ring(to_right, "gy", 1)
    from_right = ring(to_left, "gy", -1)
    inner_last, inner_total = inner_steps(rates, masks, state, winds, halo)
    turned = turn_blocks(remap_blocks)
    field, fluxes, rounded = columns(
        weights, masks, inner_last, inner_total, strip0, from_left, from_right
    )
    gathered = lax.all_gather(rounded, "grp", axis=0, tiled=True)
    state_out, fluxes, boundary = remap(table, heat, gathered, turned, fluxes, field)
    return state_out, boundary, fluxes


def solution(mesh):
    return jax.shard_map(
        body,
        mesh=mesh,
        in_specs=(
            P(None, ("grp", "gx"), "gy"),
            P(None, None, ("grp", "gx"), "gy"),
            P(),
            P(),
            P(),
            P(),
            P("gx", "gy", None, None),
            P("gx", "gy", None, None),
            P("gx", "gy", None),
        ),
        out_specs=(
            P(None, ("grp", "gx"), "gy"),
            P(("grp", "gx"), "gy"),
            P(None, ("grp", "gx"), "gy"),
        ),
        check_vma=False,
    )
```

```python
import jax
import jax.numpy as jnp
from jax import lax
from jax.experimental import pallas as pl
from jax.experimental.pallas import tpu as pltpu
from jax.sharding import PartitionSpec as P

FIELDS = 8
LEVELS = 16
SUBSTEPS = 4
INTERSECTIONS = 6
ROWS = 64
COLS = 128
TILES = ROWS // 8
BASE = 16
DEEP = ROWS + 32
UNROLL = 16
FLUX_ROWS = 32
CHUNK = 32
F32 = jnp.float32
BF16 = jnp.bfloat16

VMEM = pl.BlockSpec(memory_space=pltpu.VMEM)
SMEM = pl.BlockSpec(memory_space=pltpu.SMEM)
ANY = pl.BlockSpec(memory_space=pl.ANY)
HBM = pl.BlockSpec(memory_space=pltpu.HBM)


def sub_ids():
    return lax.broadcasted_iota(jnp.int32, (8, COLS), 0)


def lane_ids():
    return lax.broadcasted_iota(jnp.int32, (8, COLS), 1)


def edge_rows_kernel(state, winds, to_up, to_down, st_top, st_low, wi_top, wi_low,
                     sheet_up, sheet_down, sems):
    first, last = slice(0, 8), slice(ROWS - 8, ROWS)
    fetches = [
        pltpu.make_async_copy(source, target, sems.at[i])
        for i, (source, target) in enumerate((
            (winds.at[0, :, first], wi_top.at[0]),
            (winds.at[1, :, first], wi_top.at[1]),
            (winds.at[0, :, last], wi_low.at[0]),
            (winds.at[1, :, last], wi_low.at[1]),
            (state.at[:, first], st_top),
            (state.at[:, last], st_low),
        ))
    ]
    for fetch in fetches:
        fetch.start()
    for fetch in fetches:
        fetch.wait()
    upper = sub_ids() < 4
    for l in range(LEVELS):
        top, low = st_top[l], st_low[l]
        top_hi, low_hi = top.astype(BF16).astype(F32), low.astype(BF16).astype(F32)
        sheet_up[8 * l : 8 * l + 8] = jnp.where(upper, top_hi, pltpu.roll(top - top_hi, 4, 0))
        sheet_down[8 * l : 8 * l + 8] = jnp.where(upper, pltpu.roll(low_hi, 4, 0), low - low_hi)
        k = LEVELS + l
        sheet_up[8 * k : 8 * k + 8] = jnp.where(upper, wi_top[0, l], pltpu.roll(wi_top[1, l], 4, 0))
        sheet_down[8 * k : 8 * k + 8] = jnp.where(upper, pltpu.roll(wi_low[0, l], 4, 0), wi_low[1, l])
    to_up[...] = sheet_up[...].astype(BF16)
    to_down[...] = sheet_down[...].astype(BF16)


def packed(strip, tile, l):
    turned = pltpu.roll(tile, 8 * l + 4, 1)
    return jnp.where((lane_ids() >> 3) == l, turned, strip)


def own_strips_kernel(state, winds, strips):
    def row_tile(t, carry):
        r = pl.multiple_of(t * 8, 8)
        sources = (state, winds.at[0], winds.at[1])
        for c in range(3):
            strip = jnp.zeros((8, COLS), F32)
            for l in range(LEVELS):
                strip = packed(strip, sources[c][l, pl.ds(r, 8), :], l)
            strips[c, pl.ds(r, 8), :] = strip
        return carry

    lax.fori_loop(0, TILES, row_tile, 0, unroll=8)


def edge_columns_kernel(masks, from_below, from_above, own, halo, strip0, to_right, to_left,
                        below, above, full, right_sheet, left_sheet):
    below[...] = from_below[...].astype(F32)
    above[...] = from_above[...].astype(F32)
    upper = sub_ids() < 4
    ok = masks[0]
    full[:, 0:ROWS, :] = own[...]
    parts = [jnp.zeros((8, COLS), F32)] * 3
    for l in range(LEVELS):
        b, a = below[8 * l : 8 * l + 8], above[8 * l : 8 * l + 8]
        s = jnp.where(upper, b + pltpu.roll(b, 4, 0), a + pltpu.roll(a, 4, 0))
        k = LEVELS + l
        b, a = below[8 * k : 8 * k + 8], above[8 * k : 8 * k + 8]
        u = jnp.where(upper, b, pltpu.roll(a, 4, 0))
        v = jnp.where(upper, pltpu.roll(b, 4, 0), a)
        for c, x in enumerate((s, u, v)):
            x = x * ok
            halo[c, 8 * l : 8 * l + 8] = x
            parts[c] = packed(parts[c], x, l)
    for c in range(3):
        full[c, ROWS : ROWS + 8] = parts[c]
    strip0[...] = full[...]
    first = (lane_ids() & 7) < 4
    n = ROWS + 8
    for t in range(TILES + 1):
        r = 8 * t
        s, u, v = full[0, r : r + 8], full[1, r : r + 8], full[2, r : r + 8]
        hi = s.astype(BF16).astype(F32)
        lo = s - hi
        right_sheet[r : r + 8] = jnp.where(first, hi, pltpu.roll(lo, 4, 1))
        left_sheet[r : r + 8] = jnp.where(first, pltpu.roll(lo, COLS - 4, 1), hi)
        right_sheet[n + r : n + r + 8] = jnp.where(first, u, pltpu.roll(v, 4, 1))
        left_sheet[n + r : n + r + 8] = jnp.where(first, pltpu.roll(v, COLS - 4, 1), u)
    to_right[...] = right_sheet[...].astype(BF16)
    to_left[...] = left_sheet[...].astype(BF16)


def stencil(s, n, so, w, e, u, v, d, c):
    drift = u * (e - w) + v * (so - n)
    return c * s + d * ((n + so) + (w + e)) - 0.5 * drift


def inner_steps_kernel(rates, masks, state, winds, halo, last, total, cells0, cells1, cells2, cells3):
    own = slice(BASE, BASE + ROWS)
    high, low = slice(BASE - 8, BASE), slice(BASE + ROWS, BASE + ROWS + 8)
    upper = sub_ids() < 4
    lane = lane_ids()
    row_one = masks[0]

    def copy_level(l, carry):
        h = pl.multiple_of(8 * l, 8)
        cells0[l, own] = state[l]
        x = halo[0, pl.ds(h, 8), :]
        cells0[l, high] = x
        cells0[l, low] = x
        return carry

    lax.fori_loop(0, LEVELS, copy_level, 0, unroll=2)

    def step(src, dst):
        def level(l, carry):
            h = pl.multiple_of(8 * l, 8)
            d = rates[pl.ds(l, 1), :]
            for t in range(TILES if dst is None else TILES + 1):
                k = slice(8 * t, 8 * t + 8)
                r = BASE + 8 * t
                if t < TILES:
                    s, no, so = src[l, r : r + 8, :], src[l, r - 1 : r + 7, :], src[l, r + 1 : r + 9, :]
                    u, v = winds[0, l, k, :], winds[1, l, k, :]
                else:
                    s, no, so = halo_rows(lambda r: src[l, r : r + 8, :], upper)
                    u, v = halo[1, pl.ds(h, 8), :], halo[2, pl.ds(h, 8), :]
                    d = d * row_one
                w = jnp.where(lane == 0, 0.0, pltpu.roll(s, 1, 1))
                e = jnp.where(lane == COLS - 1, 0.0, pltpu.roll(s, COLS - 1, 1))
                x = stencil(s, no, so, w, e, u, v, d, 1.0 - 4.0 * d)
                if dst is None:
                    last[l, k, :] = x
                    total[l, k, :] = (cells1[l, r : r + 8, :] + cells2[l, r : r + 8, :]) + (s + x)
                elif t < TILES:
                    dst[l, r : r + 8, :] = x
                else:
                    dst[l, high, :] = x
                    dst[l, low, :] = x
            return carry

        lax.fori_loop(0, LEVELS, level, 0, unroll=UNROLL)

    step(cells0, cells1)
    step(cells1, cells2)
    step(cells2, cells3)
    step(cells3, None)


def halo_rows(load, upper):
    d, u = BASE + ROWS, BASE - 8
    return (
        load(d),
        jnp.where(upper, load(d - 1), load(u - 1)),
        jnp.where(upper, load(d + 1), load(u + 1)),
    )


def columns_kernel(weights, masks, inner_last, inner_total, strip0, from_left, from_right,
                   ready, fluxes, rounded,
                   lefts, rights, beyond, extras, left_winds, right_winds, left, right, extra_total):
    upper = sub_ids() < 4
    n = ROWS + 8
    own = slice(BASE, BASE + ROWS)
    high, low = slice(BASE - 8, BASE), slice(BASE + ROWS, BASE + ROWS + 8)
    lane = lane_ids()
    place = lane & 7
    first = place < 4
    row_one, side_one, rate = masks[0], masks[1], masks[2]

    def put(buf, t, x):
        if t < TILES:
            buf[BASE + 8 * t : BASE + 8 * t + 8] = x
        else:
            buf[high] = x
            buf[low] = x

    left[...] = from_left[...].astype(F32)
    right[...] = from_right[...].astype(F32)
    for t in range(TILES + 1):
        r, q = slice(8 * t, 8 * t + 8), slice(n + 8 * t, n + 8 * t + 8)
        a, b = left[r], right[r]
        a = (a + pltpu.roll(a, COLS - 4, 1)) * side_one
        b = (b + pltpu.roll(b, 4, 1)) * side_one
        put(lefts[0], t, jnp.where(first, a, strip0[0, r]))
        put(rights[0], t, jnp.where(first, strip0[0, r], b))
        beyond[0][r] = jnp.where(first, a, b)
        a, b = left[q], right[q]
        left_winds[0, r] = jnp.where(first, a * side_one, strip0[1, r])
        right_winds[0, r] = jnp.where(first, strip0[1, r], b * side_one)
        a, b = pltpu.roll(a, COLS - 4, 1), pltpu.roll(b, 4, 1)
        left_winds[1, r] = jnp.where(first, a * side_one, strip0[2, r])
        right_winds[1, r] = jnp.where(first, strip0[2, r], b * side_one)
    left_rate = jnp.where(first, rate * side_one, rate)
    right_rate = jnp.where(first, rate, rate * side_one)
    for step in range(SUBSTEPS):
        last = step == SUBSTEPS - 1
        if not last:
            for t in range(TILES + 1):
                r, k = BASE + 8 * t, slice(8 * t, 8 * t + 8)
                new = []
                for strip, wind, d in ((lefts[step], left_winds, left_rate), (rights[step], right_winds, right_rate)):
                    if t < TILES:
                        s, no, so = strip[r : r + 8], strip[r - 1 : r + 7], strip[r + 1 : r + 9]
                    else:
                        s, no, so = halo_rows(lambda r: strip[r : r + 8], upper)
                        d = d * row_one
                    w, e = pltpu.roll(s, 1, 1), pltpu.roll(s, COLS - 1, 1)
                    new.append(stencil(s, no, so, w, e, wind[0, k], wind[1, k], d, 1.0 - 4.0 * d))
                if step < SUBSTEPS - 2:
                    put(lefts[step + 1], t, new[0])
                    put(rights[step + 1], t, new[1])
                beyond[step + 1][k] = jnp.where(first, new[0], new[1])
        for t in range(TILES if last else TILES + 1):
            r, k = BASE + 8 * t, slice(8 * t, 8 * t + 8)
            side = beyond[step][k]
            d = rate if t < TILES else rate * row_one
            if step == 0:
                s = no = so = jnp.zeros((8, COLS), F32)
            elif t < TILES:
                old = extras[step - 1]
                s, no, so = old[r : r + 8], old[r - 1 : r + 7], old[r + 1 : r + 9]
            else:
                s, no, so = halo_rows(lambda r: extras[step - 1][r : r + 8], upper)
            w = pltpu.roll(jnp.where(place == 3, side, jnp.where(place == 7, 0.0, s)), 1, 1)
            e = pltpu.roll(jnp.where(place == 4, side, jnp.where(place == 0, 0.0, s)), COLS - 1, 1)
            x = stencil(s, no, so, w, e, strip0[1, k], strip0[2, k], d, 1.0 - 4.0 * d)
            put(extras[step], t, x)
            if t < TILES:
                extra_total[k] = x if step == 0 else extra_total[k] + x

    def edges(x, l):
        lanes = lax.broadcasted_iota(jnp.int32, x.shape, 1)
        return jnp.where((lanes < 4) | (lanes >= COLS - 4), pltpu.roll(x, COLS - 4 - 8 * l, 1), 0.0)

    def flux(t, carry):
        r = pl.multiple_of(FLUX_ROWS * t, FLUX_ROWS)
        out = pl.ds(r, FLUX_ROWS)
        inner = pl.ds(BASE + r, FLUX_ROWS)
        sums = [None] * FIELDS
        for l in range(LEVELS):
            ready[l, out, :] = inner_last[l, out, :] + edges(extras[SUBSTEPS - 1][inner, :], l)
            x = inner_total[l, out, :] + edges(extra_total[out, :], l)
            for f in range(FIELDS):
                k = f * LEVELS + l
                term = weights[k : k + 1, :] * x
                sums[f] = term if l == 0 else sums[f] + term
        for f in range(FIELDS):
            mean = sums[f] * (1.0 / SUBSTEPS)
            fluxes[f, out, :] = mean
            rounded[pl.ds(pl.multiple_of(f * ROWS + r, FLUX_ROWS), FLUX_ROWS), :] = mean.astype(BF16)
        return carry

    lax.fori_loop(0, ROWS // FLUX_ROWS, flux, 0)


def turn_blocks_kernel(blocks, turned):
    def turn(i, carry):
        turned[i] = blocks[i].T
        return carry

    lax.fori_loop(0, blocks.shape[0], turn, 0, unroll=32)


def remap_kernel(words, heat, gathered, weights, fluxes, field, state_out, flux_out, boundary_out,
                 table, patches, remapped, surface, state_sem, table_sem, out_sems, flux_sems, surface_sems):
    size = FIELDS * ROWS
    fetch = pltpu.make_async_copy(words, table, table_sem.at[0])
    fetch.start()
    keep = pltpu.make_async_copy(field, state_out, state_sem.at[0])
    keep.start()
    patches[...] = gathered[0 : 3 * size].astype(F32)
    fetch.wait()
    is_ocean = table[table.shape[0] - 1] == 1

    @pl.when(is_ocean)
    def _():
        def sends(i):
            at = pl.ds(pl.multiple_of(i * CHUNK, CHUNK), CHUNK)
            return (
                pltpu.make_async_copy(remapped.at[:, at], flux_out.at[:, at], flux_sems.at[i]),
                pltpu.make_async_copy(surface.at[at], boundary_out.at[at], surface_sems.at[i]),
            )

        def chunk(i, carry):
            at = pl.ds(pl.multiple_of(i * CHUNK, CHUNK), CHUNK)
            for j in range(CHUNK):
                o = i * CHUNK + j
                picked, chosen = [], []
                for entry in range(INTERSECTIONS):
                    at_entry = ROWS + 2 * ROWS * entry + o
                    start = table[at_entry]
                    picked.append(patches[pl.ds(start, FIELDS, stride=ROWS), :].astype(BF16))
                    chosen.append(weights[table[at_entry + ROWS]])
                total = jnp.dot(
                    jnp.concatenate(picked, 1), jnp.concatenate(chosen, 0), preferred_element_type=F32
                )
                remapped[:, o, :] = total * table[o].astype(F32)
            warmth = field[0, at, :]
            for f in range(FIELDS):
                warmth = warmth + heat[f : f + 1] * remapped[f, at, :]
            surface[at, :] = warmth
            for send in sends(i):
                send.start()
            return carry

        lax.fori_loop(0, ROWS // CHUNK, chunk, 0)
        for i in range(ROWS // CHUNK):
            for send in sends(i):
                send.wait()

    @pl.when(jnp.logical_not(is_ocean))
    def _():
        copies = (
            pltpu.make_async_copy(fluxes, flux_out, out_sems.at[0]),
            pltpu.make_async_copy(fluxes.at[0], boundary_out, out_sems.at[1]),
        )
        for copy in copies:
            copy.start()
        for copy in copies:
            copy.wait()

    keep.wait()


WIDE = pltpu.CompilerParams(vmem_limit_bytes=53 * 2**20 + 5 * 2**17)
LIMIT = pltpu.CompilerParams(vmem_limit_bytes=16 * 2**20)
N = ROWS + 8
SHEET = jax.ShapeDtypeStruct((2 * LEVELS * 8, COLS), BF16)
COLUMNS = jax.ShapeDtypeStruct((2 * N, COLS), BF16)


def cost(microseconds):
    return pl.CostEstimate(
        flops=int(1e9 * microseconds), bytes_accessed=int(3.6e6 * microseconds), transcendentals=0
    )


def f32(*shape):
    return jax.ShapeDtypeStruct(shape, F32)


def edge_rows(state, winds):
    return pl.pallas_call(
        edge_rows_kernel,
        in_specs=[HBM, HBM],
        out_specs=[VMEM, VMEM],
        out_shape=[SHEET, SHEET],
        scratch_shapes=[
            *[pltpu.VMEM((LEVELS, 8, COLS), F32)] * 2,
            *[pltpu.VMEM((2, LEVELS, 8, COLS), F32)] * 2,
            *[pltpu.VMEM(SHEET.shape, F32)] * 2,
            pltpu.SemaphoreType.DMA((6,)),
        ],
        compiler_params=WIDE,
        cost_estimate=cost(1.1),
        name="edge_rows",
    )(state, winds)


def own_strips(state, winds):
    return pl.pallas_call(
        own_strips_kernel,
        in_specs=[VMEM, VMEM],
        out_specs=VMEM,
        out_shape=f32(3, ROWS, COLS),
        compiler_params=LIMIT,
        cost_estimate=cost(1.0),
        name="own_strips",
    )(state, winds)


def edge_columns(masks, from_below, from_above, own):
    return pl.pallas_call(
        edge_columns_kernel,
        in_specs=[VMEM] * 4,
        out_specs=[VMEM] * 4,
        out_shape=[f32(3, LEVELS * 8, COLS), f32(3, N, COLS), COLUMNS, COLUMNS],
        scratch_shapes=[
            pltpu.VMEM(SHEET.shape, F32),
            pltpu.VMEM(SHEET.shape, F32),
            pltpu.VMEM((3, N, COLS), F32),
            pltpu.VMEM((2 * N, COLS), F32),
            pltpu.VMEM((2 * N, COLS), F32),
        ],
        compiler_params=LIMIT,
        cost_estimate=cost(0.2),
        name="edge_columns",
    )(masks, from_below, from_above, own)


def inner_steps(rates, masks, state, winds, halo):
    return pl.pallas_call(
        inner_steps_kernel,
        in_specs=[VMEM] * 5,
        out_specs=[VMEM] * 2,
        out_shape=[f32(LEVELS, ROWS, COLS)] * 2,
        scratch_shapes=[pltpu.VMEM((LEVELS, DEEP, COLS), F32)] * 4,
        compiler_params=LIMIT,
        cost_estimate=cost(2.5),
        name="inner_steps",
    )(rates, masks, state, winds, halo)


def columns(weights, masks, inner_last, inner_total, strip0, from_left, from_right):
    return pl.pallas_call(
        columns_kernel,
        in_specs=[VMEM] * 7,
        out_specs=[VMEM] * 3,
        out_shape=[
            f32(LEVELS, ROWS, COLS),
            f32(FIELDS, ROWS, COLS),
            jax.ShapeDtypeStruct((FIELDS * ROWS, COLS), BF16),
        ],
        scratch_shapes=[
            [pltpu.VMEM((DEEP, COLS), F32)] * 3,
            [pltpu.VMEM((DEEP, COLS), F32)] * 3,
            [pltpu.VMEM((N, COLS), F32)] * 4,
            [pltpu.VMEM((DEEP, COLS), F32)] * 4,
            *[pltpu.VMEM((2, N, COLS), F32)] * 2,
            *[pltpu.VMEM((2 * N, COLS), F32)] * 2,
            pltpu.VMEM((ROWS, COLS), F32),
        ],
        compiler_params=LIMIT,
        name="columns",
    )(weights, masks, inner_last, inner_total, strip0, from_left, from_right)


def turn_blocks(blocks):
    return pl.pallas_call(
        turn_blocks_kernel,
        in_specs=[VMEM],
        out_specs=VMEM,
        out_shape=jax.ShapeDtypeStruct(blocks.shape, BF16),
        compiler_params=LIMIT,
        cost_estimate=cost(1.0),
        name="turn_blocks",
    )(blocks)


def remap(table, heat, gathered, weights, fluxes, field):
    chunks = ROWS // CHUNK
    return pl.pallas_call(
        remap_kernel,
        in_specs=[ANY] + [VMEM] * 5,
        out_specs=[ANY] * 3,
        out_shape=[f32(LEVELS, ROWS, COLS), f32(FIELDS, ROWS, COLS), f32(ROWS, COLS)],
        scratch_shapes=[
            pltpu.SMEM(table.shape, jnp.int32),
            pltpu.VMEM((3 * FIELDS * ROWS, COLS), F32),
            pltpu.VMEM((FIELDS, ROWS, COLS), F32),
            pltpu.VMEM((ROWS, COLS), F32),
            pltpu.SemaphoreType.DMA((1,)),
            pltpu.SemaphoreType.DMA((1,)),
            pltpu.SemaphoreType.DMA((2,)),
            pltpu.SemaphoreType.DMA((chunks,)),
            pltpu.SemaphoreType.DMA((chunks,)),
        ],
        compiler_params=LIMIT,
        name="remap",
    )(table, heat, gathered, weights, fluxes, field)


def body(
    state, winds, diffusivity, coupling, heat_coef, remap_blocks, source_patch, block_ids, land_sea
):
    group = lax.axis_index("grp")
    row_tile = lax.axis_index("gx")
    column_tile = lax.axis_index("gy")
    tiles_x = lax.axis_size("gx")
    tiles_y = lax.axis_size("gy")
    groups = lax.axis_size("grp")
    ocean = group == groups - 1
    line = group * tiles_x + row_tile
    top = (line == 0) | (ocean & (row_tile == 0))
    bottom = (row_tile == tiles_x - 1) & (group >= groups - 2)
    row = lax.broadcasted_iota(jnp.int32, (8, COLS), 0)
    lane = lax.broadcasted_iota(jnp.int32, (8, COLS), 1)
    row_one = jnp.where(row < 4, ~bottom, ~top).astype(F32)
    side_one = jnp.where((lane & 7) < 4, column_tile > 0, column_tile < tiles_y - 1).astype(F32)
    own_rate = jnp.where(ocean, diffusivity[1], diffusivity[0])
    rate = jnp.broadcast_to(own_rate[:, None], (LEVELS, 8)).reshape(1, COLS) * jnp.ones((8, 1), F32)
    masks = jnp.stack([row_one, side_one, rate])
    rates = jnp.broadcast_to(own_rate[:, None], (LEVELS, COLS))
    weights = jnp.broadcast_to(coupling.reshape(-1, 1), (FIELDS * LEVELS, COLS))
    source = source_patch[0, 0].T
    starts = (source // ROWS) * (FIELDS * ROWS) + source % ROWS
    table = jnp.concatenate([
        land_sea.reshape(-1),
        jnp.concatenate([starts, block_ids[0, 0].T], 1).reshape(-1),
        ocean.astype(jnp.int32)[None],
    ])
    heat = jnp.broadcast_to(heat_coef[:, None], (FIELDS, COLS))

    def ring(x, axis, shift):
        count = lax.axis_size(axis)
        return lax.ppermute(x, axis, [(i, (i + shift) % count) for i in range(count)])

    to_up, to_down = edge_rows(state, winds)
    from_below = ring(to_up, ("grp", "gx"), -1)
    from_above = ring(to_down, ("grp", "gx"), 1)
    own = own_strips(state, winds)
    halo, strip0, to_right, to_left = edge_columns(masks, from_below, from_above, own)
    from_left = ring(to_right, "gy", 1)
    from_right = ring(to_left, "gy", -1)
    inner_last, inner_total = inner_steps(rates, masks, state, winds, halo)
    turned = turn_blocks(remap_blocks)
    field, fluxes, rounded = columns(
        weights, masks, inner_last, inner_total, strip0, from_left, from_right
    )
    gathered = lax.all_gather(rounded, "grp", axis=0, tiled=True)
    state_out, fluxes, boundary = remap(table, heat, gathered, turned, fluxes, field)
    return state_out, boundary, fluxes


def solution(mesh):
    return jax.shard_map(
        body,
        mesh=mesh,
        in_specs=(
            P(None, ("grp", "gx"), "gy"),
            P(None, None, ("grp", "gx"), "gy"),
            P(),
            P(),
            P(),
            P(),
            P("gx", "gy", None, None),
            P("gx", "gy", None, None),
            P("gx", "gy", None),
        ),
        out_specs=(
            P(None, ("grp", "gx"), "gy"),
            P(("grp", "gx"), "gy"),
            P(None, ("grp", "gx"), "gy"),
        ),
        check_vma=False,
    )
```

```python
import jax
import jax.numpy as jnp
from jax import lax
from jax.experimental import pallas as pl
from jax.experimental.pallas import tpu as pltpu
from jax.sharding import PartitionSpec as P

FIELDS = 8
LEVELS = 16
SUBSTEPS = 4
INTERSECTIONS = 6
ROWS = 64
COLS = 128
TILES = ROWS // 8
BASE = 16
DEEP = ROWS + 32
UNROLL = 16
FLUX_ROWS = 32
PARTS = ((0, 48), (48, 64))
F32 = jnp.float32
BF16 = jnp.bfloat16

VMEM = pl.BlockSpec(memory_space=pltpu.VMEM)
SMEM = pl.BlockSpec(memory_space=pltpu.SMEM)
ANY = pl.BlockSpec(memory_space=pl.ANY)
HBM = pl.BlockSpec(memory_space=pltpu.HBM)


def sub_ids():
    return lax.broadcasted_iota(jnp.int32, (8, COLS), 0)


def lane_ids():
    return lax.broadcasted_iota(jnp.int32, (8, COLS), 1)


def edge_rows_kernel(state, winds, to_up, to_down, st_top, st_low, wi_top, wi_low,
                     sheet_up, sheet_down, sems):
    first, last = slice(0, 8), slice(ROWS - 8, ROWS)
    fetches = [
        pltpu.make_async_copy(source, target, sems.at[i])
        for i, (source, target) in enumerate((
            (winds.at[0, :, first], wi_top.at[0]),
            (winds.at[1, :, first], wi_top.at[1]),
            (winds.at[0, :, last], wi_low.at[0]),
            (winds.at[1, :, last], wi_low.at[1]),
            (state.at[:, first], st_top),
            (state.at[:, last], st_low),
        ))
    ]
    for fetch in fetches:
        fetch.start()
    for fetch in fetches:
        fetch.wait()
    upper = sub_ids() < 4
    for l in range(LEVELS):
        top, low = st_top[l], st_low[l]
        top_hi, low_hi = top.astype(BF16).astype(F32), low.astype(BF16).astype(F32)
        sheet_up[8 * l : 8 * l + 8] = jnp.where(upper, top_hi, pltpu.roll(top - top_hi, 4, 0))
        sheet_down[8 * l : 8 * l + 8] = jnp.where(upper, pltpu.roll(low_hi, 4, 0), low - low_hi)
        k = LEVELS + l
        sheet_up[8 * k : 8 * k + 8] = jnp.where(upper, wi_top[0, l], pltpu.roll(wi_top[1, l], 4, 0))
        sheet_down[8 * k : 8 * k + 8] = jnp.where(upper, pltpu.roll(wi_low[0, l], 4, 0), wi_low[1, l])
    to_up[...] = sheet_up[...].astype(BF16)
    to_down[...] = sheet_down[...].astype(BF16)


def packed(strip, tile, l):
    turned = pltpu.roll(tile, 8 * l + 4, 1)
    return jnp.where((lane_ids() >> 3) == l, turned, strip)


def own_strips_kernel(state, winds, strips):
    def row_tile(t, carry):
        r = pl.multiple_of(t * 8, 8)
        sources = (state, winds.at[0], winds.at[1])
        for c in range(3):
            strip = jnp.zeros((8, COLS), F32)
            for l in range(LEVELS):
                strip = packed(strip, sources[c][l, pl.ds(r, 8), :], l)
            strips[c, pl.ds(r, 8), :] = strip
        return carry

    lax.fori_loop(0, TILES, row_tile, 0, unroll=8)


def edge_columns_kernel(masks, from_below, from_above, own, halo, strip0, to_right, to_left,
                        below, above, full, right_sheet, left_sheet):
    below[...] = from_below[...].astype(F32)
    above[...] = from_above[...].astype(F32)
    upper = sub_ids() < 4
    ok = masks[0]
    full[:, 0:ROWS, :] = own[...]
    parts = [jnp.zeros((8, COLS), F32)] * 3
    for l in range(LEVELS):
        b, a = below[8 * l : 8 * l + 8], above[8 * l : 8 * l + 8]
        s = jnp.where(upper, b + pltpu.roll(b, 4, 0), a + pltpu.roll(a, 4, 0))
        k = LEVELS + l
        b, a = below[8 * k : 8 * k + 8], above[8 * k : 8 * k + 8]
        u = jnp.where(upper, b, pltpu.roll(a, 4, 0))
        v = jnp.where(upper, pltpu.roll(b, 4, 0), a)
        for c, x in enumerate((s, u, v)):
            x = x * ok
            halo[c, 8 * l : 8 * l + 8] = x
            parts[c] = packed(parts[c], x, l)
    for c in range(3):
        full[c, ROWS : ROWS + 8] = parts[c]
    strip0[...] = full[...]
    first = (lane_ids() & 7) < 4
    n = ROWS + 8
    for t in range(TILES + 1):
        r = 8 * t
        s, u, v = full[0, r : r + 8], full[1, r : r + 8], full[2, r : r + 8]
        hi = s.astype(BF16).astype(F32)
        lo = s - hi
        right_sheet[r : r + 8] = jnp.where(first, hi, pltpu.roll(lo, 4, 1))
        left_sheet[r : r + 8] = jnp.where(first, pltpu.roll(lo, COLS - 4, 1), hi)
        right_sheet[n + r : n + r + 8] = jnp.where(first, u, pltpu.roll(v, 4, 1))
        left_sheet[n + r : n + r + 8] = jnp.where(first, pltpu.roll(v, COLS - 4, 1), u)
    to_right[...] = right_sheet[...].astype(BF16)
    to_left[...] = left_sheet[...].astype(BF16)


def stencil(s, n, so, w, e, u, v, d, c):
    drift = u * (e - w) + v * (so - n)
    return c * s + d * ((n + so) + (w + e)) - 0.5 * drift


def inner_steps_kernel(rates, masks, state, winds, halo, last, total, cells0, cells1, cells2, cells3):
    own = slice(BASE, BASE + ROWS)
    high, low = slice(BASE - 8, BASE), slice(BASE + ROWS, BASE + ROWS + 8)
    upper = sub_ids() < 4
    lane = lane_ids()
    row_one = masks[0]

    def copy_level(l, carry):
        h = pl.multiple_of(8 * l, 8)
        cells0[l, own] = state[l]
        x = halo[0, pl.ds(h, 8), :]
        cells0[l, high] = x
        cells0[l, low] = x
        return carry

    lax.fori_loop(0, LEVELS, copy_level, 0, unroll=2)

    def step(src, dst):
        def level(l, carry):
            h = pl.multiple_of(8 * l, 8)
            d = rates[pl.ds(l, 1), :]
            for t in range(TILES if dst is None else TILES + 1):
                k = slice(8 * t, 8 * t + 8)
                r = BASE + 8 * t
                if t < TILES:
                    s, no, so = src[l, r : r + 8, :], src[l, r - 1 : r + 7, :], src[l, r + 1 : r + 9, :]
                    u, v = winds[0, l, k, :], winds[1, l, k, :]
                else:
                    s, no, so = halo_rows(lambda r: src[l, r : r + 8, :], upper)
                    u, v = halo[1, pl.ds(h, 8), :], halo[2, pl.ds(h, 8), :]
                    d = d * row_one
                w = jnp.where(lane == 0, 0.0, pltpu.roll(s, 1, 1))
                e = jnp.where(lane == COLS - 1, 0.0, pltpu.roll(s, COLS - 1, 1))
                x = stencil(s, no, so, w, e, u, v, d, 1.0 - 4.0 * d)
                if dst is None:
                    last[l, k, :] = x
                    total[l, k, :] = (cells1[l, r : r + 8, :] + cells2[l, r : r + 8, :]) + (s + x)
                elif t < TILES:
                    dst[l, r : r + 8, :] = x
                else:
                    dst[l, high, :] = x
                    dst[l, low, :] = x
            return carry

        lax.fori_loop(0, LEVELS, level, 0, unroll=UNROLL)

    step(cells0, cells1)
    step(cells1, cells2)
    step(cells2, cells3)
    step(cells3, None)


def halo_rows(load, upper):
    d, u = BASE + ROWS, BASE - 8
    return (
        load(d),
        jnp.where(upper, load(d - 1), load(u - 1)),
        jnp.where(upper, load(d + 1), load(u + 1)),
    )


def columns_kernel(weights, masks, inner_last, inner_total, strip0, from_left, from_right,
                   ready, fluxes, rounded,
                   lefts, rights, beyond, extras, left_winds, right_winds, left, right, extra_total):
    upper = sub_ids() < 4
    n = ROWS + 8
    own = slice(BASE, BASE + ROWS)
    high, low = slice(BASE - 8, BASE), slice(BASE + ROWS, BASE + ROWS + 8)
    lane = lane_ids()
    place = lane & 7
    first = place < 4
    row_one, side_one, rate = masks[0], masks[1], masks[2]

    def put(buf, t, x):
        if t < TILES:
            buf[BASE + 8 * t : BASE + 8 * t + 8] = x
        else:
            buf[high] = x
            buf[low] = x

    left[...] = from_left[...].astype(F32)
    right[...] = from_right[...].astype(F32)
    for t in range(TILES + 1):
        r, q = slice(8 * t, 8 * t + 8), slice(n + 8 * t, n + 8 * t + 8)
        a, b = left[r], right[r]
        a = (a + pltpu.roll(a, COLS - 4, 1)) * side_one
        b = (b + pltpu.roll(b, 4, 1)) * side_one
        put(lefts[0], t, jnp.where(first, a, strip0[0, r]))
        put(rights[0], t, jnp.where(first, strip0[0, r], b))
        beyond[0][r] = jnp.where(first, a, b)
        a, b = left[q], right[q]
        left_winds[0, r] = jnp.where(first, a * side_one, strip0[1, r])
        right_winds[0, r] = jnp.where(first, strip0[1, r], b * side_one)
        a, b = pltpu.roll(a, COLS - 4, 1), pltpu.roll(b, 4, 1)
        left_winds[1, r] = jnp.where(first, a * side_one, strip0[2, r])
        right_winds[1, r] = jnp.where(first, strip0[2, r], b * side_one)
    left_rate = jnp.where(first, rate * side_one, rate)
    right_rate = jnp.where(first, rate, rate * side_one)
    for step in range(SUBSTEPS):
        last = step == SUBSTEPS - 1
        if not last:
            for t in range(TILES + 1):
                r, k = BASE + 8 * t, slice(8 * t, 8 * t + 8)
                new = []
                for strip, wind, d in ((lefts[step], left_winds, left_rate), (rights[step], right_winds, right_rate)):
                    if t < TILES:
                        s, no, so = strip[r : r + 8], strip[r - 1 : r + 7], strip[r + 1 : r + 9]
                    else:
                        s, no, so = halo_rows(lambda r: strip[r : r + 8], upper)
                        d = d * row_one
                    w, e = pltpu.roll(s, 1, 1), pltpu.roll(s, COLS - 1, 1)
                    new.append(stencil(s, no, so, w, e, wind[0, k], wind[1, k], d, 1.0 - 4.0 * d))
                if step < SUBSTEPS - 2:
                    put(lefts[step + 1], t, new[0])
                    put(rights[step + 1], t, new[1])
                beyond[step + 1][k] = jnp.where(first, new[0], new[1])
        for t in range(TILES if last else TILES + 1):
            r, k = BASE + 8 * t, slice(8 * t, 8 * t + 8)
            side = beyond[step][k]
            d = rate if t < TILES else rate * row_one
            if step == 0:
                s = no = so = jnp.zeros((8, COLS), F32)
            elif t < TILES:
                old = extras[step - 1]
                s, no, so = old[r : r + 8], old[r - 1 : r + 7], old[r + 1 : r + 9]
            else:
                s, no, so = halo_rows(lambda r: extras[step - 1][r : r + 8], upper)
            w = pltpu.roll(jnp.where(place == 3, side, jnp.where(place == 7, 0.0, s)), 1, 1)
            e = pltpu.roll(jnp.where(place == 4, side, jnp.where(place == 0, 0.0, s)), COLS - 1, 1)
            x = stencil(s, no, so, w, e, strip0[1, k], strip0[2, k], d, 1.0 - 4.0 * d)
            put(extras[step], t, x)
            if t < TILES:
                extra_total[k] = x if step == 0 else extra_total[k] + x

    def edges(x, l):
        lanes = lax.broadcasted_iota(jnp.int32, x.shape, 1)
        return jnp.where((lanes < 4) | (lanes >= COLS - 4), pltpu.roll(x, COLS - 4 - 8 * l, 1), 0.0)

    def flux(t, carry):
        r = pl.multiple_of(FLUX_ROWS * t, FLUX_ROWS)
        out = pl.ds(r, FLUX_ROWS)
        inner = pl.ds(BASE + r, FLUX_ROWS)
        sums = [None] * FIELDS
        for l in range(LEVELS):
            ready[l, out, :] = inner_last[l, out, :] + edges(extras[SUBSTEPS - 1][inner, :], l)
            x = inner_total[l, out, :] + edges(extra_total[out, :], l)
            for f in range(FIELDS):
                k = f * LEVELS + l
                term = weights[k : k + 1, :] * x
                sums[f] = term if l == 0 else sums[f] + term
        for f in range(FIELDS):
            mean = sums[f] * (1.0 / SUBSTEPS)
            fluxes[f, out, :] = mean
            rounded[pl.ds(pl.multiple_of(f * ROWS + r, FLUX_ROWS), FLUX_ROWS), :] = mean.astype(BF16)
        return carry

    lax.fori_loop(0, ROWS // FLUX_ROWS, flux, 0)


def turn_blocks_kernel(blocks, turned):
    def turn(i, carry):
        turned[i] = blocks[i].T
        return carry

    lax.fori_loop(0, blocks.shape[0], turn, 0, unroll=32)


def remap_kernel(words, heat, gathered, weights, fluxes, field, state_out, flux_out, boundary_out,
                 table, patches, remapped, surface, state_sem, table_sem, out_sems, flux_sems, surface_sems):
    size = FIELDS * ROWS
    fetch = pltpu.make_async_copy(words, table, table_sem.at[0])
    fetch.start()
    keep = pltpu.make_async_copy(field, state_out, state_sem.at[0])
    keep.start()
    patches[...] = gathered[0 : 3 * size].astype(F32)
    fetch.wait()
    is_ocean = table[table.shape[0] - 1] == 1

    @pl.when(is_ocean)
    def _():
        def sends(i):
            start, end = PARTS[i]
            at = pl.ds(start, end - start)
            return (
                pltpu.make_async_copy(remapped.at[:, at], flux_out.at[:, at], flux_sems.at[i]),
                pltpu.make_async_copy(surface.at[at], boundary_out.at[at], surface_sems.at[i]),
            )

        for i, (begin, end) in enumerate(PARTS):
            for o in range(begin, end):
                picked, chosen = [], []
                for entry in range(INTERSECTIONS):
                    at_entry = ROWS + 2 * ROWS * entry + o
                    start = table[at_entry]
                    picked.append(patches[pl.ds(start, FIELDS, stride=ROWS), :].astype(BF16))
                    chosen.append(weights[table[at_entry + ROWS]])
                total = jnp.dot(
                    jnp.concatenate(picked, 1), jnp.concatenate(chosen, 0), preferred_element_type=F32
                )
                remapped[:, o, :] = total * table[o].astype(F32)
            at = slice(begin, end)
            warmth = field[0, at, :]
            for f in range(FIELDS):
                warmth = warmth + heat[f : f + 1] * remapped[f, at, :]
            surface[at, :] = warmth
            for send in sends(i):
                send.start()
        for i in range(len(PARTS)):
            for send in sends(i):
                send.wait()

    @pl.when(jnp.logical_not(is_ocean))
    def _():
        copies = (
            pltpu.make_async_copy(fluxes, flux_out, out_sems.at[0]),
            pltpu.make_async_copy(fluxes.at[0], boundary_out, out_sems.at[1]),
        )
        for copy in copies:
            copy.start()
        for copy in copies:
            copy.wait()

    keep.wait()


WIDE = pltpu.CompilerParams(vmem_limit_bytes=53 * 2**20 + 5 * 2**17)
LIMIT = pltpu.CompilerParams(vmem_limit_bytes=16 * 2**20)
N = ROWS + 8
SHEET = jax.ShapeDtypeStruct((2 * LEVELS * 8, COLS), BF16)
COLUMNS = jax.ShapeDtypeStruct((2 * N, COLS), BF16)


def cost(microseconds):
    return pl.CostEstimate(
        flops=int(1e9 * microseconds), bytes_accessed=int(3.6e6 * microseconds), transcendentals=0
    )


def f32(*shape):
    return jax.ShapeDtypeStruct(shape, F32)


def edge_rows(state, winds):
    return pl.pallas_call(
        edge_rows_kernel,
        in_specs=[HBM, HBM],
        out_specs=[VMEM, VMEM],
        out_shape=[SHEET, SHEET],
        scratch_shapes=[
            *[pltpu.VMEM((LEVELS, 8, COLS), F32)] * 2,
            *[pltpu.VMEM((2, LEVELS, 8, COLS), F32)] * 2,
            *[pltpu.VMEM(SHEET.shape, F32)] * 2,
            pltpu.SemaphoreType.DMA((6,)),
        ],
        compiler_params=WIDE,
        cost_estimate=cost(1.1),
        name="edge_rows",
    )(state, winds)


def own_strips(state, winds):
    return pl.pallas_call(
        own_strips_kernel,
        in_specs=[VMEM, VMEM],
        out_specs=VMEM,
        out_shape=f32(3, ROWS, COLS),
        compiler_params=LIMIT,
        cost_estimate=cost(1.0),
        name="own_strips",
    )(state, winds)


def edge_columns(masks, from_below, from_above, own):
    return pl.pallas_call(
        edge_columns_kernel,
        in_specs=[VMEM] * 4,
        out_specs=[VMEM] * 4,
        out_shape=[f32(3, LEVELS * 8, COLS), f32(3, N, COLS), COLUMNS, COLUMNS],
        scratch_shapes=[
            pltpu.VMEM(SHEET.shape, F32),
            pltpu.VMEM(SHEET.shape, F32),
            pltpu.VMEM((3, N, COLS), F32),
            pltpu.VMEM((2 * N, COLS), F32),
            pltpu.VMEM((2 * N, COLS), F32),
        ],
        compiler_params=LIMIT,
        cost_estimate=cost(0.2),
        name="edge_columns",
    )(masks, from_below, from_above, own)


def inner_steps(rates, masks, state, winds, halo):
    return pl.pallas_call(
        inner_steps_kernel,
        in_specs=[VMEM] * 5,
        out_specs=[VMEM] * 2,
        out_shape=[f32(LEVELS, ROWS, COLS)] * 2,
        scratch_shapes=[pltpu.VMEM((LEVELS, DEEP, COLS), F32)] * 4,
        compiler_params=LIMIT,
        cost_estimate=cost(2.5),
        name="inner_steps",
    )(rates, masks, state, winds, halo)


def columns(weights, masks, inner_last, inner_total, strip0, from_left, from_right):
    return pl.pallas_call(
        columns_kernel,
        in_specs=[VMEM] * 7,
        out_specs=[VMEM] * 3,
        out_shape=[
            f32(LEVELS, ROWS, COLS),
            f32(FIELDS, ROWS, COLS),
            jax.ShapeDtypeStruct((FIELDS * ROWS, COLS), BF16),
        ],
        scratch_shapes=[
            [pltpu.VMEM((DEEP, COLS), F32)] * 3,
            [pltpu.VMEM((DEEP, COLS), F32)] * 3,
            [pltpu.VMEM((N, COLS), F32)] * 4,
            [pltpu.VMEM((DEEP, COLS), F32)] * 4,
            *[pltpu.VMEM((2, N, COLS), F32)] * 2,
            *[pltpu.VMEM((2 * N, COLS), F32)] * 2,
            pltpu.VMEM((ROWS, COLS), F32),
        ],
        compiler_params=LIMIT,
        name="columns",
    )(weights, masks, inner_last, inner_total, strip0, from_left, from_right)


def turn_blocks(blocks):
    return pl.pallas_call(
        turn_blocks_kernel,
        in_specs=[VMEM],
        out_specs=VMEM,
        out_shape=jax.ShapeDtypeStruct(blocks.shape, BF16),
        compiler_params=LIMIT,
        cost_estimate=cost(1.0),
        name="turn_blocks",
    )(blocks)


def remap(table, heat, gathered, weights, fluxes, field):
    chunks = len(PARTS)
    return pl.pallas_call(
        remap_kernel,
        in_specs=[ANY] + [VMEM] * 5,
        out_specs=[ANY] * 3,
        out_shape=[f32(LEVELS, ROWS, COLS), f32(FIELDS, ROWS, COLS), f32(ROWS, COLS)],
        scratch_shapes=[
            pltpu.SMEM(table.shape, jnp.int32),
            pltpu.VMEM((3 * FIELDS * ROWS, COLS), F32),
            pltpu.VMEM((FIELDS, ROWS, COLS), F32),
            pltpu.VMEM((ROWS, COLS), F32),
            pltpu.SemaphoreType.DMA((1,)),
            pltpu.SemaphoreType.DMA((1,)),
            pltpu.SemaphoreType.DMA((2,)),
            pltpu.SemaphoreType.DMA((chunks,)),
            pltpu.SemaphoreType.DMA((chunks,)),
        ],
        compiler_params=LIMIT,
        name="remap",
    )(table, heat, gathered, weights, fluxes, field)


def body(
    state, winds, diffusivity, coupling, heat_coef, remap_blocks, source_patch, block_ids, land_sea
):
    group = lax.axis_index("grp")
    row_tile = lax.axis_index("gx")
    column_tile = lax.axis_index("gy")
    tiles_x = lax.axis_size("gx")
    tiles_y = lax.axis_size("gy")
    groups = lax.axis_size("grp")
    ocean = group == groups - 1
    line = group * tiles_x + row_tile
    top = (line == 0) | (ocean & (row_tile == 0))
    bottom = (row_tile == tiles_x - 1) & (group >= groups - 2)
    row = lax.broadcasted_iota(jnp.int32, (8, COLS), 0)
    lane = lax.broadcasted_iota(jnp.int32, (8, COLS), 1)
    row_one = jnp.where(row < 4, ~bottom, ~top).astype(F32)
    side_one = jnp.where((lane & 7) < 4, column_tile > 0, column_tile < tiles_y - 1).astype(F32)
    own_rate = jnp.where(ocean, diffusivity[1], diffusivity[0])
    rate = jnp.broadcast_to(own_rate[:, None], (LEVELS, 8)).reshape(1, COLS) * jnp.ones((8, 1), F32)
    masks = jnp.stack([row_one, side_one, rate])
    rates = jnp.broadcast_to(own_rate[:, None], (LEVELS, COLS))
    weights = jnp.broadcast_to(coupling.reshape(-1, 1), (FIELDS * LEVELS, COLS))
    source = source_patch[0, 0].T
    starts = (source // ROWS) * (FIELDS * ROWS) + source % ROWS
    table = jnp.concatenate([
        land_sea.reshape(-1),
        jnp.concatenate([starts, block_ids[0, 0].T], 1).reshape(-1),
        ocean.astype(jnp.int32)[None],
    ])
    heat = jnp.broadcast_to(heat_coef[:, None], (FIELDS, COLS))

    def ring(x, axis, shift):
        count = lax.axis_size(axis)
        return lax.ppermute(x, axis, [(i, (i + shift) % count) for i in range(count)])

    to_up, to_down = edge_rows(state, winds)
    from_below = ring(to_up, ("grp", "gx"), -1)
    from_above = ring(to_down, ("grp", "gx"), 1)
    own = own_strips(state, winds)
    halo, strip0, to_right, to_left = edge_columns(masks, from_below, from_above, own)
    from_left = ring(to_right, "gy", 1)
    from_right = ring(to_left, "gy", -1)
    inner_last, inner_total = inner_steps(rates, masks, state, winds, halo)
    turned = turn_blocks(remap_blocks)
    field, fluxes, rounded = columns(
        weights, masks, inner_last, inner_total, strip0, from_left, from_right
    )
    gathered = lax.all_gather(rounded, "grp", axis=0, tiled=True)
    state_out, fluxes, boundary = remap(table, heat, gathered, turned, fluxes, field)
    return state_out, boundary, fluxes


def solution(mesh):
    return jax.shard_map(
        body,
        mesh=mesh,
        in_specs=(
            P(None, ("grp", "gx"), "gy"),
            P(None, None, ("grp", "gx"), "gy"),
            P(),
            P(),
            P(),
            P(),
            P("gx", "gy", None, None),
            P("gx", "gy", None, None),
            P("gx", "gy", None),
        ),
        out_specs=(
            P(None, ("grp", "gx"), "gy"),
            P(("grp", "gx"), "gy"),
            P(None, ("grp", "gx"), "gy"),
        ),
        check_vma=False,
    )
```

```python
import jax
import jax.numpy as jnp
from jax import lax
from jax.experimental import pallas as pl
from jax.experimental.pallas import tpu as pltpu
from jax.sharding import PartitionSpec as P

FIELDS = 8
LEVELS = 16
SUBSTEPS = 4
INTERSECTIONS = 6
ROWS = 64
COLS = 128
TILES = ROWS // 8
BASE = 16
DEEP = ROWS + 32
UNROLL = 8
FLUX_ROWS = 32
PARTS = ((0, 48), (48, 64))
F32 = jnp.float32
BF16 = jnp.bfloat16

VMEM = pl.BlockSpec(memory_space=pltpu.VMEM)
SMEM = pl.BlockSpec(memory_space=pltpu.SMEM)
ANY = pl.BlockSpec(memory_space=pl.ANY)
HBM = pl.BlockSpec(memory_space=pltpu.HBM)


def sub_ids():
    return lax.broadcasted_iota(jnp.int32, (8, COLS), 0)


def lane_ids():
    return lax.broadcasted_iota(jnp.int32, (8, COLS), 1)


def edge_rows_kernel(state, winds, to_up, to_down, st_top, st_low, wi_top, wi_low,
                     sheet_up, sheet_down, sems):
    first, last = slice(0, 8), slice(ROWS - 8, ROWS)
    fetches = [
        pltpu.make_async_copy(source, target, sems.at[i])
        for i, (source, target) in enumerate((
            (winds.at[0, :, first], wi_top.at[0]),
            (winds.at[1, :, first], wi_top.at[1]),
            (winds.at[0, :, last], wi_low.at[0]),
            (winds.at[1, :, last], wi_low.at[1]),
            (state.at[:, first], st_top),
            (state.at[:, last], st_low),
        ))
    ]
    for fetch in fetches:
        fetch.start()
    for fetch in fetches:
        fetch.wait()
    upper = sub_ids() < 4
    for l in range(LEVELS):
        top, low = st_top[l], st_low[l]
        top_hi, low_hi = top.astype(BF16).astype(F32), low.astype(BF16).astype(F32)
        sheet_up[8 * l : 8 * l + 8] = jnp.where(upper, top_hi, pltpu.roll(top - top_hi, 4, 0))
        sheet_down[8 * l : 8 * l + 8] = jnp.where(upper, pltpu.roll(low_hi, 4, 0), low - low_hi)
        k = LEVELS + l
        sheet_up[8 * k : 8 * k + 8] = jnp.where(upper, wi_top[0, l], pltpu.roll(wi_top[1, l], 4, 0))
        sheet_down[8 * k : 8 * k + 8] = jnp.where(upper, pltpu.roll(wi_low[0, l], 4, 0), wi_low[1, l])
    to_up[...] = sheet_up[...].astype(BF16)
    to_down[...] = sheet_down[...].astype(BF16)


def packed(strip, tile, l):
    turned = pltpu.roll(tile, 8 * l + 4, 1)
    return jnp.where((lane_ids() >> 3) == l, turned, strip)


def own_strips_kernel(state, winds, strips):
    def row_tile(t, carry):
        r = pl.multiple_of(t * 8, 8)
        sources = (state, winds.at[0], winds.at[1])
        for c in range(3):
            strip = jnp.zeros((8, COLS), F32)
            for l in range(LEVELS):
                strip = packed(strip, sources[c][l, pl.ds(r, 8), :], l)
            strips[c, pl.ds(r, 8), :] = strip
        return carry

    lax.fori_loop(0, TILES, row_tile, 0, unroll=8)


def edge_columns_kernel(masks, from_below, from_above, own, halo, strip0, to_right, to_left,
                        below, above, full, right_sheet, left_sheet):
    below[...] = from_below[...].astype(F32)
    above[...] = from_above[...].astype(F32)
    upper = sub_ids() < 4
    ok = masks[0]
    full[:, 0:ROWS, :] = own[...]
    parts = [jnp.zeros((8, COLS), F32)] * 3
    for l in range(LEVELS):
        b, a = below[8 * l : 8 * l + 8], above[8 * l : 8 * l + 8]
        s = jnp.where(upper, b + pltpu.roll(b, 4, 0), a + pltpu.roll(a, 4, 0))
        k = LEVELS + l
        b, a = below[8 * k : 8 * k + 8], above[8 * k : 8 * k + 8]
        u = jnp.where(upper, b, pltpu.roll(a, 4, 0))
        v = jnp.where(upper, pltpu.roll(b, 4, 0), a)
        for c, x in enumerate((s, u, v)):
            x = x * ok
            halo[c, 8 * l : 8 * l + 8] = x
            parts[c] = packed(parts[c], x, l)
    for c in range(3):
        full[c, ROWS : ROWS + 8] = parts[c]
    strip0[...] = full[...]
    first = (lane_ids() & 7) < 4
    n = ROWS + 8
    for t in range(TILES + 1):
        r = 8 * t
        s, u, v = full[0, r : r + 8], full[1, r : r + 8], full[2, r : r + 8]
        hi = s.astype(BF16).astype(F32)
        lo = s - hi
        right_sheet[r : r + 8] = jnp.where(first, hi, pltpu.roll(lo, 4, 1))
        left_sheet[r : r + 8] = jnp.where(first, pltpu.roll(lo, COLS - 4, 1), hi)
        right_sheet[n + r : n + r + 8] = jnp.where(first, u, pltpu.roll(v, 4, 1))
        left_sheet[n + r : n + r + 8] = jnp.where(first, pltpu.roll(v, COLS - 4, 1), u)
    to_right[...] = right_sheet[...].astype(BF16)
    to_left[...] = left_sheet[...].astype(BF16)


def stencil(s, n, so, w, e, u, v, d, c):
    drift = u * (e - w) + v * (so - n)
    return c * s + d * ((n + so) + (w + e)) - 0.5 * drift


def inner_steps_kernel(rates, masks, state, winds, halo, last, total, cells0, cells1, cells2, cells3):
    own = slice(BASE, BASE + ROWS)
    high, low = slice(BASE - 8, BASE), slice(BASE + ROWS, BASE + ROWS + 8)
    upper = sub_ids() < 4
    lane = lane_ids()
    row_one = masks[0]

    def copy_level(l, carry):
        h = pl.multiple_of(8 * l, 8)
        cells0[l, own] = state[l]
        x = halo[0, pl.ds(h, 8), :]
        cells0[l, high] = x
        cells0[l, low] = x
        return carry

    lax.fori_loop(0, LEVELS, copy_level, 0, unroll=2)

    def step(src, dst):
        def level(l, carry):
            h = pl.multiple_of(8 * l, 8)
            d = rates[pl.ds(l, 1), :]
            for t in range(TILES if dst is None else TILES + 1):
                k = slice(8 * t, 8 * t + 8)
                r = BASE + 8 * t
                if t < TILES:
                    s, no, so = src[l, r : r + 8, :], src[l, r - 1 : r + 7, :], src[l, r + 1 : r + 9, :]
                    u, v = winds[0, l, k, :], winds[1, l, k, :]
                else:
                    s, no, so = halo_rows(lambda r: src[l, r : r + 8, :], upper)
                    u, v = halo[1, pl.ds(h, 8), :], halo[2, pl.ds(h, 8), :]
                    d = d * row_one
                w = jnp.where(lane == 0, 0.0, pltpu.roll(s, 1, 1))
                e = jnp.where(lane == COLS - 1, 0.0, pltpu.roll(s, COLS - 1, 1))
                x = stencil(s, no, so, w, e, u, v, d, 1.0 - 4.0 * d)
                if dst is None:
                    last[l, k, :] = x
                    total[l, k, :] = (cells1[l, r : r + 8, :] + cells2[l, r : r + 8, :]) + (s + x)
                elif t < TILES:
                    dst[l, r : r + 8, :] = x
                else:
                    dst[l, high, :] = x
                    dst[l, low, :] = x
            return carry

        lax.fori_loop(0, LEVELS, level, 0, unroll=UNROLL)

    step(cells0, cells1)
    step(cells1, cells2)
    step(cells2, cells3)
    step(cells3, None)


def halo_rows(load, upper):
    d, u = BASE + ROWS, BASE - 8
    return (
        load(d),
        jnp.where(upper, load(d - 1), load(u - 1)),
        jnp.where(upper, load(d + 1), load(u + 1)),
    )


def columns_kernel(weights, masks, inner_last, inner_total, strip0, from_left, from_right,
                   ready, fluxes, rounded,
                   lefts, rights, beyond, extras, left_winds, right_winds, left, right, extra_total):
    upper = sub_ids() < 4
    n = ROWS + 8
    own = slice(BASE, BASE + ROWS)
    high, low = slice(BASE - 8, BASE), slice(BASE + ROWS, BASE + ROWS + 8)
    lane = lane_ids()
    place = lane & 7
    first = place < 4
    row_one, side_one, rate = masks[0], masks[1], masks[2]

    def put(buf, t, x):
        if t < TILES:
            buf[BASE + 8 * t : BASE + 8 * t + 8] = x
        else:
            buf[high] = x
            buf[low] = x

    left[...] = from_left[...].astype(F32)
    right[...] = from_right[...].astype(F32)
    for t in range(TILES + 1):
        r, q = slice(8 * t, 8 * t + 8), slice(n + 8 * t, n + 8 * t + 8)
        a, b = left[r], right[r]
        a = (a + pltpu.roll(a, COLS - 4, 1)) * side_one
        b = (b + pltpu.roll(b, 4, 1)) * side_one
        put(lefts[0], t, jnp.where(first, a, strip0[0, r]))
        put(rights[0], t, jnp.where(first, strip0[0, r], b))
        beyond[0][r] = jnp.where(first, a, b)
        a, b = left[q], right[q]
        left_winds[0, r] = jnp.where(first, a * side_one, strip0[1, r])
        right_winds[0, r] = jnp.where(first, strip0[1, r], b * side_one)
        a, b = pltpu.roll(a, COLS - 4, 1), pltpu.roll(b, 4, 1)
        left_winds[1, r] = jnp.where(first, a * side_one, strip0[2, r])
        right_winds[1, r] = jnp.where(first, strip0[2, r], b * side_one)
    left_rate = jnp.where(first, rate * side_one, rate)
    right_rate = jnp.where(first, rate, rate * side_one)
    for step in range(SUBSTEPS):
        last = step == SUBSTEPS - 1
        if not last:
            for t in range(TILES + 1):
                r, k = BASE + 8 * t, slice(8 * t, 8 * t + 8)
                new = []
                for strip, wind, d in ((lefts[step], left_winds, left_rate), (rights[step], right_winds, right_rate)):
                    if t < TILES:
                        s, no, so = strip[r : r + 8], strip[r - 1 : r + 7], strip[r + 1 : r + 9]
                    else:
                        s, no, so = halo_rows(lambda r: strip[r : r + 8], upper)
                        d = d * row_one
                    w, e = pltpu.roll(s, 1, 1), pltpu.roll(s, COLS - 1, 1)
                    new.append(stencil(s, no, so, w, e, wind[0, k], wind[1, k], d, 1.0 - 4.0 * d))
                if step < SUBSTEPS - 2:
                    put(lefts[step + 1], t, new[0])
                    put(rights[step + 1], t, new[1])
                beyond[step + 1][k] = jnp.where(first, new[0], new[1])
        for t in range(TILES if last else TILES + 1):
            r, k = BASE + 8 * t, slice(8 * t, 8 * t + 8)
            side = beyond[step][k]
            d = rate if t < TILES else rate * row_one
            if step == 0:
                s = no = so = jnp.zeros((8, COLS), F32)
            elif t < TILES:
                old = extras[step - 1]
                s, no, so = old[r : r + 8], old[r - 1 : r + 7], old[r + 1 : r + 9]
            else:
                s, no, so = halo_rows(lambda r: extras[step - 1][r : r + 8], upper)
            w = pltpu.roll(jnp.where(place == 3, side, jnp.where(place == 7, 0.0, s)), 1, 1)
            e = pltpu.roll(jnp.where(place == 4, side, jnp.where(place == 0, 0.0, s)), COLS - 1, 1)
            x = stencil(s, no, so, w, e, strip0[1, k], strip0[2, k], d, 1.0 - 4.0 * d)
            put(extras[step], t, x)
            if t < TILES:
                extra_total[k] = x if step == 0 else extra_total[k] + x

    def edges(x, l):
        lanes = lax.broadcasted_iota(jnp.int32, x.shape, 1)
        return jnp.where((lanes < 4) | (lanes >= COLS - 4), pltpu.roll(x, COLS - 4 - 8 * l, 1), 0.0)

    def flux(t, carry):
        r = pl.multiple_of(FLUX_ROWS * t, FLUX_ROWS)
        out = pl.ds(r, FLUX_ROWS)
        inner = pl.ds(BASE + r, FLUX_ROWS)
        sums = [None] * FIELDS
        for l in range(LEVELS):
            ready[l, out, :] = inner_last[l, out, :] + edges(extras[SUBSTEPS - 1][inner, :], l)
            x = inner_total[l, out, :] + edges(extra_total[out, :], l)
            for f in range(FIELDS):
                k = f * LEVELS + l
                term = weights[k : k + 1, :] * x
                sums[f] = term if l == 0 else sums[f] + term
        for f in range(FIELDS):
            mean = sums[f] * (1.0 / SUBSTEPS)
            fluxes[f, out, :] = mean
            rounded[pl.ds(pl.multiple_of(f * ROWS + r, FLUX_ROWS), FLUX_ROWS), :] = mean.astype(BF16)
        return carry

    lax.fori_loop(0, ROWS // FLUX_ROWS, flux, 0)


def turn_blocks_kernel(blocks, turned):
    def turn(i, carry):
        turned[i] = blocks[i].T
        return carry

    lax.fori_loop(0, blocks.shape[0], turn, 0, unroll=32)


def remap_kernel(words, heat, gathered, weights, fluxes, field, state_out, flux_out, boundary_out,
                 table, patches, remapped, surface, state_sem, table_sem, out_sems, flux_sems, surface_sems):
    size = FIELDS * ROWS
    fetch = pltpu.make_async_copy(words, table, table_sem.at[0])
    fetch.start()
    keep = pltpu.make_async_copy(field, state_out, state_sem.at[0])
    keep.start()
    patches[...] = gathered[0 : 3 * size].astype(F32)
    fetch.wait()
    is_ocean = table[table.shape[0] - 1] == 1

    @pl.when(is_ocean)
    def _():
        def sends(i):
            start, end = PARTS[i]
            at = pl.ds(start, end - start)
            return (
                pltpu.make_async_copy(remapped.at[:, at], flux_out.at[:, at], flux_sems.at[i]),
                pltpu.make_async_copy(surface.at[at], boundary_out.at[at], surface_sems.at[i]),
            )

        for i, (begin, end) in enumerate(PARTS):
            for o in range(begin, end):
                picked, chosen = [], []
                for entry in range(INTERSECTIONS):
                    at_entry = ROWS + 2 * ROWS * entry + o
                    start = table[at_entry]
                    picked.append(patches[pl.ds(start, FIELDS, stride=ROWS), :].astype(BF16))
                    chosen.append(weights[table[at_entry + ROWS]])
                total = jnp.dot(
                    jnp.concatenate(picked, 1), jnp.concatenate(chosen, 0), preferred_element_type=F32
                )
                remapped[:, o, :] = total * table[o].astype(F32)
            at = slice(begin, end)
            warmth = field[0, at, :]
            for f in range(FIELDS):
                warmth = warmth + heat[f : f + 1] * remapped[f, at, :]
            surface[at, :] = warmth
            for send in sends(i):
                send.start()
        for i in range(len(PARTS)):
            for send in sends(i):
                send.wait()

    @pl.when(jnp.logical_not(is_ocean))
    def _():
        copies = (
            pltpu.make_async_copy(fluxes, flux_out, out_sems.at[0]),
            pltpu.make_async_copy(fluxes.at[0], boundary_out, out_sems.at[1]),
        )
        for copy in copies:
            copy.start()
        for copy in copies:
            copy.wait()

    keep.wait()


WIDE = pltpu.CompilerParams(vmem_limit_bytes=53 * 2**20 + 5 * 2**17)
LIMIT = pltpu.CompilerParams(vmem_limit_bytes=16 * 2**20)
N = ROWS + 8
SHEET = jax.ShapeDtypeStruct((2 * LEVELS * 8, COLS), BF16)
COLUMNS = jax.ShapeDtypeStruct((2 * N, COLS), BF16)


def cost(microseconds):
    return pl.CostEstimate(
        flops=int(1e9 * microseconds), bytes_accessed=int(3.6e6 * microseconds), transcendentals=0
    )


def f32(*shape):
    return jax.ShapeDtypeStruct(shape, F32)


def edge_rows(state, winds):
    return pl.pallas_call(
        edge_rows_kernel,
        in_specs=[HBM, HBM],
        out_specs=[VMEM, VMEM],
        out_shape=[SHEET, SHEET],
        scratch_shapes=[
            *[pltpu.VMEM((LEVELS, 8, COLS), F32)] * 2,
            *[pltpu.VMEM((2, LEVELS, 8, COLS), F32)] * 2,
            *[pltpu.VMEM(SHEET.shape, F32)] * 2,
            pltpu.SemaphoreType.DMA((6,)),
        ],
        compiler_params=WIDE,
        cost_estimate=cost(1.1),
        name="edge_rows",
    )(state, winds)


def own_strips(state, winds):
    return pl.pallas_call(
        own_strips_kernel,
        in_specs=[VMEM, VMEM],
        out_specs=VMEM,
        out_shape=f32(3, ROWS, COLS),
        compiler_params=LIMIT,
        cost_estimate=cost(1.0),
        name="own_strips",
    )(state, winds)


def edge_columns(masks, from_below, from_above, own):
    return pl.pallas_call(
        edge_columns_kernel,
        in_specs=[VMEM] * 4,
        out_specs=[VMEM] * 4,
        out_shape=[f32(3, LEVELS * 8, COLS), f32(3, N, COLS), COLUMNS, COLUMNS],
        scratch_shapes=[
            pltpu.VMEM(SHEET.shape, F32),
            pltpu.VMEM(SHEET.shape, F32),
            pltpu.VMEM((3, N, COLS), F32),
            pltpu.VMEM((2 * N, COLS), F32),
            pltpu.VMEM((2 * N, COLS), F32),
        ],
        compiler_params=LIMIT,
        cost_estimate=cost(0.2),
        name="edge_columns",
    )(masks, from_below, from_above, own)


def inner_steps(rates, masks, state, winds, halo):
    return pl.pallas_call(
        inner_steps_kernel,
        in_specs=[VMEM] * 5,
        out_specs=[VMEM] * 2,
        out_shape=[f32(LEVELS, ROWS, COLS)] * 2,
        scratch_shapes=[pltpu.VMEM((LEVELS, DEEP, COLS), F32)] * 4,
        compiler_params=LIMIT,
        cost_estimate=cost(2.5),
        name="inner_steps",
    )(rates, masks, state, winds, halo)


def columns(weights, masks, inner_last, inner_total, strip0, from_left, from_right):
    return pl.pallas_call(
        columns_kernel,
        in_specs=[VMEM] * 7,
        out_specs=[VMEM] * 3,
        out_shape=[
            f32(LEVELS, ROWS, COLS),
            f32(FIELDS, ROWS, COLS),
            jax.ShapeDtypeStruct((FIELDS * ROWS, COLS), BF16),
        ],
        scratch_shapes=[
            [pltpu.VMEM((DEEP, COLS), F32)] * 3,
            [pltpu.VMEM((DEEP, COLS), F32)] * 3,
            [pltpu.VMEM((N, COLS), F32)] * 4,
            [pltpu.VMEM((DEEP, COLS), F32)] * 4,
            *[pltpu.VMEM((2, N, COLS), F32)] * 2,
            *[pltpu.VMEM((2 * N, COLS), F32)] * 2,
            pltpu.VMEM((ROWS, COLS), F32),
        ],
        compiler_params=LIMIT,
        name="columns",
    )(weights, masks, inner_last, inner_total, strip0, from_left, from_right)


def turn_blocks(blocks):
    return pl.pallas_call(
        turn_blocks_kernel,
        in_specs=[VMEM],
        out_specs=VMEM,
        out_shape=jax.ShapeDtypeStruct(blocks.shape, BF16),
        compiler_params=LIMIT,
        cost_estimate=cost(1.0),
        name="turn_blocks",
    )(blocks)


def remap(table, heat, gathered, weights, fluxes, field):
    chunks = len(PARTS)
    return pl.pallas_call(
        remap_kernel,
        in_specs=[ANY] + [VMEM] * 5,
        out_specs=[ANY] * 3,
        out_shape=[f32(LEVELS, ROWS, COLS), f32(FIELDS, ROWS, COLS), f32(ROWS, COLS)],
        scratch_shapes=[
            pltpu.SMEM(table.shape, jnp.int32),
            pltpu.VMEM((3 * FIELDS * ROWS, COLS), F32),
            pltpu.VMEM((FIELDS, ROWS, COLS), F32),
            pltpu.VMEM((ROWS, COLS), F32),
            pltpu.SemaphoreType.DMA((1,)),
            pltpu.SemaphoreType.DMA((1,)),
            pltpu.SemaphoreType.DMA((2,)),
            pltpu.SemaphoreType.DMA((chunks,)),
            pltpu.SemaphoreType.DMA((chunks,)),
        ],
        compiler_params=LIMIT,
        name="remap",
    )(table, heat, gathered, weights, fluxes, field)


def body(
    state, winds, diffusivity, coupling, heat_coef, remap_blocks, source_patch, block_ids, land_sea
):
    group = lax.axis_index("grp")
    row_tile = lax.axis_index("gx")
    column_tile = lax.axis_index("gy")
    tiles_x = lax.axis_size("gx")
    tiles_y = lax.axis_size("gy")
    groups = lax.axis_size("grp")
    ocean = group == groups - 1
    line = group * tiles_x + row_tile
    top = (line == 0) | (ocean & (row_tile == 0))
    bottom = (row_tile == tiles_x - 1) & (group >= groups - 2)
    row = lax.broadcasted_iota(jnp.int32, (8, COLS), 0)
    lane = lax.broadcasted_iota(jnp.int32, (8, COLS), 1)
    row_one = jnp.where(row < 4, ~bottom, ~top).astype(F32)
    side_one = jnp.where((lane & 7) < 4, column_tile > 0, column_tile < tiles_y - 1).astype(F32)
    own_rate = jnp.where(ocean, diffusivity[1], diffusivity[0])
    rate = jnp.broadcast_to(own_rate[:, None], (LEVELS, 8)).reshape(1, COLS) * jnp.ones((8, 1), F32)
    masks = jnp.stack([row_one, side_one, rate])
    rates = jnp.broadcast_to(own_rate[:, None], (LEVELS, COLS))
    weights = jnp.broadcast_to(coupling.reshape(-1, 1), (FIELDS * LEVELS, COLS))
    source = source_patch[0, 0].T
    starts = (source // ROWS) * (FIELDS * ROWS) + source % ROWS
    table = jnp.concatenate([
        land_sea.reshape(-1),
        jnp.concatenate([starts, block_ids[0, 0].T], 1).reshape(-1),
        ocean.astype(jnp.int32)[None],
    ])
    heat = jnp.broadcast_to(heat_coef[:, None], (FIELDS, COLS))

    def ring(x, axis, shift):
        count = lax.axis_size(axis)
        return lax.ppermute(x, axis, [(i, (i + shift) % count) for i in range(count)])

    to_up, to_down = edge_rows(state, winds)
    from_below = ring(to_up, ("grp", "gx"), -1)
    from_above = ring(to_down, ("grp", "gx"), 1)
    own = own_strips(state, winds)
    halo, strip0, to_right, to_left = edge_columns(masks, from_below, from_above, own)
    from_left = ring(to_right, "gy", 1)
    from_right = ring(to_left, "gy", -1)
    inner_last, inner_total = inner_steps(rates, masks, state, winds, halo)
    turned = turn_blocks(remap_blocks)
    field, fluxes, rounded = columns(
        weights, masks, inner_last, inner_total, strip0, from_left, from_right
    )
    gathered = lax.all_gather(rounded, "grp", axis=0, tiled=True)
    state_out, fluxes, boundary = remap(table, heat, gathered, turned, fluxes, field)
    return state_out, boundary, fluxes


def solution(mesh):
    return jax.shard_map(
        body,
        mesh=mesh,
        in_specs=(
            P(None, ("grp", "gx"), "gy"),
            P(None, None, ("grp", "gx"), "gy"),
            P(),
            P(),
            P(),
            P(),
            P("gx", "gy", None, None),
            P("gx", "gy", None, None),
            P("gx", "gy", None),
        ),
        out_specs=(
            P(None, ("grp", "gx"), "gy"),
            P(("grp", "gx"), "gy"),
            P(None, ("grp", "gx"), "gy"),
        ),
        check_vma=False,
    )
```
